32 devices in a mesh: grp: 2 (over x), cell: 16 (over z, y, core).
Axes of the slice: x: 2, y: 2, z: 4, core: 2. Of those that a mesh axis runs over, the one named last changes fastest.
Arguments:
- source_expr: bfloat16 [32768, 2048], P(('grp', 'cell')), parts along dimension 0, may hold values from 0 to 2
- target_expr: bfloat16 [32768, 2048], P(('grp', 'cell')), parts along dimension 0, may hold values from 0 to 2
- loadings: bfloat16 [2048, 256], P('cell'), may hold values from -0.125 to 0.125
- source_prev: float32 [32768, 256], P(('grp', 'cell')), parts along dimension 0, may hold values from 0.25 to 4, as said below
- target_prev: float32 [32768, 256], P(('grp', 'cell')), parts along dimension 0, may hold values from 0.25 to 4, as said below
- weights_prev: float32 [512], P('grp'), parts along dimension 0, may hold values from 0.25 to 4
- live_counts: int32 [2, 32], P(None, ('grp', 'cell')), parts along dimension 1, may hold values from 512 to 1024, as said below
Outputs:
- source_factor: float32 [32768, 256], P(('grp', 'cell')), parts along dimension 0
- target_factor: float32 [32768, 256], P(('grp', 'cell')), parts along dimension 0
- weights: float32 [512], P('grp'), parts along dimension 0
The draws below stay inside these ranges and needn't reach their ends.
There are 2 independent parts, one for each index of `grp`. The reference program is written for one: setup_inputs(seed, part) draws one part's arguments, and reference() takes and returns one part's arrays. A program takes and returns all parts, laid end to end along the dimension named above; an argument that names none is the same for every part. Nothing has to cross between parts.
Inputs may be any that keep to these rules, and one draw needn't show every extreme that they name: `live_counts`: live cells of a time point on one device; the first that many rows of its block are live; in every draw some device holds 1024 live cells of each time point. `source_prev`: entries of the scaled source factor. `target_prev`: entries of the scaled target factor.
All inputs are finite; a program needn't handle non-finite values.
Results may differ from the reference program's by a relative error of at most 0.0003.
Values may be sent and summed in bfloat16 or wider, within the bound.
No kernel may reach another device: no remote copies, remote signals or barrier semaphores. Data moves between devices by JAX's collectives and lax.ppermute only.
A program may use at most 64 MiB of HBM per device.

```python
import math
import jax
import jax.numpy as jnp
from jax import lax

CELLS_DEV = 1024
G = 2048
D = 256
R = 256
ITERS = 3
SHARDS = 16
CELLS = 16384


def draw_live_counts(key, part):
    key = jax.random.fold_in(key, 11)
    first, second, third = jax.random.split(key, 3)
    counts = jax.random.randint(first, (2, SHARDS), CELLS_DEV // 2, CELLS_DEV + 1)
    top_slot = jax.random.randint(second, (2,), 0, SHARDS)
    low_slot = jax.random.randint(third, (2,), 0, SHARDS)
    places = jnp.arange(SHARDS, dtype=jnp.int32)[None, :]
    counts = jnp.where(places == low_slot[:, None], CELLS_DEV // 2, counts)
    counts = jnp.where(places == top_slot[:, None], CELLS_DEV, counts)
    return counts.astype(jnp.int32)


def blocked_factor(level_key, noise, span):
    levels = jax.random.uniform(level_key, (16, 16), jnp.float32, -span, span)
    row_block = jnp.arange(CELLS, dtype=jnp.int32) * 16 // CELLS
    col_block = jnp.arange(R, dtype=jnp.int32) * 16 // R
    table = levels[row_block][:, col_block]
    return jnp.clip(jnp.exp(table + noise), 0.25, 4.0).astype(jnp.float32)


def draw_source_prev(key, part):
    key = jax.random.fold_in(key, 23)
    level_key, noise_key = jax.random.split(key)
    noise = jax.random.uniform(noise_key, (CELLS, R), jnp.float32, -0.7, 0.7)
    return blocked_factor(level_key, noise, 1.3)


def draw_target_prev(key, part):
    key = jax.random.fold_in(key, 37)
    level_key, noise_key = jax.random.split(key)
    noise = jax.random.uniform(noise_key, (CELLS, R), jnp.float32, -0.7, 0.7)
    return blocked_factor(level_key, noise, 1.3)


def block_levels(key, dims, cuts, low, top_value):
    gain, own = 1.0, jax.random.fold_in(key, 6)
    for dim, parts in cuts:
        steps = jnp.exp(jax.random.uniform(jax.random.fold_in(own, dim), (parts,), jnp.float32, low / len(cuts), top_value / len(cuts)))
        gain = gain * jnp.repeat(steps, dims[dim] // parts).reshape([-1 if axis == dim else 1 for axis in range(len(dims))])
    return gain


def normal_values(stream_key, extent, deviation, limit, shards=(), kind=jnp.bfloat16):
    values = deviation * jax.random.normal(stream_key, extent, jnp.float32)
    if shards:
        values = values * block_levels(stream_key, extent, shards, -0.22, 0.18)
    return jnp.clip(values, -limit, limit).astype(kind)


def setup_inputs(seed: int = 0, part: int = 0) -> dict:
    key_of = jax.random.split(jax.random.key(seed), 8)
    part_keys = jax.random.split(jax.random.fold_in(key_of[7], part), 8)
    source_expr = jnp.clip(2.0 * jax.random.uniform(part_keys[0], (CELLS, G), jnp.float32) ** block_levels(part_keys[0], (CELLS, G), ((0, 16),), -0.2, 0.2), 0.0, 2.0).astype(jnp.bfloat16)
    target_expr = jnp.clip(2.0 * jax.random.uniform(part_keys[1], (CELLS, G), jnp.float32) ** block_levels(part_keys[1], (CELLS, G), ((0, 16),), -0.2, 0.2), 0.0, 2.0).astype(jnp.bfloat16)
    loadings = normal_values(key_of[2], (G, D), G ** -0.5, 0.125, ((0, 16),))
    source_prev = draw_source_prev(jax.random.fold_in(jax.random.fold_in(key_of[7], part), 71), part)
    target_prev = draw_target_prev(jax.random.fold_in(jax.random.fold_in(key_of[7], part), 71), part)
    weights_prev = jnp.clip(jnp.exp(jax.random.uniform(part_keys[5], (R,), jnp.float32, math.log(0.25), math.log(4.0))), 0.25, 4.0)
    live_counts = draw_live_counts(jax.random.fold_in(jax.random.fold_in(key_of[7], part), 71), part)
    return dict(source_expr=source_expr, target_expr=target_expr, loadings=loadings, source_prev=source_prev, target_prev=target_prev, weights_prev=weights_prev, live_counts=live_counts)


step_size = 1.0
precise = lax.Precision.HIGHEST


def column_tables(cross_src, cross_tgt, stats, col_mass):
    inverse = 1.0 / (D * col_mass)
    norm_q = stats[0]
    total_q = stats[1]
    norm_p = stats[2]
    total_p = stats[3]
    cost_cols = (norm_q * total_p + total_q * norm_p - 2.0 * jnp.sum(cross_src * cross_tgt, axis=0)) / D
    kernel_mass = col_mass * jnp.exp(step_size * cost_cols / (col_mass * col_mass))
    mat_src = (-2.0 * inverse) * cross_tgt
    mat_tgt = (-2.0 * inverse) * cross_src
    coeffs = jnp.stack([total_p * inverse, norm_p * inverse, total_q * inverse, norm_q * inverse, kernel_mass])
    return mat_src, mat_tgt, coeffs


def kernel_of(embed, norms, factor, matrix, slope, offset):
    grad = norms[:, None] * slope[None, :] + offset[None, :] + jnp.dot(embed, matrix, precision=precise)
    return factor * jnp.exp(-step_size * grad)


def reference(source_expr, target_expr, loadings, source_prev, target_prev, weights_prev, live_counts):
    emb_src = jnp.dot(source_expr, loadings, preferred_element_type=jnp.float32)
    emb_tgt = jnp.dot(target_expr, loadings, preferred_element_type=jnp.float32)
    src_factor = source_prev / R
    tgt_factor = target_prev / R
    col_mass = weights_prev * (CELLS / R)
    norm_src = jnp.sum(emb_src * emb_src, axis=1)
    norm_tgt = jnp.sum(emb_tgt * emb_tgt, axis=1)
    cross_src = jnp.dot(emb_src.T, src_factor, precision=precise)
    cross_tgt = jnp.dot(emb_tgt.T, tgt_factor, precision=precise)
    stats = jnp.stack([jnp.dot(norm_src, src_factor, precision=precise), jnp.sum(src_factor, axis=0),
                       jnp.dot(norm_tgt, tgt_factor, precision=precise), jnp.sum(tgt_factor, axis=0)])
    mat_src, mat_tgt, coeffs = column_tables(cross_src, cross_tgt, stats, col_mass)
    kernel_src = kernel_of(emb_src, norm_src, src_factor, mat_src, coeffs[0], coeffs[1])
    kernel_tgt = kernel_of(emb_tgt, norm_tgt, tgt_factor, mat_tgt, coeffs[2], coeffs[3])
    kernel_mass = coeffs[4]
    row_ids = jnp.arange(CELLS, dtype=jnp.int32)
    shard_ids = row_ids // CELLS_DEV
    local_ids = row_ids % CELLS_DEV
    live_src = local_ids < live_counts[0][shard_ids]
    live_tgt = local_ids < live_counts[1][shard_ids]
    totals = jnp.sum(live_counts.astype(jnp.float32), axis=1)
    marg_src = jnp.where(live_src, CELLS / totals[0], jnp.float32(0.0))
    marg_tgt = jnp.where(live_tgt, CELLS / totals[1], jnp.float32(0.0))
    dual_src = jnp.ones((R,), jnp.float32)
    dual_tgt = jnp.ones((R,), jnp.float32)
    scale_src = marg_src
    scale_tgt = marg_tgt
    new_mass = dual_src
    for step_index in range(ITERS):
        scale_src = marg_src / jnp.dot(kernel_src, dual_src, precision=precise)
        scale_tgt = marg_tgt / jnp.dot(kernel_tgt, dual_tgt, precision=precise)
        sum_src = jnp.dot(scale_src, kernel_src, precision=precise)
        sum_tgt = jnp.dot(scale_tgt, kernel_tgt, precision=precise)
        new_mass = jnp.cbrt(kernel_mass * sum_src * sum_tgt)
        dual_src = new_mass / sum_src
        dual_tgt = new_mass / sum_tgt
    source_factor = R * (scale_src[:, None] * kernel_src * dual_src[None, :])
    target_factor = R * (scale_tgt[:, None] * kernel_tgt * dual_tgt[None, :])
    weights = new_mass * (R / CELLS)
    return source_factor, target_factor, weights
```

```python
import jax
import jax.numpy as jnp
from jax import lax
from jax.sharding import PartitionSpec as P

D = 256
ITERS = 3


step_size = 1.0
precise = lax.Precision.HIGHEST


def partners(count, mask):
    return [(i, i ^ mask) for i in range(count)]


def swap(value, count, mask):
    return lax.ppermute(value, "cell", partners(count, mask))


def gather_loadings(loadings, count):
    top = count.bit_length() - 1
    stack = loadings[None]
    masks = [1 << b for b in range(top)]
    if top >= 3:
        high, low = masks[-1], masks[-2]
        pieces = [stack] + [swap(stack, count, m) for m in (low, high, low | high)]
        stack = jnp.concatenate(pieces)
        masks = masks[:-2]
    order = list(range(stack.shape[0]))
    order = [0, low, high, low | high] if top >= 3 else [0]
    for mask in reversed(masks):
        stack = jnp.concatenate([stack, swap(stack, count, mask)])
        order = order + [o | mask for o in order]
    return stack, order


def total_over_cells(value, count):
    copies = jnp.broadcast_to(value[None], (count,) + value.shape)
    return jnp.sum(lax.all_to_all(copies, "cell", 0, 0), axis=0)


def same_core(count):
    return [list(range(0, count, 2)), list(range(1, count, 2))]


def column_tables(cross_src, cross_tgt, stats, col_mass):
    inverse = 1.0 / (D * col_mass)
    norm_q = stats[0]
    total_q = stats[1]
    norm_p = stats[2]
    total_p = stats[3]
    cost_cols = (
        norm_q * total_p + total_q * norm_p - 2.0 * jnp.sum(cross_src * cross_tgt, axis=0)
    ) / D
    kernel_mass = col_mass * jnp.exp(step_size * cost_cols / (col_mass * col_mass))
    mat_src = -2.0 * inverse * cross_tgt
    mat_tgt = -2.0 * inverse * cross_src
    coeffs = jnp.stack(
        [total_p * inverse, norm_p * inverse, total_q * inverse, norm_q * inverse, kernel_mass]
    )
    return (mat_src, mat_tgt, coeffs)


def kernel_of(embed, norms, factor, matrix, slope, offset):
    grad = (
        norms[:, None] * slope[None, :]
        + offset[None, :]
        + jnp.dot(embed, matrix, precision=precise)
    )
    return factor * jnp.exp(-step_size * grad)


def on_device(
    source_expr, target_expr, loadings, source_prev, target_prev, weights_prev, live_counts
):
    count = lax.axis_size("cell")
    me = lax.axis_index("cell")
    core = me % 2
    half = count // 2
    row_count = source_expr.shape[0]
    rank_size = source_prev.shape[1]
    cell_total = row_count * count
    stack, order = gather_loadings(loadings, count)
    place = [0] * count
    for position, mask in enumerate(order):
        place[mask] = position
    chosen = jnp.asarray(place, jnp.int32)[jnp.arange(count, dtype=jnp.int32) ^ me]
    gathered = stack[chosen].reshape(-1, loadings.shape[1])
    emb_src = jnp.dot(source_expr, gathered, preferred_element_type=jnp.float32)
    emb_tgt = jnp.dot(target_expr, gathered, preferred_element_type=jnp.float32)
    src_factor = source_prev / rank_size
    tgt_factor = target_prev / rank_size
    col_mass = weights_prev * (cell_total / rank_size)
    norm_src = jnp.sum(emb_src * emb_src, axis=1)
    norm_tgt = jnp.sum(emb_tgt * emb_tgt, axis=1)
    contract = (((0,), (0,)), ((), ()))
    cross_src = lax.dot_general(emb_src, src_factor, contract, precision=precise)
    cross_tgt = lax.dot_general(emb_tgt, tgt_factor, contract, precision=precise)
    live = live_counts[:, 0].astype(jnp.float32)

    def extras(norms, factor, number):
        return jnp.concatenate(
            [
                jnp.dot(norms[None, :], factor, precision=precise),
                jnp.sum(factor, axis=0)[None, :],
                jnp.full((1, rank_size), number),
                jnp.zeros((5, rank_size), jnp.float32),
            ]
        )

    part_src = jnp.concatenate([cross_src, extras(norm_src, src_factor, live[0])])
    part_tgt = jnp.concatenate([cross_tgt, extras(norm_tgt, tgt_factor, live[1])])
    first = core == 0
    own = jnp.where(first, part_src, part_tgt)
    own = own + swap(jnp.where(first, part_tgt, part_src), count, 1)
    rows = D // half
    blocks = jnp.concatenate(
        [
            own[:D].reshape(half, rows, rank_size),
            jnp.broadcast_to(own[D:][None], (half, 8, rank_size)),
        ],
        axis=1,
    )
    groups = same_core(count)
    blocks = jnp.sum(lax.all_to_all(blocks, "cell", 0, 0, axis_index_groups=groups), axis=0)
    copies = jnp.broadcast_to(blocks[:rows][None], (half, rows, rank_size))
    full = lax.all_to_all(copies, "cell", 0, 0, axis_index_groups=groups).reshape(D, rank_size)
    full = jnp.concatenate([full, blocks[rows:]])
    other = swap(full, count, 1)
    sum_a = jnp.where(first, full, other)
    sum_b = jnp.where(first, other, full)
    full_stats = jnp.concatenate([sum_a[D : D + 2], sum_b[D : D + 2]])
    mat_src, mat_tgt, coeffs = column_tables(sum_a[:D], sum_b[:D], full_stats, col_mass)
    kernel_src = kernel_of(emb_src, norm_src, src_factor, mat_src, coeffs[0], coeffs[1])
    kernel_tgt = kernel_of(emb_tgt, norm_tgt, tgt_factor, mat_tgt, coeffs[2], coeffs[3])
    kernel_mass = coeffs[4]
    local_row = jnp.arange(row_count, dtype=jnp.int32)
    live_src = local_row < live_counts[0, 0]
    live_tgt = local_row < live_counts[1, 0]
    marg_src = jnp.where(live_src, cell_total / sum_a[D + 2, 0], jnp.float32(0.0))
    marg_tgt = jnp.where(live_tgt, cell_total / sum_b[D + 2, 0], jnp.float32(0.0))
    dual_src = jnp.ones((rank_size,), jnp.float32)
    dual_tgt = jnp.ones((rank_size,), jnp.float32)
    for _ in range(ITERS):
        scale_src = marg_src / jnp.dot(kernel_src, dual_src, precision=precise)
        scale_tgt = marg_tgt / jnp.dot(kernel_tgt, dual_tgt, precision=precise)
        sums = jnp.concatenate(
            [
                jnp.dot(scale_src[None, :], kernel_src, precision=precise),
                jnp.dot(scale_tgt[None, :], kernel_tgt, precision=precise),
            ],
            axis=1,
        )
        sums = total_over_cells(sums, count)
        sum_src, sum_tgt = sums[0, :rank_size], sums[0, rank_size:]
        new_mass = jnp.cbrt(kernel_mass * sum_src * sum_tgt)
        dual_src = new_mass / sum_src
        dual_tgt = new_mass / sum_tgt
    source_factor = rank_size * (scale_src[:, None] * kernel_src * dual_src[None, :])
    target_factor = rank_size * (scale_tgt[:, None] * kernel_tgt * dual_tgt[None, :])
    weights = new_mass * (rank_size / cell_total)
    return (source_factor, target_factor, weights)


def solution(mesh):
    in_specs = (
        P(("grp", "cell"), None),
        P(("grp", "cell"), None),
        P("cell", None),
        P(("grp", "cell"), None),
        P(("grp", "cell"), None),
        P("grp"),
        P(None, ("grp", "cell")),
    )
    out_specs = (P(("grp", "cell"), None), P(("grp", "cell"), None), P("grp"))
    return jax.shard_map(
        on_device, mesh=mesh, in_specs=in_specs, out_specs=out_specs, check_vma=False
    )
```

```python
import functools

import jax
import jax.numpy as jnp
from jax import lax
from jax.experimental import pallas as pl
from jax.experimental.pallas import tpu as pltpu
from jax.sharding import PartitionSpec as P

D = 256
ITERS = 3
STEPS = 4
EXTRA = 8

step_size = 1.0
f32 = jnp.float32
bf16 = jnp.bfloat16
LIMIT = 24 * 1024 * 1024


def swap(value, count, mask):
    return lax.ppermute(value, "cell", [(i, i ^ mask) for i in range(count)])


def gather_loadings(loadings, count):
    bits = [1 << b for b in range(count.bit_length() - 1)]
    low, high = bits[-2], bits[-1]
    own = loadings[None]
    stack = jnp.concatenate([own] + [swap(own, count, m) for m in (low, high, low | high)])
    masks = [0, low, high, low | high]
    for bit in reversed(bits[2:-2]):
        stack = jnp.concatenate([stack, swap(stack, count, bit)])
        masks = masks + [m | bit for m in masks]
    across = swap(stack, count, 2)
    pair = swap(stack, count, 1)
    both = swap(across, count, 1)
    return [
        (stack, masks),
        (pair, [m | 1 for m in masks]),
        (across, [m | 2 for m in masks]),
        (both, [m | 3 for m in masks]),
    ]


def halves(value):
    upper = value.astype(bf16)
    return upper, (value - upper.astype(f32)).astype(bf16)


def dot3(a, b, left, right):
    dims = (((left,), (right,)), ((), ()))
    dot = functools.partial(lax.dot_general, dimension_numbers=dims, preferred_element_type=f32)
    return dot(a[0], b[0]) + (dot(a[0], b[1]) + dot(a[1], b[0]))


def embed_kernel(masks, place, live, xs, xt, *refs):
    pieces = refs[: len(masks)]
    qs, qt, emb_s, emb_t, own, send, table, cross, stats = refs[len(masks) :]
    step = pl.program_id(0)
    me = place[0]
    rank = qs.shape[1]

    @pl.when(step == 0)
    def _():
        rows = pieces[0].shape[1]
        for piece, mask_list in zip(pieces, masks):
            for j, mask in enumerate(mask_list):
                start = pl.multiple_of((me ^ mask) * rows, rows)
                table[pl.ds(start, rows), :] = piece[j]
        cross[...] = jnp.zeros_like(cross)
        stats[...] = jnp.zeros_like(stats)

    for t, (x, q, emb) in enumerate(((xs, qs, emb_s), (xt, qt, emb_t))):
        value = jnp.dot(x[...], table[...], preferred_element_type=f32)
        emb[...] = value
        factor = q[...] / rank
        norms = jnp.sum(value * value, axis=1, keepdims=True)
        stats[2 * t : 2 * t + 1, :] += jnp.sum(norms * factor, axis=0, keepdims=True)
        stats[2 * t + 1 : 2 * t + 2, :] += jnp.sum(factor, axis=0, keepdims=True)
        cross[t] += dot3(halves(value), halves(factor), 0, 0)

    @pl.when(step == pl.num_programs(0) - 1)
    def _():
        stats[4:5, :] = jnp.full((1, rank), live[0].astype(f32))
        stats[5:6, :] = jnp.full((1, rank), live[1].astype(f32))
        core = me % 2
        blocks, rows = own.shape[0], own.shape[1] - EXTRA
        for b in range(blocks):
            own[b, 0:rows, :] = cross[core, b * rows : (b + 1) * rows, :]
            send[b, 0:rows, :] = cross[1 - core, b * rows : (b + 1) * rows, :]
            own[b, rows:, :] = stats[...]
            send[b, rows:, :] = stats[...]


def embed(place, live, xs, xt, pieces, qs, qt, half):
    rows, genes = xs.shape
    rank = qs.shape[1]
    block = rows // STEPS
    dim = pieces[0][0].shape[2]
    block_rows = dim // half + EXTRA
    masks = [m for _, m in pieces]
    whole = lambda shape: pl.BlockSpec(shape, lambda i: (0,) * len(shape))
    part = lambda width: pl.BlockSpec((block, width), lambda i: (i, 0))
    smem = pl.BlockSpec(memory_space=pltpu.SMEM)
    return pl.pallas_call(
        functools.partial(embed_kernel, masks),
        grid=(STEPS,),
        in_specs=[smem, smem, part(genes), part(genes)]
        + [whole(p.shape) for p, _ in pieces]
        + [part(rank), part(rank)],
        out_specs=[part(dim), part(dim), whole((half, block_rows, rank)), whole((half, block_rows, rank))],
        out_shape=[jax.ShapeDtypeStruct((rows, dim), f32)] * 2
        + [jax.ShapeDtypeStruct((half, block_rows, rank), f32)] * 2,
        scratch_shapes=[
            pltpu.VMEM((genes, dim), bf16),
            pltpu.VMEM((2, dim, rank), f32),
            pltpu.VMEM((EXTRA, rank), f32),
        ],
        compiler_params=pltpu.CompilerParams(vmem_limit_bytes=LIMIT),
        name="embed",
    )(place, live, xs, xt, *[p for p, _ in pieces], qs, qt)


def marginal(step, block, live, total, cells):
    row = lax.broadcasted_iota(jnp.int32, (block, 1), 0) + step * block
    return jnp.where(row < live, cells / total, 0.0)


def store_sums(sums, copies):
    for i in range(copies.shape[0]):
        copies[i] = sums[...]


def kernels_kernel(
    cells, place, live, es, et, qs, qt, mine, other, stats, weights, ks, kt, copies, mass_out,
    mats, coeffs, sums,
):
    step = pl.program_id(0)
    core = place[0] % 2
    block, rank = qs.shape

    @pl.when(step == 0)
    def _():
        first = core == 0
        a, b = mine[...], other[...]
        cross_s, cross_t = jnp.where(first, a, b), jnp.where(first, b, a)
        col_mass = weights[...] * (cells / rank)
        inverse = 1.0 / (D * col_mass)
        norm_q, total_q, norm_p, total_p = (stats[i : i + 1, :] for i in range(4))
        cost = (
            norm_q * total_p + total_q * norm_p
            - 2.0 * jnp.sum(cross_s * cross_t, axis=0, keepdims=True)
        ) / D
        mass_out[...] = col_mass * jnp.exp(step_size * cost / (col_mass * col_mass))
        mats[0], mats[1] = halves((-2.0 * inverse) * cross_t)
        mats[2], mats[3] = halves((-2.0 * inverse) * cross_s)
        coeffs[0:1, :] = total_p * inverse
        coeffs[1:2, :] = norm_p * inverse
        coeffs[2:3, :] = total_q * inverse
        coeffs[3:4, :] = norm_q * inverse
        sums[...] = jnp.zeros_like(sums)

    for t, (e, q, k) in enumerate(((es, qs, ks), (et, qt, kt))):
        value = e[...]
        norms = jnp.sum(value * value, axis=1, keepdims=True)
        grad = (
            norms * coeffs[2 * t : 2 * t + 1, :] + coeffs[2 * t + 1 : 2 * t + 2, :]
            + dot3(halves(value), (mats[2 * t], mats[2 * t + 1]), 1, 0)
        )
        kernel = (q[...] / rank) * jnp.exp(-step_size * grad)
        k[...] = kernel
        total = stats[4 + t, 0]
        scale = marginal(step, block, live[t], total, cells) / jnp.sum(kernel, axis=1, keepdims=True)
        sums[t : t + 1, :] += jnp.sum(scale * kernel, axis=0, keepdims=True)

    @pl.when(step == pl.num_programs(0) - 1)
    def _():
        store_sums(sums, copies)


def cube_root(x):
    y = jnp.exp(jnp.log(x) * (1.0 / 3.0))
    refined = y - (y - x / (y * y)) * (1.0 / 3.0)
    return jnp.where((x > 0.0) & (x < jnp.inf), refined, y)


def duals_of(parts, kernel_mass):
    sums = jnp.sum(parts[...], axis=0)
    sum_s, sum_t = sums[0:1, :], sums[1:2, :]
    mass = cube_root(kernel_mass[...] * sum_s * sum_t)
    return mass, mass / sum_s, mass / sum_t


def sweep_kernel(cells, last, live, ks, kt, parts, kernel_mass, stats, *refs):
    if last:
        ss, st, copies, sums, duals = refs
    else:
        copies, sums, duals = refs
    step = pl.program_id(0)
    block = ks.shape[0]

    @pl.when(step == 0)
    def _():
        _, dual_s, dual_t = duals_of(parts, kernel_mass)
        duals[0:1, :] = dual_s
        duals[1:2, :] = dual_t
        sums[...] = jnp.zeros_like(sums)

    for t, k in enumerate((ks, kt)):
        kernel = k[...]
        weighted = jnp.sum(kernel * duals[t : t + 1, :], axis=1, keepdims=True)
        scale = marginal(step, block, live[t], stats[4 + t, 0], cells) / weighted
        scaled = scale * kernel
        sums[t : t + 1, :] += jnp.sum(scaled, axis=0, keepdims=True)
        if last:
            (ss, st)[t][...] = scaled

    @pl.when(step == pl.num_programs(0) - 1)
    def _():
        store_sums(sums, copies)


def finish_kernel(cells, ss, st, parts, kernel_mass, fs, ft, weights, duals):
    step = pl.program_id(0)
    rank = ss.shape[1]

    @pl.when(step == 0)
    def _():
        mass, dual_s, dual_t = duals_of(parts, kernel_mass)
        duals[0:1, :] = dual_s
        duals[1:2, :] = dual_t
        weights[...] = mass * (rank / cells)

    fs[...] = rank * (ss[...] * duals[0:1, :])
    ft[...] = rank * (st[...] * duals[1:2, :])


def specs(rows, rank):
    block = rows // STEPS
    whole = lambda shape: pl.BlockSpec(shape, lambda i: (0,) * len(shape))
    part = pl.BlockSpec((block, rank), lambda i: (i, 0))
    smem = pl.BlockSpec(memory_space=pltpu.SMEM)
    return whole, part, smem


def kernels(cells, count, place, live, es, et, qs, qt, mine, other, stats, weights):
    rows, rank = qs.shape
    dim = es.shape[1]
    whole, part, smem = specs(rows, rank)
    wide = pl.BlockSpec((rows // STEPS, dim), lambda i: (i, 0))
    return pl.pallas_call(
        functools.partial(kernels_kernel, cells),
        grid=(STEPS,),
        in_specs=[smem, smem, wide, wide, part, part, whole((dim, rank)), whole((dim, rank)),
                  whole((EXTRA, rank)), whole((1, rank))],
        out_specs=[part, part, whole((count, 2, rank)), whole((1, rank))],
        out_shape=[jax.ShapeDtypeStruct((rows, rank), f32)] * 2
        + [jax.ShapeDtypeStruct((count, 2, rank), f32), jax.ShapeDtypeStruct((1, rank), f32)],
        scratch_shapes=[
            pltpu.VMEM((4, dim, rank), bf16),
            pltpu.VMEM((8, rank), f32),
            pltpu.VMEM((2, rank), f32),
        ],
        compiler_params=pltpu.CompilerParams(vmem_limit_bytes=LIMIT),
        name="kernels",
    )(place, live, es, et, qs, qt, mine, other, stats, weights)


def sweep(cells, count, last, live, ks, kt, parts, kernel_mass, stats):
    rows, rank = ks.shape
    whole, part, smem = specs(rows, rank)
    scaled = [jax.ShapeDtypeStruct((rows, rank), f32)] * 2 if last else []
    return pl.pallas_call(
        functools.partial(sweep_kernel, cells, last),
        grid=(STEPS,),
        in_specs=[smem, part, part, whole(parts.shape), whole((1, rank)), whole((EXTRA, rank))],
        out_specs=[part] * len(scaled) + [whole((count, 2, rank))],
        out_shape=scaled + [jax.ShapeDtypeStruct((count, 2, rank), f32)],
        scratch_shapes=[pltpu.VMEM((2, rank), f32), pltpu.VMEM((2, rank), f32)],
        compiler_params=pltpu.CompilerParams(vmem_limit_bytes=LIMIT),
        name="sweep",
    )(live, ks, kt, parts, kernel_mass, stats)


def finish(cells, ss, st, parts, kernel_mass):
    rows, rank = ss.shape
    whole, part, _ = specs(rows, rank)
    return pl.pallas_call(
        functools.partial(finish_kernel, cells),
        grid=(STEPS,),
        in_specs=[part, part, whole(parts.shape), whole((1, rank))],
        out_specs=[part, part, whole((1, rank))],
        out_shape=[jax.ShapeDtypeStruct((rows, rank), f32)] * 2
        + [jax.ShapeDtypeStruct((1, rank), f32)],
        scratch_shapes=[pltpu.VMEM((2, rank), f32)],
        compiler_params=pltpu.CompilerParams(vmem_limit_bytes=LIMIT),
        name="finish",
    )(ss, st, parts, kernel_mass)


def on_device(
    source_expr, target_expr, loadings, source_prev, target_prev, weights_prev, live_counts
):
    count = lax.axis_size("cell")
    half = count // 2
    place = lax.axis_index("cell").astype(jnp.int32)[None]
    live = live_counts[:, 0]
    rows, rank = source_prev.shape
    dim = loadings.shape[1]
    cells = rows * count
    exchange = functools.partial(lax.all_to_all, axis_name="cell", split_axis=0, concat_axis=0)
    groups = [list(range(0, count, 2)), list(range(1, count, 2))]

    pieces = gather_loadings(loadings, count)
    emb_s, emb_t, own, send = embed(
        place, live, source_expr, target_expr, pieces, source_prev, target_prev, half
    )
    own = own + swap(send, count, 1)
    shard = jnp.sum(exchange(own, axis_index_groups=groups), axis=0)
    share = dim // half
    mine = exchange(
        jnp.broadcast_to(shard[:share][None], (half, share, rank)), axis_index_groups=groups
    ).reshape(dim, rank)
    stats = shard[share:]
    other = swap(mine, count, 1)
    ks, kt, copies, kernel_mass = kernels(
        cells, count, place, live, emb_s, emb_t, source_prev, target_prev, mine, other, stats,
        weights_prev[None],
    )
    scaled = []
    for step_index in range(1, ITERS):
        last = step_index == ITERS - 1
        *scaled, copies = sweep(
            cells, count, last, live, ks, kt, exchange(copies), kernel_mass, stats
        )
    out_s, out_t, weights = finish(cells, *scaled, exchange(copies), kernel_mass)
    return out_s, out_t, weights[0]


def solution(mesh):
    in_specs = (
        P(("grp", "cell"), None),
        P(("grp", "cell"), None),
        P("cell", None),
        P(("grp", "cell"), None),
        P(("grp", "cell"), None),
        P("grp"),
        P(None, ("grp", "cell")),
    )
    out_specs = (P(("grp", "cell"), None), P(("grp", "cell"), None), P("grp"))
    return jax.shard_map(
        on_device, mesh=mesh, in_specs=in_specs, out_specs=out_specs, check_vma=False
    )
```

```python
import functools

import jax
import jax.numpy as jnp
from jax import lax
from jax.experimental import pallas as pl
from jax.experimental.pallas import tpu as pltpu
from jax.sharding import PartitionSpec as P

D = 256
ITERS = 3
STEPS = 4

step_size = 1.0
f32 = jnp.float32
bf16 = jnp.bfloat16
LIMIT = 16 * 1024 * 1024


def swap(value, count, mask):
    return lax.ppermute(value, "cell", [(i, i ^ mask) for i in range(count)])


def halves(value):
    upper = value.astype(bf16)
    return upper, (value - upper.astype(f32)).astype(bf16)


def dot3(a, b, left, right):
    dims = (((left,), (right,)), ((), ()))
    dot = functools.partial(lax.dot_general, dimension_numbers=dims, preferred_element_type=f32)
    return dot(a[0], b[0]) + (dot(a[0], b[1]) + dot(a[1], b[0]))


VMEM = pl.BlockSpec(memory_space=pltpu.VMEM)
SMEM = pl.BlockSpec(memory_space=pltpu.SMEM)
HBM = pl.BlockSpec(memory_space=pltpu.HBM)
ANY = pl.BlockSpec(memory_space=pl.ANY)


def far(*arrays):
    return [pltpu.with_memory_space_constraint(a, pltpu.HBM) for a in arrays]


def near(*arrays):
    return [pltpu.with_memory_space_constraint(a, pltpu.VMEM) for a in arrays]


def array(shape, dtype=f32):
    return jax.ShapeDtypeStruct(shape, dtype)


def call(body, name, in_specs, out_specs, out_shape, scratch=(), cost=None):
    return pl.pallas_call(
        body,
        in_specs=in_specs,
        out_specs=out_specs,
        out_shape=out_shape,
        scratch_shapes=list(scratch),
        compiler_params=pltpu.CompilerParams(vmem_limit_bytes=LIMIT),
        cost_estimate=cost,
        name=name,
    )


def rows_of(step, block):
    return pl.ds(pl.multiple_of(step * block, block), block)


def fetch_kernel(qs, qt, qs_out, qt_out, turned, totals, sems):
    pairs = ((qs, qs_out), (qt, qt_out))
    copies = [pltpu.make_async_copy(a, b, sems.at[i]) for i, (a, b) in enumerate(pairs)]
    for copy in copies:
        copy.start()
    rank = qs.shape[1]
    for t, q in enumerate((qs_out, qt_out)):
        copies[t].wait()
        factor = q[...] / rank
        totals[t : t + 1, :] = jnp.sum(factor, axis=0, keepdims=True)
        turned[t] = factor.T.astype(bf16)


def fetch(*arrays):
    rows, rank = arrays[0].shape
    size = sum(a.size * a.dtype.itemsize for a in arrays)
    return call(
        fetch_kernel, "fetch", [HBM] * 2, [VMEM] * 4,
        [pltpu.VMEM(a.shape, a.dtype) for a in arrays]
        + [pltpu.VMEM((2, rank, rows), bf16), array((2, rank))],
        [pltpu.SemaphoreType.DMA((2,))],
        pl.CostEstimate(flops=0, bytes_accessed=size, transcendentals=0),
    )(*far(*arrays))


def stack_kernel(*refs):
    pieces, out = refs[:4], refs[-1]
    for i, piece in enumerate(pieces):
        out[i] = piece[...]


def stack_pieces(pieces, after):
    return call(
        stack_kernel, "stack", [VMEM] * 4 + [ANY] * len(after), VMEM,
        array((4,) + pieces[0].shape, pieces[0].dtype),
    )(*pieces, *after)


def joined_table(me, j, even, odd):
    swapped = (me & 1) == 1
    a, b = even[j], odd[j]
    return jnp.concatenate([jnp.where(swapped, b, a), jnp.where(swapped, a, b)])


def first_kernel(masks, place, xs, xt, even, odd, part_s, part_t, later_s, later_t, held, sems):
    me = place[0]
    width = 2 * even.shape[1]

    def copy(x, mask, out, sem):
        start = pl.multiple_of(((me ^ mask) >> 1) * width, width)
        made = pltpu.make_async_copy(x.at[:, pl.ds(start, width)], out, sem)
        made.start()
        return made

    sets = ((xs, part_s, later_s), (xt, part_t, later_t))
    now = [
        [copy(x, m, held.at[t, j], sems.at[0, t, j]) for j, m in enumerate(masks)]
        for t, (x, _, _) in enumerate(sets)
    ]
    after = [
        copy(x, m | 2, later.at[j], sems.at[1, t, j])
        for t, (x, _, later) in enumerate(sets)
        for j, m in enumerate(masks)
    ]
    for t, (_, part, _) in enumerate(sets):
        value = None
        for j in range(len(masks)):
            now[t][j].wait()
            term = jnp.dot(held[t, j], joined_table(me, j, even, odd), preferred_element_type=f32)
            value = term if value is None else value + term
        part[...] = value
    for made in after:
        made.wait()


def first_half(place, xs, xt, masks, even, odd):
    rows, genes = xs.shape
    blocks, width, dim = even.shape
    held = (blocks, rows, 2 * width)
    return call(
        functools.partial(first_kernel, masks), "embed_first", [SMEM, HBM, HBM, VMEM, VMEM], [VMEM] * 4,
        [array((rows, dim))] * 2 + [pltpu.VMEM(held, bf16)] * 2,
        [pltpu.VMEM((2,) + held, bf16), pltpu.SemaphoreType.DMA((2, 2, blocks))],
        pl.CostEstimate(
            flops=2 * rows * genes * dim, bytes_accessed=4 * rows * genes, transcendentals=0
        ),
    )(place, *far(xs, xt), even, odd)


def gate_kernel(value, after, out):
    out[...] = value[...]


def gate(value, after):
    return call(
        gate_kernel, "gate", [VMEM, ANY], VMEM, array(value.shape, value.dtype)
    )(value, after)


def whole_kernel(masks, place, xs, xt, *refs):
    pieces, (part_s, part_t, table) = refs[:4], refs[4:]
    genes = pieces[0].shape[1]
    for piece, extra in zip(pieces, range(4)):
        for j, mask in enumerate(masks):
            start = pl.multiple_of((place[0] ^ (mask | extra)) * genes, genes)
            table[pl.ds(start, genes), :] = piece[j]
    for x, part in ((xs, part_s), (xt, part_t)):
        part[...] = jnp.dot(x[...], table[...], preferred_element_type=f32)


def whole_product(place, xs, xt, masks, *pieces):
    rows, genes = xs.shape
    dim = pieces[0].shape[2]
    return call(
        functools.partial(whole_kernel, masks), "embed_whole", [SMEM] + [VMEM] * 6, [VMEM] * 2,
        [array((rows, dim))] * 2, [pltpu.VMEM((genes, dim), bf16)],
    )(place, xs, xt, *pieces)


def second_kernel(
    place, live, xs, xt, part_s, part_t, even, odd, qs, qt, turned, totals,
    emb_s, emb_t, own, send,
):
    me = place[0]
    core = me & 1
    rows, rank = qs.shape
    dim = emb_s.shape[1]
    for t, (x, q, part, emb) in enumerate(
        ((xs, qs, part_s, emb_s), (xt, qt, part_t, emb_t))
    ):
        value = part[...]
        for j in range(x.shape[0]):
            table = joined_table(me, j, even, odd)
            value = value + jnp.dot(x[j], table, preferred_element_type=f32)
        emb[...] = value
        norms = jnp.sum(value * value, axis=1, keepdims=True)
        norm_sum = jnp.sum(norms * (q[...] / rank), axis=0, keepdims=True)
        mean = (jnp.sum(value, axis=0, keepdims=True) / rows).astype(bf16).astype(f32)
        rest = jnp.dot(turned[t], (value - mean).astype(bf16), preferred_element_type=f32)
        number = jnp.full((1, rank), live[t].astype(f32))
        tail = jnp.concatenate(
            [mean, totals[t : t + 1, :], norm_sum, number, jnp.zeros((4, rank), f32)]
        )

        def put(out):
            out[0:rank, :] = rest
            out[rank:, :] = tail

        pl.when(core == t)(lambda: put(own))
        pl.when(core != t)(lambda: put(send))


def second_half(place, live, xs, xt, parts, even, odd, qs, qt, turned, totals):
    rows, rank = qs.shape
    dim = even.shape[2]
    return call(
        second_kernel, "embed_second", [SMEM] * 2 + [VMEM] * 10, [VMEM] * 4,
        [array((rows, dim))] * 2 + [array((rank + 8, dim))] * 2,
    )(place, live, *near(xs, xt), *parts, even, odd, *near(qs, qt, turned), totals)


def split_row(row):
    high = row.astype(bf16).astype(f32)
    middle = (row - high).astype(bf16).astype(f32)
    return [high, middle, row - high - middle]


def tail_rows(cards):
    return -(-(8 + 4 * cards) // 16) * 16


def make_tail(norm, number, cards):
    width = norm.shape[1]
    rows = split_row(norm) + split_row(number) + [jnp.zeros((2, width), f32)] + cards
    used = sum(r.shape[0] for r in rows)
    filler = tail_rows((used - 8) // 4) - used
    if filler:
        rows.append(jnp.zeros((filler, width), f32))
    return jnp.concatenate(rows)


def three(tail, start):
    return (tail[start : start + 1] + tail[start + 1 : start + 2]) + tail[start + 2 : start + 3]


def pack_pair_kernel(own, recv, out):
    rank = own.shape[0] - 8
    out[0:rank, :] = (own[0:rank, :] + recv[0:rank, :]).astype(bf16)
    cards = []
    for ref in (own, recv):
        cards += [ref[rank : rank + 1, :]] + split_row(ref[rank + 1 : rank + 2, :])
    norm = own[rank + 2 : rank + 3, :] + recv[rank + 2 : rank + 3, :]
    number = own[rank + 3 : rank + 4, :] + recv[rank + 3 : rank + 4, :]
    out[rank:, :] = make_tail(norm, number, cards).astype(bf16)


def pack_pair(own, recv):
    rank, dim = own.shape[0] - 8, own.shape[1]
    return call(
        pack_pair_kernel, "pack_pair", [VMEM] * 2, VMEM, array((rank + tail_rows(2), dim), bf16)
    )(own, recv)


def pack_next_kernel(rank, cards, bit, place, own, recv, out):
    out[0:rank, :] = (own[0:rank, :].astype(f32) + recv[0:rank, :].astype(f32)).astype(bf16)
    a, b = own[rank:, :].astype(f32), recv[rank:, :].astype(f32)
    first = (place[0] & bit) == 0
    a_cards, b_cards = a[8 : 8 + 4 * cards], b[8 : 8 + 4 * cards]
    ordered = [jnp.where(first, a_cards, b_cards), jnp.where(first, b_cards, a_cards)]
    tail = make_tail(three(a, 0) + three(b, 0), three(a, 3) + three(b, 3), ordered)
    out[rank:, :] = tail.astype(bf16)


def pack_next(rank, cards, bit, place, own, recv):
    return call(
        functools.partial(pack_next_kernel, rank, cards, bit), "pack_next", [SMEM, VMEM, VMEM], VMEM,
        array((rank + tail_rows(2 * cards), own.shape[1]), bf16),
    )(place, own, recv)


def total_kernel(rank, cards, own, low, high, both, out):
    def unpack(ref):
        tail = ref[rank:, :].astype(f32)
        heights, means, sums = [], [], jnp.zeros((1, tail.shape[1]), f32)
        for c in range(cards):
            at = 8 + 4 * c
            heights.append(tail[at + 1 : at + 4])
            means += [tail[at : at + 1]] * 3
            sums = sums + three(tail, at + 1)
        left, right = jnp.concatenate(heights), jnp.concatenate(means)
        joined = lax.dot_general(
            left.T.astype(bf16), right.astype(bf16), (((1,), (0,)), ((), ())),
            preferred_element_type=f32,
        )
        return ref[0:rank, :].astype(f32) + joined, three(tail, 0), sums, three(tail, 3)

    parts = [unpack(ref) for ref in (own, low, high, both)]
    joined = [(a + b) + (c + d) for a, b, c, d in zip(*parts)]
    out[0:rank, :] = joined[0]
    out[rank:, :] = jnp.concatenate(joined[1:] + [jnp.zeros((5, out.shape[1]), f32)])


def total(rank, cards, *payloads):
    dim = payloads[0].shape[1]
    return call(
        functools.partial(total_kernel, rank, cards), "total", [VMEM] * 4, VMEM,
        array((rank + 8, dim)),
    )(*payloads)


def live_rows(step, block, live):
    return lax.broadcasted_iota(jnp.int32, (block, 1), 0) + step * block < live


def store_sums(sums, copies):
    for i in range(copies.shape[0]):
        copies[i] = sums[...]


def kernels_kernel(
    cells, place, live, es, et, qs, qt, mine, other, weights, ks, kt, copies, consts,
    mats, coeffs, sums,
):
    first = (place[0] & 1) == 0
    rows, rank = qs.shape
    block = rows // STEPS

    a, b = mine[...], other[...]
    source, target = jnp.where(first, a, b), jnp.where(first, b, a)
    cross_s, cross_t = source[0:rank].T, target[0:rank].T
    norm_q, total_q = source[rank : rank + 1], source[rank + 1 : rank + 2]
    norm_p, total_p = target[rank : rank + 1], target[rank + 1 : rank + 2]
    col_mass = weights[...] * (cells / rank)
    inverse = 1.0 / (D * col_mass)
    cost = (
        norm_q * total_p + total_q * norm_p
        - 2.0 * jnp.sum(cross_s * cross_t, axis=0, keepdims=True)
    ) / D
    consts[0:1, :] = col_mass * jnp.exp(step_size * cost / (col_mass * col_mass))
    consts[1:2, :] = cells / source[rank + 2 : rank + 3]
    consts[2:3, :] = cells / target[rank + 2 : rank + 3]
    mats[0], mats[1] = halves((-2.0 * inverse) * cross_t)
    mats[2], mats[3] = halves((-2.0 * inverse) * cross_s)
    coeffs[0:1, :] = total_p * inverse
    coeffs[1:2, :] = norm_p * inverse
    coeffs[2:3, :] = total_q * inverse
    coeffs[3:4, :] = norm_q * inverse
    sums[...] = jnp.zeros_like(sums)

    @pl.loop(0, STEPS)
    def _(step):
        at = rows_of(step, block)
        for t, (e, q, k) in enumerate(((es, qs, ks), (et, qt, kt))):
            value = e[at, :]
            norms = jnp.sum(value * value, axis=1, keepdims=True)
            grad = (
                norms * coeffs[2 * t : 2 * t + 1, :] + coeffs[2 * t + 1 : 2 * t + 2, :]
                + dot3(halves(value), (mats[2 * t], mats[2 * t + 1]), 1, 0)
            )
            kernel = (q[at, :] / rank) * jnp.exp(-step_size * grad)
            k[at, :] = kernel
            level = jnp.where(live_rows(step, block, live[t]), consts[1 + t : 2 + t, 0:1], 0.0)
            scale = level / jnp.sum(kernel, axis=1, keepdims=True)
            sums[t : t + 1, :] += jnp.sum(scale * kernel, axis=0, keepdims=True)

    store_sums(sums, copies)


def cube_root(x):
    y = jnp.exp(jnp.log(x) * (1.0 / 3.0))
    refined = y - (y - x / (y * y)) * (1.0 / 3.0)
    return jnp.where((x > 0.0) & (x < jnp.inf), refined, y)


def duals_of(parts, consts):
    sums = jnp.sum(parts[...], axis=0)
    sum_s, sum_t = sums[0:1, :], sums[1:2, :]
    mass = cube_root(consts[0:1, :] * sum_s * sum_t)
    return mass, mass / sum_s, mass / sum_t


def sweep_kernel(last, live, ks, kt, parts, consts, *refs):
    if last:
        ss, st, copies, sums, duals = refs
    else:
        copies, sums, duals = refs
    block = ks.shape[0] // STEPS

    _, duals[0:1, :], duals[1:2, :] = duals_of(parts, consts)
    sums[...] = jnp.zeros_like(sums)

    @pl.loop(0, STEPS)
    def _(step):
        at = rows_of(step, block)
        for t, k in enumerate((ks, kt)):
            kernel = k[at, :]
            weighted = jnp.sum(kernel * duals[t : t + 1, :], axis=1, keepdims=True)
            level = jnp.where(live_rows(step, block, live[t]), consts[1 + t : 2 + t, 0:1], 0.0)
            scaled = (level / weighted) * kernel
            sums[t : t + 1, :] += jnp.sum(scaled, axis=0, keepdims=True)
            if last:
                (ss, st)[t][at, :] = scaled

    store_sums(sums, copies)


def finish_kernel(cells, ss, st, parts, consts, fs, ft, weights, duals, held, sems):
    rows, rank = ss.shape
    block = rows // STEPS
    mass, duals[0:1, :], duals[1:2, :] = duals_of(parts, consts)
    weights[...] = mass * (rank / cells)
    copies = []
    for step in range(STEPS):
        at = slice(step * block, (step + 1) * block)
        for t, (s, out) in enumerate(((ss, fs), (st, ft))):
            held[t, at, :] = rank * (s[at, :] * duals[t : t + 1, :])
            copy = pltpu.make_async_copy(held.at[t, at], out.at[at], sems.at[t, step])
            copy.start()
            copies.append(copy)
    for copy in copies:
        copy.wait()


def kernels(cells, count, place, live, es, et, qs, qt, mine, other, weights):
    rows, rank = qs.shape
    dim = es.shape[1]
    return call(
        functools.partial(kernels_kernel, cells), "kernels", [SMEM, SMEM] + [VMEM] * 7, [VMEM] * 4,
        [array((rows, rank))] * 2 + [array((count, 2, rank)), array((8, rank))],
        [pltpu.VMEM((4, dim, rank), bf16), pltpu.VMEM((8, rank), f32), pltpu.VMEM((2, rank), f32)],
    )(place, live, es, et, *near(qs, qt), mine, other, weights)


def sweep(count, last, live, ks, kt, parts, consts):
    rows, rank = ks.shape
    scaled = [array((rows, rank))] * 2 if last else []
    return call(
        functools.partial(sweep_kernel, last), "sweep", [SMEM] + [VMEM] * 4,
        [VMEM] * (len(scaled) + 1), scaled + [array((count, 2, rank))],
        [pltpu.VMEM((2, rank), f32), pltpu.VMEM((2, rank), f32)],
    )(live, ks, kt, parts, consts)


def finish(cells, ss, st, parts, consts):
    rows, rank = ss.shape
    return call(
        functools.partial(finish_kernel, cells), "finish", [VMEM] * 4, [HBM, HBM, VMEM],
        [array((rows, rank))] * 2 + [array((1, rank))],
        [
            pltpu.VMEM((2, rank), f32),
            pltpu.VMEM((2, rows, rank), f32),
            pltpu.SemaphoreType.DMA((2, STEPS)),
        ],
    )(ss, st, parts, consts)


def on_device(
    source_expr, target_expr, loadings, source_prev, target_prev, weights_prev, live_counts
):
    count = lax.axis_size("cell")
    place = lax.axis_index("cell").astype(jnp.int32)[None]
    live = live_counts[:, 0]
    rows, rank = source_prev.shape
    cells = rows * count
    bits = [1 << b for b in range(count.bit_length() - 1)]
    low, high = bits[-2], bits[-1]
    between = bits[1:-2]
    exchange = functools.partial(lax.all_to_all, axis_name="cell", split_axis=0, concat_axis=0)

    masks = [0, low, high, low | high]
    pieces = [loadings] + [swap(loadings, count, m) for m in masks[1:]]
    qs, qt, turned, totals = fetch(source_prev, target_prev)
    stack = stack_pieces(pieces, [totals])
    for bit in reversed(between[1:]):
        stack = jnp.concatenate([stack, swap(stack, count, bit)])
        masks = masks + [m | bit for m in masks]
    across = swap(stack, count, 2)
    pair = swap(stack, count, 1)
    if loadings.shape[0] % 64 == 0:
        *parts, xs, xt = first_half(place, source_expr, target_expr, masks, stack, pair)
        both = swap(gate(across, parts[0]), count, 1)
    else:
        both = swap(across, count, 1)
        parts = whole_product(place, source_expr, target_expr, masks, stack, pair, across, both)
        xs = xt = jnp.zeros((1, rows, 2 * loadings.shape[0]), bf16)
    emb_s, emb_t, own, send = second_half(
        place, live, xs, xt, parts, across, both, qs, qt, turned, totals
    )

    payload = pack_pair(own, swap(send, count, 1))
    cards = 2
    for bit in between:
        payload = pack_next(rank, cards, bit, place, payload, swap(payload, count, bit))
        cards = 2 * cards
    others = [swap(payload, count, m) for m in (low, high, low | high)]
    mine = total(rank, cards, payload, *others)
    other = swap(mine, count, 1)

    ks, kt, copies, consts = kernels(
        cells, count, place, live, emb_s, emb_t, qs, qt, mine, other, weights_prev[None]
    )
    scaled = []
    for step_index in range(1, ITERS):
        last = step_index == ITERS - 1
        *scaled, copies = sweep(count, last, live, ks, kt, exchange(copies), consts)
    out_s, out_t, weights = finish(cells, *scaled, exchange(copies), consts)
    return out_s, out_t, weights[0]


def solution(mesh):
    in_specs = (
        P(("grp", "cell"), None),
        P(("grp", "cell"), None),
        P("cell", None),
        P(("grp", "cell"), None),
        P(("grp", "cell"), None),
        P("grp"),
        P(None, ("grp", "cell")),
    )
    out_specs = (P(("grp", "cell"), None), P(("grp", "cell"), None), P("grp"))
    return jax.shard_map(
        on_device, mesh=mesh, in_specs=in_specs, out_specs=out_specs, check_vma=False
    )
```

```python
import functools

import jax
import jax.numpy as jnp
from jax import lax
from jax.experimental import pallas as pl
from jax.experimental.pallas import tpu as pltpu
from jax.sharding import PartitionSpec as P

D = 256
ITERS = 3
STEPS = 4

step_size = 1.0
f32 = jnp.float32
bf16 = jnp.bfloat16
LIMIT = 16 * 1024 * 1024


def swap(value, count, mask):
    return lax.ppermute(value, "cell", [(i, i ^ mask) for i in range(count)])


def halves(value):
    upper = value.astype(bf16)
    return upper, (value - upper.astype(f32)).astype(bf16)


def dot3(a, b, left, right):
    dims = (((left,), (right,)), ((), ()))
    dot = functools.partial(lax.dot_general, dimension_numbers=dims, preferred_element_type=f32)
    return dot(a[0], b[0]) + (dot(a[0], b[1]) + dot(a[1], b[0]))


VMEM = pl.BlockSpec(memory_space=pltpu.VMEM)
SMEM = pl.BlockSpec(memory_space=pltpu.SMEM)
HBM = pl.BlockSpec(memory_space=pltpu.HBM)
ANY = pl.BlockSpec(memory_space=pl.ANY)


def far(*arrays):
    return [pltpu.with_memory_space_constraint(a, pltpu.HBM) for a in arrays]


def near(*arrays):
    return [pltpu.with_memory_space_constraint(a, pltpu.VMEM) for a in arrays]


def array(shape, dtype=f32):
    return jax.ShapeDtypeStruct(shape, dtype)


def call(body, name, in_specs, out_specs, out_shape, scratch=(), cost=None):
    return pl.pallas_call(
        body,
        in_specs=in_specs,
        out_specs=out_specs,
        out_shape=out_shape,
        scratch_shapes=list(scratch),
        compiler_params=pltpu.CompilerParams(vmem_limit_bytes=LIMIT),
        cost_estimate=cost,
        name=name,
    )


def rows_of(step, block):
    return pl.ds(pl.multiple_of(step * block, block), block)


def fetch_kernel(qs, qt, qs_out, qt_out, turned, totals, sems):
    pairs = ((qs, qs_out), (qt, qt_out))
    copies = [pltpu.make_async_copy(a, b, sems.at[i]) for i, (a, b) in enumerate(pairs)]
    for copy in copies:
        copy.start()
    rank = qs.shape[1]
    for t, q in enumerate((qs_out, qt_out)):
        copies[t].wait()
        factor = q[...] / rank
        totals[t : t + 1, :] = jnp.sum(factor, axis=0, keepdims=True)
        turned[t] = factor.T.astype(bf16)


def fetch(*arrays):
    rows, rank = arrays[0].shape
    size = sum(a.size * a.dtype.itemsize for a in arrays)
    return call(
        fetch_kernel, "fetch", [HBM] * 2, [VMEM] * 4,
        [pltpu.VMEM(a.shape, a.dtype) for a in arrays]
        + [pltpu.VMEM((2, rank, rows), bf16), array((2, rank))],
        [pltpu.SemaphoreType.DMA((2,))],
        pl.CostEstimate(flops=0, bytes_accessed=size, transcendentals=0),
    )(*far(*arrays))


def stack_kernel(*refs):
    out = refs[-1]
    for i in range(out.shape[0]):
        out[i] = refs[i][...]


def stack_pieces(pieces, after):
    return call(
        stack_kernel, "stack", [VMEM] * len(pieces) + [ANY] * len(after), VMEM,
        array((len(pieces),) + pieces[0].shape, pieces[0].dtype),
    )(*pieces, *after)


def joined_table(me, j, even, odd):
    swapped = (me & 1) == 1
    a, b = even[j], odd[j]
    return jnp.concatenate([jnp.where(swapped, b, a), jnp.where(swapped, a, b)])


def first_kernel(masks, later_masks, place, xs, xt, even, odd, part_s, part_t, later_s, later_t, held, sems):
    me = place[0]
    width = 2 * even.shape[1]

    def copy(x, mask, out, sem):
        start = pl.multiple_of(((me ^ mask) >> 1) * width, width)
        made = pltpu.make_async_copy(x.at[:, pl.ds(start, width)], out, sem)
        made.start()
        return made

    sets = ((xs, part_s, later_s), (xt, part_t, later_t))
    blocks = len(masks)
    now = [
        [copy(x, m, held.at[t, j], sems.at[t, j]) for j, m in enumerate(masks)]
        for t, (x, _, _) in enumerate(sets)
    ]
    after = [
        copy(x, m, later.at[j], sems.at[t, blocks + j])
        for j, m in enumerate(later_masks)
        for t, (x, _, later) in enumerate(sets)
    ]
    for t, (_, part, _) in enumerate(sets):
        value = None
        for j in range(blocks):
            now[t][j].wait()
            term = jnp.dot(held[t, j], joined_table(me, j, even, odd), preferred_element_type=f32)
            value = term if value is None else value + term
        part[...] = value
    for made in after:
        made.wait()


def first_share(place, xs, xt, masks, later_masks, even, odd):
    rows, genes = xs.shape
    blocks, width, dim = even.shape
    later = (len(later_masks), rows, 2 * width)
    return call(
        functools.partial(first_kernel, masks, later_masks), "embed_first",
        [SMEM, HBM, HBM, VMEM, VMEM], [VMEM] * 4,
        [array((rows, dim))] * 2 + [pltpu.VMEM(later, bf16)] * 2,
        [
            pltpu.VMEM((2, blocks, rows, 2 * width), bf16),
            pltpu.SemaphoreType.DMA((2, blocks + len(later_masks))),
        ],
        pl.CostEstimate(
            flops=2 * rows * genes * dim, bytes_accessed=4 * rows * genes, transcendentals=0
        ),
    )(place, *far(xs, xt), even, odd)


def gate_kernel(value, after, out):
    out[...] = value[...]


def gate(value, after):
    return call(
        gate_kernel, "gate", [VMEM, ANY], VMEM, array(value.shape, value.dtype)
    )(value, after)


def next_kernel(at, place, xs, xt, part_s, part_t, even, odd, out_s, out_t):
    me = place[0]
    for x, part, out in ((xs, part_s, out_s), (xt, part_t, out_t)):
        value = part[...]
        for j in range(even.shape[0]):
            table = joined_table(me, j, even, odd)
            value = value + jnp.dot(x[at + j], table, preferred_element_type=f32)
        out[...] = value


def next_share(at, place, xs, xt, parts, even, odd):
    shape = parts[0].shape
    return call(
        functools.partial(next_kernel, at), "embed_next", [SMEM] + [VMEM] * 6, [VMEM] * 2,
        [array(shape)] * 2,
        cost=pl.CostEstimate(
            flops=4 * shape[0] * shape[1] * 4 * even.shape[1], bytes_accessed=0, transcendentals=0
        ),
    )(place, xs, xt, *parts, even, odd)


def whole_kernel(masks, place, xs, xt, *refs):
    pieces, (part_s, part_t, table) = refs[:-3], refs[-3:]
    genes = pieces[0].shape[1]
    for piece, places in zip(pieces, masks):
        for j, mask in enumerate(places):
            start = pl.multiple_of((place[0] ^ mask) * genes, genes)
            table[pl.ds(start, genes), :] = piece[j]
    for x, part in ((xs, part_s), (xt, part_t)):
        part[...] = jnp.dot(x[...], table[...], preferred_element_type=f32)


def whole_product(place, xs, xt, masks, pieces):
    rows, genes = xs.shape
    dim = pieces[0].shape[2]
    return call(
        functools.partial(whole_kernel, masks), "embed_whole", [SMEM] + [VMEM] * (2 + len(pieces)),
        [VMEM] * 2, [array((rows, dim))] * 2, [pltpu.VMEM((genes, dim), bf16)],
    )(place, xs, xt, *pieces)


def cross_kernel(place, live, es, et, qs, qt, turned, totals, own, send):
    core = place[0] & 1
    rows, rank = qs.shape
    for t, (emb, q) in enumerate(((es, qs), (et, qt))):
        value = emb[...]
        norms = jnp.sum(value * value, axis=1, keepdims=True)
        norm_sum = jnp.sum(norms * (q[...] / rank), axis=0, keepdims=True)
        mean = (jnp.sum(value, axis=0, keepdims=True) / rows).astype(bf16).astype(f32)
        rest = jnp.dot(turned[t], (value - mean).astype(bf16), preferred_element_type=f32)
        number = jnp.full((1, rank), live[t].astype(f32))
        tail = jnp.concatenate(
            [mean, totals[t : t + 1, :], norm_sum, number, jnp.zeros((4, rank), f32)]
        )

        def put(out):
            out[0:rank, :] = rest
            out[rank:, :] = tail

        pl.when(core == t)(lambda: put(own))
        pl.when(core != t)(lambda: put(send))


def cross(place, live, es, et, qs, qt, turned, totals):
    rank, dim = qs.shape[1], es.shape[1]
    return call(
        cross_kernel, "cross", [SMEM] * 2 + [VMEM] * 6, [VMEM] * 2, [array((rank + 8, dim))] * 2,
    )(place, live, es, et, *near(qs, qt, turned), totals)


def split_row(row):
    high = row.astype(bf16).astype(f32)
    middle = (row - high).astype(bf16).astype(f32)
    return [high, middle, row - high - middle]


def tail_rows(cards):
    return -(-(8 + 4 * cards) // 16) * 16


def make_tail(norm, number, cards):
    width = norm.shape[1]
    rows = split_row(norm) + split_row(number) + [jnp.zeros((2, width), f32)] + cards
    used = sum(r.shape[0] for r in rows)
    filler = tail_rows((used - 8) // 4) - used
    if filler:
        rows.append(jnp.zeros((filler, width), f32))
    return jnp.concatenate(rows)


def three(tail, start):
    return (tail[start : start + 1] + tail[start + 1 : start + 2]) + tail[start + 2 : start + 3]


def pack_pair_kernel(own, recv, out):
    rank = own.shape[0] - 8
    out[0:rank, :] = (own[0:rank, :] + recv[0:rank, :]).astype(bf16)
    cards = []
    for ref in (own, recv):
        cards += [ref[rank : rank + 1, :]] + split_row(ref[rank + 1 : rank + 2, :])
    norm = own[rank + 2 : rank + 3, :] + recv[rank + 2 : rank + 3, :]
    number = own[rank + 3 : rank + 4, :] + recv[rank + 3 : rank + 4, :]
    out[rank:, :] = make_tail(norm, number, cards).astype(bf16)


def pack_pair(own, recv):
    rank, dim = own.shape[0] - 8, own.shape[1]
    return call(
        pack_pair_kernel, "pack_pair", [VMEM] * 2, VMEM, array((rank + tail_rows(2), dim), bf16)
    )(own, recv)


def ordered_cards(tails, cards, flags):
    lists = [tail[8 : 8 + 4 * cards] for tail in tails]
    for flag in flags:
        lists = [
            jnp.concatenate([jnp.where(flag, a, b), jnp.where(flag, b, a)])
            for a, b in zip(lists[::2], lists[1::2])
        ]
    return lists[0]


def tree(values):
    while len(values) > 1:
        values = [a + b for a, b in zip(values[::2], values[1::2])]
    return values[0]


def merge_kernel(rank, cards, bits, place, *refs):
    payloads, out = refs[:-1], refs[-1]
    out[0:rank, :] = tree([p[0:rank, :].astype(f32) for p in payloads]).astype(bf16)
    tails = [p[rank:, :].astype(f32) for p in payloads]
    listed = ordered_cards(tails, cards, [(place[0] & bit) == 0 for bit in bits])
    norm, number = (tree([three(tail, i) for tail in tails]) for i in (0, 3))
    out[rank:, :] = make_tail(norm, number, [listed]).astype(bf16)


def merge(rank, cards, bits, place, *payloads):
    return call(
        functools.partial(merge_kernel, rank, cards, bits), "merge",
        [SMEM] + [VMEM] * len(payloads), VMEM,
        array((rank + tail_rows(len(payloads) * cards), payloads[0].shape[1]), bf16),
    )(place, *payloads)


def total_kernel(rank, cards, *refs):
    payloads, out = refs[:-1], refs[-1]

    def unpack(ref):
        tail = ref[rank:, :].astype(f32)
        heights, means, sums = [], [], jnp.zeros((1, tail.shape[1]), f32)
        for c in range(cards):
            at = 8 + 4 * c
            heights.append(tail[at + 1 : at + 4])
            means += [tail[at : at + 1]] * 3
            sums = sums + three(tail, at + 1)
        left, right = jnp.concatenate(heights), jnp.concatenate(means)
        joined = lax.dot_general(
            left.T.astype(bf16), right.astype(bf16), (((1,), (0,)), ((), ())),
            preferred_element_type=f32,
        )
        return ref[0:rank, :].astype(f32) + joined, three(tail, 0), sums, three(tail, 3)

    joined = [tree(list(values)) for values in zip(*[unpack(ref) for ref in payloads])]
    out[0:rank, :] = joined[0]
    out[rank:, :] = jnp.concatenate(joined[1:] + [jnp.zeros((5, out.shape[1]), f32)])


def total(rank, cards, *payloads):
    dim = payloads[0].shape[1]
    return call(
        functools.partial(total_kernel, rank, cards), "total", [VMEM] * len(payloads), VMEM,
        array((rank + 8, dim)),
    )(*payloads)


def live_rows(step, block, live):
    return lax.broadcasted_iota(jnp.int32, (block, 1), 0) + step * block < live


def store_sums(sums, copies):
    for i in range(copies.shape[0]):
        copies[i] = sums[...]


def kernels_kernel(
    cells, place, live, es, et, qs, qt, mine, other, weights, ks, kt, copies, consts,
    mats, coeffs, sums,
):
    first = (place[0] & 1) == 0
    rows, rank = qs.shape
    block = rows // STEPS

    a, b = mine[...], other[...]
    source, target = jnp.where(first, a, b), jnp.where(first, b, a)
    cross_s, cross_t = source[0:rank].T, target[0:rank].T
    norm_q, total_q = source[rank : rank + 1], source[rank + 1 : rank + 2]
    norm_p, total_p = target[rank : rank + 1], target[rank + 1 : rank + 2]
    col_mass = weights[...] * (cells / rank)
    inverse = 1.0 / (D * col_mass)
    cost = (
        norm_q * total_p + total_q * norm_p
        - 2.0 * jnp.sum(cross_s * cross_t, axis=0, keepdims=True)
    ) / D
    consts[0:1, :] = col_mass * jnp.exp(step_size * cost / (col_mass * col_mass))
    consts[1:2, :] = cells / source[rank + 2 : rank + 3]
    consts[2:3, :] = cells / target[rank + 2 : rank + 3]
    mats[0], mats[1] = halves((-2.0 * inverse) * cross_t)
    mats[2], mats[3] = halves((-2.0 * inverse) * cross_s)
    coeffs[0:1, :] = total_p * inverse
    coeffs[1:2, :] = norm_p * inverse
    coeffs[2:3, :] = total_q * inverse
    coeffs[3:4, :] = norm_q * inverse
    sums[...] = jnp.zeros_like(sums)

    @pl.loop(0, STEPS)
    def _(step):
        at = rows_of(step, block)
        for t, (e, q, k) in enumerate(((es, qs, ks), (et, qt, kt))):
            value = e[at, :]
            norms = jnp.sum(value * value, axis=1, keepdims=True)
            grad = (
                norms * coeffs[2 * t : 2 * t + 1, :] + coeffs[2 * t + 1 : 2 * t + 2, :]
                + dot3(halves(value), (mats[2 * t], mats[2 * t + 1]), 1, 0)
            )
            kernel = (q[at, :] / rank) * jnp.exp(-step_size * grad)
            k[at, :] = kernel
            level = jnp.where(live_rows(step, block, live[t]), consts[1 + t : 2 + t, 0:1], 0.0)
            scale = level / jnp.sum(kernel, axis=1, keepdims=True)
            sums[t : t + 1, :] += jnp.sum(scale * kernel, axis=0, keepdims=True)

    store_sums(sums, copies)


def cube_root(x):
    y = jnp.exp(jnp.log(x) * (1.0 / 3.0))
    refined = y - (y - x / (y * y)) * (1.0 / 3.0)
    return jnp.where((x > 0.0) & (x < jnp.inf), refined, y)


def duals_of(parts, consts):
    sums = jnp.sum(parts[...], axis=0)
    sum_s, sum_t = sums[0:1, :], sums[1:2, :]
    mass = cube_root(consts[0:1, :] * sum_s * sum_t)
    return mass, mass / sum_s, mass / sum_t


def sweep_kernel(last, live, ks, kt, parts, consts, *refs):
    if last:
        ss, st, copies, sums, duals = refs
    else:
        copies, sums, duals = refs
    block = ks.shape[0] // STEPS

    _, duals[0:1, :], duals[1:2, :] = duals_of(parts, consts)
    sums[...] = jnp.zeros_like(sums)

    @pl.loop(0, STEPS)
    def _(step):
        at = rows_of(step, block)
        for t, k in enumerate((ks, kt)):
            kernel = k[at, :]
            weighted = jnp.sum(kernel * duals[t : t + 1, :], axis=1, keepdims=True)
            level = jnp.where(live_rows(step, block, live[t]), consts[1 + t : 2 + t, 0:1], 0.0)
            scaled = (level / weighted) * kernel
            sums[t : t + 1, :] += jnp.sum(scaled, axis=0, keepdims=True)
            if last:
                (ss, st)[t][at, :] = scaled

    store_sums(sums, copies)


def finish_kernel(cells, ss, st, parts, consts, fs, ft, weights, duals, held, sems):
    rows, rank = ss.shape
    block = rows // STEPS
    mass, duals[0:1, :], duals[1:2, :] = duals_of(parts, consts)
    weights[...] = mass * (rank / cells)
    copies = []
    for step in range(STEPS):
        at = slice(step * block, (step + 1) * block)
        for t, (s, out) in enumerate(((ss, fs), (st, ft))):
            held[t, at, :] = rank * (s[at, :] * duals[t : t + 1, :])
            copy = pltpu.make_async_copy(held.at[t, at], out.at[at], sems.at[t, step])
            copy.start()
            copies.append(copy)
    for copy in copies:
        copy.wait()


def kernels(cells, count, place, live, es, et, qs, qt, mine, other, weights):
    rows, rank = qs.shape
    dim = es.shape[1]
    return call(
        functools.partial(kernels_kernel, cells), "kernels", [SMEM, SMEM] + [VMEM] * 7, [VMEM] * 4,
        [array((rows, rank))] * 2 + [array((count, 2, rank)), array((8, rank))],
        [pltpu.VMEM((4, dim, rank), bf16), pltpu.VMEM((8, rank), f32), pltpu.VMEM((2, rank), f32)],
    )(place, live, es, et, *near(qs, qt), mine, other, weights)


def sweep(count, last, live, ks, kt, parts, consts):
    rows, rank = ks.shape
    scaled = [array((rows, rank))] * 2 if last else []
    return call(
        functools.partial(sweep_kernel, last), "sweep", [SMEM] + [VMEM] * 4,
        [VMEM] * (len(scaled) + 1), scaled + [array((count, 2, rank))],
        [pltpu.VMEM((2, rank), f32), pltpu.VMEM((2, rank), f32)],
    )(live, ks, kt, parts, consts)


def finish(cells, ss, st, parts, consts):
    rows, rank = ss.shape
    return call(
        functools.partial(finish_kernel, cells), "finish", [VMEM] * 4, [HBM, HBM, VMEM],
        [array((rows, rank))] * 2 + [array((1, rank))],
        [
            pltpu.VMEM((2, rank), f32),
            pltpu.VMEM((2, rows, rank), f32),
            pltpu.SemaphoreType.DMA((2, STEPS)),
        ],
    )(ss, st, parts, consts)


def on_device(
    source_expr, target_expr, loadings, source_prev, target_prev, weights_prev, live_counts
):
    count = lax.axis_size("cell")
    place = lax.axis_index("cell").astype(jnp.int32)[None]
    live = live_counts[:, 0]
    rows, rank = source_prev.shape
    cells = rows * count
    bits = [1 << b for b in range(count.bit_length() - 1)]
    opposite = bits[-1] | bits[-2]
    exchange = functools.partial(lax.all_to_all, axis_name="cell", split_axis=0, concat_axis=0)

    qs, qt, turned, totals = fetch(source_prev, target_prev)
    stack = stack_pieces([loadings, swap(loadings, count, opposite)], [totals])
    masks = [0, opposite]
    if count == 16 and loadings.shape[0] % 64 == 0:
        quad = [2, 4, 6]
        arrived = [swap(stack, count, m) for m in quad]
        later = [m ^ q for q in quad for m in masks]
        *parts, xs, xt = first_share(
            place, source_expr, target_expr, masks, later, stack, swap(stack, count, 1)
        )
        arrived = [gate(piece, parts[0]) for piece in arrived]
        for i, piece in enumerate(arrived):
            parts = next_share(2 * i, place, xs, xt, parts, piece, swap(piece, count, 1))
    else:
        for bit in reversed(bits[:-1]):
            stack = jnp.concatenate([stack, swap(stack, count, bit)])
            masks = masks + [m ^ bit for m in masks]
        parts = whole_product(place, source_expr, target_expr, [masks], [stack])
    emb_s, emb_t = parts
    own, send = cross(place, live, emb_s, emb_t, qs, qt, turned, totals)

    payload = pack_pair(own, swap(send, count, 1))
    cards = 2
    inner = bits[1:-1]
    while inner:
        used, inner = inner[:2], inner[2:]
        steps = [used[0], used[1], used[0] | used[1]] if len(used) == 2 else used
        others = [swap(payload, count, m) for m in steps]
        payload = merge(rank, cards, used, place, payload, *others)
        cards = cards * (1 + len(others))
    mine = total(rank, cards, payload, swap(payload, count, opposite))
    other = swap(mine, count, 1)

    ks, kt, copies, consts = kernels(
        cells, count, place, live, emb_s, emb_t, qs, qt, mine, other, weights_prev[None]
    )
    scaled = []
    for step_index in range(1, ITERS):
        last = step_index == ITERS - 1
        *scaled, copies = sweep(count, last, live, ks, kt, exchange(copies), consts)
    out_s, out_t, weights = finish(cells, *scaled, exchange(copies), consts)
    return out_s, out_t, weights[0]


def solution(mesh):
    in_specs = (
        P(("grp", "cell"), None),
        P(("grp", "cell"), None),
        P("cell", None),
        P(("grp", "cell"), None),
        P(("grp", "cell"), None),
        P("grp"),
        P(None, ("grp", "cell")),
    )
    out_specs = (P(("grp", "cell"), None), P(("grp", "cell"), None), P("grp"))
    return jax.shard_map(
        on_device, mesh=mesh, in_specs=in_specs, out_specs=out_specs, check_vma=False
    )
```

```python
import functools

import jax
import jax.numpy as jnp
from jax import lax
from jax.experimental import pallas as pl
from jax.experimental.pallas import tpu as pltpu
from jax.sharding import PartitionSpec as P

D = 256
ITERS = 3
STEPS = 4

step_size = 1.0
f32 = jnp.float32
bf16 = jnp.bfloat16
LIMIT = 16 * 1024 * 1024


def swap(value, count, mask):
    return lax.ppermute(value, "cell", [(i, i ^ mask) for i in range(count)])


def halves(value):
    upper = value.astype(bf16)
    return upper, (value - upper.astype(f32)).astype(bf16)


def dot3(a, b, left, right):
    dims = (((left,), (right,)), ((), ()))
    dot = functools.partial(lax.dot_general, dimension_numbers=dims, preferred_element_type=f32)
    return dot(a[0], b[0]) + (dot(a[0], b[1]) + dot(a[1], b[0]))


VMEM = pl.BlockSpec(memory_space=pltpu.VMEM)
SMEM = pl.BlockSpec(memory_space=pltpu.SMEM)
HBM = pl.BlockSpec(memory_space=pltpu.HBM)
ANY = pl.BlockSpec(memory_space=pl.ANY)


def far(*arrays):
    return [pltpu.with_memory_space_constraint(a, pltpu.HBM) for a in arrays]


def near(*arrays):
    return [pltpu.with_memory_space_constraint(a, pltpu.VMEM) for a in arrays]


def array(shape, dtype=f32):
    return jax.ShapeDtypeStruct(shape, dtype)


def call(body, name, in_specs, out_specs, out_shape, scratch=(), cost=None):
    return pl.pallas_call(
        body,
        in_specs=in_specs,
        out_specs=out_specs,
        out_shape=out_shape,
        scratch_shapes=list(scratch),
        compiler_params=pltpu.CompilerParams(vmem_limit_bytes=LIMIT),
        cost_estimate=cost,
        name=name,
    )


def rows_of(step, block):
    return pl.ds(pl.multiple_of(step * block, block), block)


def fetch_kernel(qs, qt, table, q_out, table_out, turned, totals, sems):
    pairs = ((qs, q_out.at[0]), (qt, q_out.at[1]), (table, table_out))
    copies = [pltpu.make_async_copy(a, b, sems.at[i]) for i, (a, b) in enumerate(pairs)]
    for copy in copies:
        copy.start()
    rank = qs.shape[1]
    for t in range(2):
        copies[t].wait()
        factor = q_out[t] / rank
        totals[t] = jnp.sum(factor, axis=0, keepdims=True)
        turned[t] = factor.T.astype(bf16)
    copies[2].wait()


def fetch(qs, qt, table):
    rows, rank = qs.shape
    return call(
        fetch_kernel, "fetch", [HBM] * 3, [VMEM] * 4,
        [
            pltpu.VMEM((2, rows, rank), f32), pltpu.VMEM(table.shape, table.dtype),
            pltpu.VMEM((2, rank, rows), bf16), array((2, 1, rank)),
        ],
        [pltpu.SemaphoreType.DMA((3,))],
        pl.CostEstimate(flops=0, bytes_accessed=8 * rows * rank, transcendentals=0),
    )(*far(qs, qt, table))


def stack_kernel(*refs):
    out = refs[-1]
    for i in range(out.shape[0]):
        out[i] = refs[i][...]


def stack_pieces(pieces, after):
    return call(
        stack_kernel, "stack", [VMEM] * len(pieces) + [ANY] * len(after), VMEM,
        array((len(pieces),) + pieces[0].shape, pieces[0].dtype),
    )(*pieces, *after)


def joined_table(me, j, even, odd):
    swapped = (me & 1) == 1
    a, b = even[j], odd[j]
    return jnp.concatenate([jnp.where(swapped, b, a), jnp.where(swapped, a, b)])


def first_kernel(masks, later_masks, place, xs, xt, even, odd, part, later, held, sems):
    me = place[0]
    width = 2 * even.shape[1]

    def copy(x, mask, out, sem):
        start = pl.multiple_of(((me ^ mask) >> 1) * width, width)
        made = pltpu.make_async_copy(x.at[:, pl.ds(start, width)], out, sem)
        made.start()
        return made

    blocks = len(masks)
    now = [
        [copy(x, m, held.at[t, j], sems.at[t, j]) for j, m in enumerate(masks)]
        for t, x in enumerate((xs, xt))
    ]
    after = [
        copy(x, m, later.at[t, j], sems.at[t, blocks + j])
        for j, m in enumerate(later_masks)
        for t, x in enumerate((xs, xt))
    ]
    for t in range(2):
        value = None
        for j in range(blocks):
            now[t][j].wait()
            term = jnp.dot(held[t, j], joined_table(me, j, even, odd), preferred_element_type=f32)
            value = term if value is None else value + term
        part[t] = value
    for made in after:
        made.wait()


def first_share(place, xs, xt, masks, later_masks, even, odd):
    rows, genes = xs.shape
    blocks, width, dim = even.shape
    return call(
        functools.partial(first_kernel, masks, later_masks), "embed_first",
        [SMEM, HBM, HBM, VMEM, VMEM], [VMEM] * 2,
        [array((2, rows, dim)), pltpu.VMEM((2, len(later_masks), rows, 2 * width), bf16)],
        [
            pltpu.VMEM((2, blocks, rows, 2 * width), bf16),
            pltpu.SemaphoreType.DMA((2, blocks + len(later_masks))),
        ],
        pl.CostEstimate(
            flops=2 * rows * genes * dim, bytes_accessed=4 * rows * genes, transcendentals=0
        ),
    )(place, *far(xs, xt), even, odd)


def gate_kernel(value, after, out):
    out[...] = value[...]


def gate(value, after):
    return call(
        gate_kernel, "gate", [VMEM, ANY], VMEM, array(value.shape, value.dtype)
    )(value, after)


def next_kernel(at, place, x, part, even, odd, out):
    me = place[0]
    tables = [joined_table(me, j, even, odd) for j in range(even.shape[0])]
    for t in range(2):
        value = part[t]
        for j, table in enumerate(tables):
            value = value + jnp.dot(x[t, at + j], table, preferred_element_type=f32)
        out[t] = value


def next_share(at, place, x, part, even, odd):
    _, rows, dim = part.shape
    return call(
        functools.partial(next_kernel, at), "embed_next", [SMEM] + [VMEM] * 4, VMEM, array(part.shape),
        cost=pl.CostEstimate(
            flops=16 * rows * dim * even.shape[1], bytes_accessed=0, transcendentals=0
        ),
    )(place, x, part, even, odd)


def whole_kernel(masks, place, xs, xt, pieces, part, table):
    genes = pieces.shape[1]
    for j, mask in enumerate(masks):
        start = pl.multiple_of((place[0] ^ mask) * genes, genes)
        table[pl.ds(start, genes), :] = pieces[j]
    for t, x in enumerate((xs, xt)):
        part[t] = jnp.dot(x[...], table[...], preferred_element_type=f32)


def whole_product(place, xs, xt, masks, pieces):
    rows, genes = xs.shape
    dim = pieces.shape[2]
    return call(
        functools.partial(whole_kernel, masks), "embed_whole", [SMEM] + [VMEM] * 3, VMEM,
        array((2, rows, dim)), [pltpu.VMEM((genes, dim), bf16)],
    )(place, xs, xt, pieces)


def fold(value):
    return jnp.sum(value.reshape(value.shape[0] // 8, 8, value.shape[1]), axis=0)


def add_to(sums, value):
    return value if sums is None else sums + value


def cross_kernel(flip, place, live, emb, q, turned, totals, out):
    t = (place[0] & 1) ^ flip
    _, rows, rank = q.shape
    block = rows // STEPS
    means = norms = rest = None
    for step in range(STEPS):
        at = slice(step * block, (step + 1) * block)
        value = emb[t, at, :]
        means = add_to(means, fold(value))
        squares = jnp.sum(value * value, axis=1, keepdims=True)
        norms = add_to(norms, fold(squares * q[t, at, :]))
    mean = (jnp.sum(means, axis=0, keepdims=True) / rows).astype(bf16).astype(f32)
    for step in range(STEPS):
        at = slice(step * block, (step + 1) * block)
        centred = (emb[t, at, :] - mean).astype(bf16)
        rest = add_to(rest, jnp.dot(turned[t, :, at], centred, preferred_element_type=f32))
    norm_sum = jnp.sum(norms, axis=0, keepdims=True) / rank
    lane = lax.broadcasted_iota(jnp.int32, (1, rank), 1)
    number = jnp.where(lane < rank // 2, live[0], live[1]).astype(f32)
    out[0:rank, :] = rest
    out[rank:, :] = jnp.concatenate([mean, totals[t], norm_sum, number, jnp.zeros((4, rank), f32)])


def cross(flip, place, live, emb, q, turned, totals):
    rank, dim = q.shape[2], emb.shape[2]
    return call(
        functools.partial(cross_kernel, flip), "cross", [SMEM] * 2 + [VMEM] * 4, VMEM,
        array((rank + 8, dim)),
        cost=pl.CostEstimate(flops=2 * rank * dim * q.shape[1], bytes_accessed=0, transcendentals=0),
    )(place, live, emb, *near(q, turned), totals)


def split_row(row):
    high = row.astype(bf16).astype(f32)
    middle = (row - high).astype(bf16).astype(f32)
    return [high, middle, row - high - middle]


def tail_rows(cards):
    return -(-(8 + 4 * cards) // 16) * 16


def make_tail(norm, number, cards):
    width = norm.shape[1]
    rows = split_row(norm) + split_row(number) + [jnp.zeros((2, width), f32)] + cards
    used = sum(r.shape[0] for r in rows)
    filler = tail_rows((used - 8) // 4) - used
    if filler:
        rows.append(jnp.zeros((filler, width), f32))
    return jnp.concatenate(rows)


def three(tail, start):
    return (tail[start : start + 1] + tail[start + 1 : start + 2]) + tail[start + 2 : start + 3]


def pack_pair_kernel(own, recv, out):
    rank = own.shape[0] - 8
    out[0:rank, :] = (own[0:rank, :] + recv[0:rank, :]).astype(bf16)
    cards = []
    for ref in (own, recv):
        cards += [ref[rank : rank + 1, :]] + split_row(ref[rank + 1 : rank + 2, :])
    norm = own[rank + 2 : rank + 3, :] + recv[rank + 2 : rank + 3, :]
    number = own[rank + 3 : rank + 4, :] + recv[rank + 3 : rank + 4, :]
    out[rank:, :] = make_tail(norm, number, cards).astype(bf16)


def pack_pair(own, recv):
    rank, dim = own.shape[0] - 8, own.shape[1]
    return call(
        pack_pair_kernel, "pack_pair", [VMEM] * 2, VMEM, array((rank + tail_rows(2), dim), bf16)
    )(own, recv)


def ordered_cards(tails, cards, flags):
    lists = [tail[8 : 8 + 4 * cards] for tail in tails]
    for flag in flags:
        lists = [
            jnp.concatenate([jnp.where(flag, a, b), jnp.where(flag, b, a)])
            for a, b in zip(lists[::2], lists[1::2])
        ]
    return lists[0]


def tree(values):
    while len(values) > 1:
        values = [a + b for a, b in zip(values[::2], values[1::2])]
    return values[0]


def merge_kernel(rank, cards, bits, place, *refs):
    payloads, out = refs[:-1], refs[-1]
    out[0:rank, :] = tree([p[0:rank, :].astype(f32) for p in payloads]).astype(bf16)
    tails = [p[rank:, :].astype(f32) for p in payloads]
    listed = ordered_cards(tails, cards, [(place[0] & bit) == 0 for bit in bits])
    norm, number = (tree([three(tail, i) for tail in tails]) for i in (0, 3))
    out[rank:, :] = make_tail(norm, number, [listed]).astype(bf16)


def merge(rank, cards, bits, place, *payloads):
    return call(
        functools.partial(merge_kernel, rank, cards, bits), "merge",
        [SMEM] + [VMEM] * len(payloads), VMEM,
        array((rank + tail_rows(len(payloads) * cards), payloads[0].shape[1]), bf16),
    )(place, *payloads)


def total_kernel(rank, cards, *refs):
    payloads, out = refs[:-1], refs[-1]

    def unpack(ref):
        tail = ref[rank:, :].astype(f32)
        heights, means, sums = [], [], jnp.zeros((1, tail.shape[1]), f32)
        for c in range(cards):
            at = 8 + 4 * c
            heights.append(tail[at + 1 : at + 4])
            means += [tail[at : at + 1]] * 3
            sums = sums + three(tail, at + 1)
        left, right = jnp.concatenate(heights), jnp.concatenate(means)
        joined = lax.dot_general(
            left.T.astype(bf16), right.astype(bf16), (((1,), (0,)), ((), ())),
            preferred_element_type=f32,
        )
        return ref[0:rank, :].astype(f32) + joined, three(tail, 0), sums, three(tail, 3)

    joined = [tree(list(values)) for values in zip(*[unpack(ref) for ref in payloads])]
    out[0:rank, :] = joined[0]
    out[rank:, :] = jnp.concatenate(joined[1:] + [jnp.zeros((5, out.shape[1]), f32)])


def total(rank, cards, *payloads):
    dim = payloads[0].shape[1]
    return call(
        functools.partial(total_kernel, rank, cards), "total", [VMEM] * len(payloads), VMEM,
        array((rank + 8, dim)),
    )(*payloads)


def live_rows(step, block, live):
    return lax.broadcasted_iota(jnp.int32, (block, 1), 0) + step * block < live


def store_sums(sums, copies):
    both = jnp.concatenate([jnp.sum(part, axis=0, keepdims=True) for part in sums])
    for i in range(copies.shape[0]):
        copies[i] = both


def kernel_half(cells, t, live, emb, q, weights, summed, put):
    _, rows, rank = q.shape
    block = rows // STEPS
    inverse = 1.0 / (D * (weights[...] * (cells / rank)))
    matrix = halves((-2.0 * inverse) * summed[0:rank, :].T)
    slope, offset = summed[rank + 1 : rank + 2, :] * inverse, summed[rank : rank + 1, :] * inverse
    numbers = summed[rank + 2 : rank + 3, :]
    level = cells / jnp.where(t == 0, numbers[:, 0:1], numbers[:, rank // 2 : rank // 2 + 1])
    sums = None
    for step in range(STEPS):
        at = slice(step * block, (step + 1) * block)
        value = emb[t, at, :]
        norms = jnp.sum(value * value, axis=1, keepdims=True)
        grad = norms * slope + offset + dot3(halves(value), matrix, 1, 0)
        kernel = (q[t, at, :] / rank) * jnp.exp(-step_size * grad)
        put(at, kernel)
        scale = jnp.where(live_rows(step, block, live[t]), level, 0.0)
        scale = scale / jnp.sum(kernel, axis=1, keepdims=True)
        sums = add_to(sums, fold(scale * kernel))
    return sums


def other_kernel(cells, place, live, emb, q, weights, mine, k, sums):
    def put(at, kernel):
        k[at, :] = kernel

    t = 1 - (place[0] & 1)
    sums[...] = kernel_half(cells, t, live, emb, q, weights, mine, put)


def own_kernel(cells, place, live, emb, q, weights, mine, other, k_other, sums_other, k, copies, consts):
    core = place[0] & 1
    rank = q.shape[2]

    def put(at, kernel):
        k[core, at, :] = kernel
        k[1 - core, at, :] = k_other[at, :]

    sums_own = kernel_half(cells, core, live, emb, q, weights, other, put)
    sums_out = sums_other[...]
    first = core == 0
    store_sums([jnp.where(first, sums_own, sums_out), jnp.where(first, sums_out, sums_own)], copies)

    a, b = mine[...], other[...]
    col_mass = weights[...] * (cells / rank)
    norm_a, total_a = a[rank : rank + 1], a[rank + 1 : rank + 2]
    norm_b, total_b = b[rank : rank + 1], b[rank + 1 : rank + 2]
    products = jnp.sum((a[0:rank] * b[0:rank]).T, axis=0, keepdims=True)
    mixed_a, mixed_b = norm_a * total_b, total_a * norm_b
    mixed = jnp.where(first, mixed_a, mixed_b) + jnp.where(first, mixed_b, mixed_a)
    cost = (mixed - 2.0 * products) / D
    consts[0:1, :] = col_mass * jnp.exp(step_size * cost / (col_mass * col_mass))
    numbers = a[rank + 2 : rank + 3]
    for t in range(2):
        at = t * (rank // 2)
        consts[1 + t : 2 + t, :] = jnp.broadcast_to(cells / numbers[:, at : at + 1], (1, rank))


def cube_root(x):
    y = jnp.exp(jnp.log(x) * (1.0 / 3.0))
    refined = y - (y - x / (y * y)) * (1.0 / 3.0)
    return jnp.where((x > 0.0) & (x < jnp.inf), refined, y)


def duals_of(parts, consts):
    sums = jnp.sum(parts[...], axis=0)
    sum_s, sum_t = sums[0:1, :], sums[1:2, :]
    mass = cube_root(consts[0:1, :] * sum_s * sum_t)
    return mass, mass / sum_s, mass / sum_t


def sweep_kernel(last, live, k, parts, consts, *refs):
    copies = refs[-1]
    block = k.shape[1] // STEPS

    _, dual_s, dual_t = duals_of(parts, consts)
    sums = [None, None]
    for step in range(STEPS):
        at = slice(step * block, (step + 1) * block)
        for t, dual in enumerate((dual_s, dual_t)):
            kernel = k[t, at, :]
            weighted = jnp.sum(kernel * dual, axis=1, keepdims=True)
            level = jnp.where(live_rows(step, block, live[t]), consts[1 + t : 2 + t, 0:1], 0.0)
            scaled = (level / weighted) * kernel
            if last:
                refs[0][t, at, :] = scaled
            sums[t] = add_to(sums[t], fold(scaled))
    store_sums(sums, copies)


def finish_kernel(cells, scaled, parts, consts, fs, ft, weights, held, sems):
    _, rows, rank = scaled.shape
    block = rows // STEPS
    mass, dual_s, dual_t = duals_of(parts, consts)
    weights[...] = mass * (rank / cells)
    copies = []
    for step in range(STEPS):
        at = slice(step * block, (step + 1) * block)
        for t, (dual, out) in enumerate(((dual_s, fs), (dual_t, ft))):
            held[t, at, :] = rank * (scaled[t, at, :] * dual)
            copy = pltpu.make_async_copy(held.at[t, at], out.at[at], sems.at[t, step])
            copy.start()
            copies.append(copy)
    for copy in copies:
        copy.wait()


def kernels(cells, count, place, live, emb, q, weights, mine, other):
    _, rows, rank = q.shape
    dim = emb.shape[2]
    k_other, sums_other = call(
        functools.partial(other_kernel, cells), "kernel_other", [SMEM, SMEM] + [VMEM] * 4, [VMEM] * 2,
        [array((rows, rank)), array((8, rank))],
        cost=pl.CostEstimate(flops=6 * rows * rank * dim, bytes_accessed=0, transcendentals=rows * rank),
    )(place, live, emb, *near(q), weights, mine)
    return call(
        functools.partial(own_kernel, cells), "kernel_own", [SMEM, SMEM] + [VMEM] * 7, [VMEM] * 3,
        [array((2, rows, rank)), array((count, 2, rank)), array((8, rank))],
        cost=pl.CostEstimate(flops=6 * rows * rank * dim, bytes_accessed=0, transcendentals=rows * rank),
    )(place, live, emb, *near(q), weights, mine, other, k_other, sums_other)


def sweep(count, last, live, k, parts, consts):
    _, rows, rank = k.shape
    scaled = [array((2, rows, rank))] if last else []
    return call(
        functools.partial(sweep_kernel, last), "sweep", [SMEM] + [VMEM] * 3,
        [VMEM] * (len(scaled) + 1), scaled + [array((count, 2, rank))],
    )(live, k, parts, consts)


def finish(cells, scaled, parts, consts):
    _, rows, rank = scaled.shape
    return call(
        functools.partial(finish_kernel, cells), "finish", [VMEM] * 3, [HBM, HBM, VMEM],
        [array((rows, rank))] * 2 + [array((1, rank))],
        [pltpu.VMEM((2, rows, rank), f32), pltpu.SemaphoreType.DMA((2, STEPS))],
    )(scaled, parts, consts)


def on_device(
    source_expr, target_expr, loadings, source_prev, target_prev, weights_prev, live_counts
):
    count = lax.axis_size("cell")
    place = lax.axis_index("cell").astype(jnp.int32)[None]
    live = live_counts[:, 0]
    rows, rank = source_prev.shape
    cells = rows * count
    bits = [1 << b for b in range(count.bit_length() - 1)]
    opposite = bits[-1] | bits[-2]
    exchange = functools.partial(lax.all_to_all, axis_name="cell", split_axis=0, concat_axis=0)

    q, own_table, turned, totals = fetch(source_prev, target_prev, loadings)
    stack = stack_pieces([own_table, swap(loadings, count, opposite)], [totals])
    masks = [0, opposite]
    if count == 16 and loadings.shape[0] % 64 == 0:
        quad = [2, 4, 6]
        arrived = [swap(stack, count, m) for m in quad]
        later = [m ^ q for q in quad for m in masks]
        emb, x = first_share(
            place, source_expr, target_expr, masks, later, stack, swap(stack, count, 1)
        )
        arrived = [gate(piece, emb) for piece in arrived]
        for i, piece in enumerate(arrived):
            emb = next_share(2 * i, place, x, emb, piece, swap(piece, count, 1))
    else:
        for bit in reversed(bits[:-1]):
            stack = jnp.concatenate([stack, swap(stack, count, bit)])
            masks = masks + [m ^ bit for m in masks]
        emb = whole_product(place, source_expr, target_expr, masks, stack)
    send = cross(1, place, live, emb, q, turned, totals)
    own = cross(0, place, live, emb, q, turned, totals)

    payload = pack_pair(own, swap(send, count, 1))
    cards = 2
    inner = bits[1:-1]
    while inner:
        used, inner = inner[:2], inner[2:]
        steps = [used[0], used[1], used[0] | used[1]] if len(used) == 2 else used
        others = [swap(payload, count, m) for m in steps]
        payload = merge(rank, cards, used, place, payload, *others)
        cards = cards * (1 + len(others))
    mine = total(rank, cards, payload, swap(payload, count, opposite))
    other = swap(mine, count, 1)

    k, copies, consts = kernels(
        cells, count, place, live, emb, q, weights_prev[None], mine, other
    )
    scaled = []
    for step_index in range(1, ITERS):
        last = step_index == ITERS - 1
        *scaled, copies = sweep(count, last, live, k, exchange(copies), consts)
    out_s, out_t, weights = finish(cells, *scaled, exchange(copies), consts)
    return out_s, out_t, weights[0]


def solution(mesh):
    in_specs = (
        P(("grp", "cell"), None),
        P(("grp", "cell"), None),
        P("cell", None),
        P(("grp", "cell"), None),
        P(("grp", "cell"), None),
        P("grp"),
        P(None, ("grp", "cell")),
    )
    out_specs = (P(("grp", "cell"), None), P(("grp", "cell"), None), P("grp"))
    return jax.shard_map(
        on_device, mesh=mesh, in_specs=in_specs, out_specs=out_specs, check_vma=False
    )
```

```python
import functools

import jax
import jax.numpy as jnp
from jax import lax
from jax.experimental import pallas as pl
from jax.experimental.pallas import tpu as pltpu
from jax.sharding import PartitionSpec as P

D = 256
ITERS = 3
STEPS = 4

step_size = 1.0
f32 = jnp.float32
bf16 = jnp.bfloat16
LIMIT = 16 * 1024 * 1024


def swap(value, count, mask):
    return lax.ppermute(value, "cell", [(i, i ^ mask) for i in range(count)])


def halves(value):
    upper = value.astype(bf16)
    return upper, (value - upper.astype(f32)).astype(bf16)


def dot3(a, b, left, right):
    dims = (((left,), (right,)), ((), ()))
    dot = functools.partial(lax.dot_general, dimension_numbers=dims, preferred_element_type=f32)
    return dot(a[0], b[0]) + (dot(a[0], b[1]) + dot(a[1], b[0]))


VMEM = pl.BlockSpec(memory_space=pltpu.VMEM)
SMEM = pl.BlockSpec(memory_space=pltpu.SMEM)
HBM = pl.BlockSpec(memory_space=pltpu.HBM)
ANY = pl.BlockSpec(memory_space=pl.ANY)


def far(*arrays):
    return [pltpu.with_memory_space_constraint(a, pltpu.HBM) for a in arrays]


def near(*arrays):
    return [pltpu.with_memory_space_constraint(a, pltpu.VMEM) for a in arrays]


def array(shape, dtype=f32):
    return jax.ShapeDtypeStruct(shape, dtype)


def call(body, name, in_specs, out_specs, out_shape, scratch=(), cost=None):
    return pl.pallas_call(
        body,
        in_specs=in_specs,
        out_specs=out_specs,
        out_shape=out_shape,
        scratch_shapes=list(scratch),
        compiler_params=pltpu.CompilerParams(vmem_limit_bytes=LIMIT),
        cost_estimate=cost,
        name=name,
    )


def rows_of(step, block):
    return pl.ds(pl.multiple_of(step * block, block), block)


def fetch_kernel(qs, qt, table, q_out, table_out, turned, totals, sems):
    pairs = ((qs, q_out.at[0]), (qt, q_out.at[1]), (table, table_out))
    copies = [pltpu.make_async_copy(a, b, sems.at[i]) for i, (a, b) in enumerate(pairs)]
    for copy in copies:
        copy.start()
    rank = qs.shape[1]
    for t in range(2):
        copies[t].wait()
        factor = q_out[t] / rank
        totals[t] = jnp.sum(factor, axis=0, keepdims=True)
        turned[t] = factor.T.astype(bf16)
    copies[2].wait()


def fetch(qs, qt, table):
    rows, rank = qs.shape
    return call(
        fetch_kernel, "fetch", [HBM] * 3, [VMEM] * 4,
        [
            pltpu.VMEM((2, rows, rank), f32), pltpu.VMEM(table.shape, table.dtype),
            pltpu.VMEM((2, rank, rows), bf16), array((2, 1, rank)),
        ],
        [pltpu.SemaphoreType.DMA((3,))],
        pl.CostEstimate(flops=0, bytes_accessed=8 * rows * rank, transcendentals=0),
    )(*far(qs, qt, table))


def stack_kernel(*refs):
    out = refs[-1]
    for i in range(out.shape[0]):
        out[i] = refs[i][...]


def stack_pieces(pieces, after):
    return call(
        stack_kernel, "stack", [VMEM] * len(pieces) + [ANY] * len(after), VMEM,
        array((len(pieces),) + pieces[0].shape, pieces[0].dtype),
    )(*pieces, *after)


def joined_table(me, j, even, odd):
    swapped = (me & 1) == 1
    a, b = even[j], odd[j]
    return jnp.concatenate([jnp.where(swapped, b, a), jnp.where(swapped, a, b)])


def first_kernel(masks, later_masks, place, xs, xt, even, odd, part, later, held, sems):
    me = place[0]
    width = 2 * even.shape[1]

    def copy(x, mask, out, sem):
        start = pl.multiple_of(((me ^ mask) >> 1) * width, width)
        made = pltpu.make_async_copy(x.at[:, pl.ds(start, width)], out, sem)
        made.start()
        return made

    blocks = len(masks)
    now = [
        [copy(x, m, held.at[t, j], sems.at[t, j]) for j, m in enumerate(masks)]
        for t, x in enumerate((xs, xt))
    ]
    after = [
        copy(x, m, later.at[t, j], sems.at[t, blocks + j])
        for j, m in enumerate(later_masks)
        for t, x in enumerate((xs, xt))
    ]
    for t in range(2):
        value = None
        for j in range(blocks):
            now[t][j].wait()
            term = jnp.dot(held[t, j], joined_table(me, j, even, odd), preferred_element_type=f32)
            value = term if value is None else value + term
        part[t] = value
    for made in after:
        made.wait()


def first_share(place, xs, xt, masks, later_masks, even, odd):
    rows, genes = xs.shape
    blocks, width, dim = even.shape
    return call(
        functools.partial(first_kernel, masks, later_masks), "embed_first",
        [SMEM, HBM, HBM, VMEM, VMEM], [VMEM] * 2,
        [array((2, rows, dim)), pltpu.VMEM((2, len(later_masks), rows, 2 * width), bf16)],
        [
            pltpu.VMEM((2, blocks, rows, 2 * width), bf16),
            pltpu.SemaphoreType.DMA((2, blocks + len(later_masks))),
        ],
        pl.CostEstimate(
            flops=2 * rows * genes * dim, bytes_accessed=4 * rows * genes, transcendentals=0
        ),
    )(place, *far(xs, xt), even, odd)


def gate_kernel(value, after, out):
    out[...] = value[...]


def gate(value, after):
    return call(
        gate_kernel, "gate", [VMEM, ANY], VMEM, array(value.shape, value.dtype)
    )(value, after)


def next_kernel(at, place, x, part, even, odd, out):
    me = place[0]
    tables = [joined_table(me, j, even, odd) for j in range(even.shape[0])]
    for t in range(2):
        value = part[t]
        for j, table in enumerate(tables):
            value = value + jnp.dot(x[t, at + j], table, preferred_element_type=f32)
        out[t] = value


def next_share(at, place, x, part, even, odd):
    _, rows, dim = part.shape
    return call(
        functools.partial(next_kernel, at), "embed_next", [SMEM] + [VMEM] * 4, VMEM, array(part.shape),
        cost=pl.CostEstimate(
            flops=16 * rows * dim * even.shape[1], bytes_accessed=0, transcendentals=0
        ),
    )(place, x, part, even, odd)


def whole_kernel(masks, place, xs, xt, pieces, part, table):
    genes = pieces.shape[1]
    for j, mask in enumerate(masks):
        start = pl.multiple_of((place[0] ^ mask) * genes, genes)
        table[pl.ds(start, genes), :] = pieces[j]
    for t, x in enumerate((xs, xt)):
        part[t] = jnp.dot(x[...], table[...], preferred_element_type=f32)


def whole_product(place, xs, xt, masks, pieces):
    rows, genes = xs.shape
    dim = pieces.shape[2]
    return call(
        functools.partial(whole_kernel, masks), "embed_whole", [SMEM] + [VMEM] * 3, VMEM,
        array((2, rows, dim)), [pltpu.VMEM((genes, dim), bf16)],
    )(place, xs, xt, pieces)


def fold(value):
    return jnp.sum(value.reshape(value.shape[0] // 8, 8, value.shape[1]), axis=0)


def add_to(sums, value):
    return value if sums is None else sums + value


def cross_kernel(flip, place, live, emb, q, turned, totals, out, *masks):
    t = (place[0] & 1) ^ flip
    _, rows, rank = q.shape
    block = rows // STEPS
    means = norms = rest = None
    for step in range(STEPS):
        at = slice(step * block, (step + 1) * block)
        value = emb[t, at, :]
        means = add_to(means, fold(value))
        squares = jnp.sum(value * value, axis=1, keepdims=True)
        norms = add_to(norms, fold(squares * q[t, at, :]))
    mean = (jnp.sum(means, axis=0, keepdims=True) / rows).astype(bf16).astype(f32)
    for step in range(STEPS):
        at = slice(step * block, (step + 1) * block)
        centred = (emb[t, at, :] - mean).astype(bf16)
        rest = add_to(rest, jnp.dot(turned[t, :, at], centred, preferred_element_type=f32))
    norm_sum = jnp.sum(norms, axis=0, keepdims=True) / rank
    lane = lax.broadcasted_iota(jnp.int32, (1, rank), 1)
    number = jnp.where(lane < rank // 2, live[0], live[1]).astype(f32)
    out[0:rank, :] = rest
    out[rank:, :] = jnp.concatenate([mean, totals[t], norm_sum, number, jnp.zeros((4, rank), f32)])
    for mask in masks:
        for i in range(2):
            mask[i] = (lax.broadcasted_iota(jnp.int32, (rows, 1), 0) < live[i]).astype(f32)


def cross(flip, place, live, emb, q, turned, totals):
    _, rows, rank = q.shape
    dim = emb.shape[2]
    masks = [] if flip else [array((2, rows, 1))]
    return call(
        functools.partial(cross_kernel, flip), "cross", [SMEM] * 2 + [VMEM] * 4,
        [VMEM] * (1 + len(masks)), [array((rank + 8, dim))] + masks,
        cost=pl.CostEstimate(flops=2 * rank * dim * q.shape[1], bytes_accessed=0, transcendentals=0),
    )(place, live, emb, *near(q, turned), totals)


def split_row(row):
    high = row.astype(bf16).astype(f32)
    middle = (row - high).astype(bf16).astype(f32)
    return [high, middle, row - high - middle]


def tail_rows(cards):
    return -(-(8 + 4 * cards) // 16) * 16


def make_tail(norm, number, cards):
    width = norm.shape[1]
    rows = split_row(norm) + split_row(number) + [jnp.zeros((2, width), f32)] + cards
    used = sum(r.shape[0] for r in rows)
    filler = tail_rows((used - 8) // 4) - used
    if filler:
        rows.append(jnp.zeros((filler, width), f32))
    return jnp.concatenate(rows)


def three(tail, start):
    return (tail[start : start + 1] + tail[start + 1 : start + 2]) + tail[start + 2 : start + 3]


def pack_pair_kernel(own, recv, out):
    rank = own.shape[0] - 8
    out[0:rank, :] = (own[0:rank, :] + recv[0:rank, :]).astype(bf16)
    cards = []
    for ref in (own, recv):
        cards += [ref[rank : rank + 1, :]] + split_row(ref[rank + 1 : rank + 2, :])
    norm = own[rank + 2 : rank + 3, :] + recv[rank + 2 : rank + 3, :]
    number = own[rank + 3 : rank + 4, :] + recv[rank + 3 : rank + 4, :]
    out[rank:, :] = make_tail(norm, number, cards).astype(bf16)


def pack_pair(own, recv):
    rank, dim = own.shape[0] - 8, own.shape[1]
    return call(
        pack_pair_kernel, "pack_pair", [VMEM] * 2, VMEM, array((rank + tail_rows(2), dim), bf16)
    )(own, recv)


def ordered_cards(tails, cards, flags):
    lists = [tail[8 : 8 + 4 * cards] for tail in tails]
    for flag in flags:
        lists = [
            jnp.concatenate([jnp.where(flag, a, b), jnp.where(flag, b, a)])
            for a, b in zip(lists[::2], lists[1::2])
        ]
    return lists[0]


def tree(values):
    while len(values) > 1:
        values = [a + b for a, b in zip(values[::2], values[1::2])]
    return values[0]


def merge_kernel(rank, cards, bits, place, *refs):
    payloads, out = refs[:-1], refs[-1]
    out[0:rank, :] = tree([p[0:rank, :].astype(f32) for p in payloads]).astype(bf16)
    tails = [p[rank:, :].astype(f32) for p in payloads]
    listed = ordered_cards(tails, cards, [(place[0] & bit) == 0 for bit in bits])
    norm, number = (tree([three(tail, i) for tail in tails]) for i in (0, 3))
    out[rank:, :] = make_tail(norm, number, [listed]).astype(bf16)


def merge(rank, cards, bits, place, *payloads):
    return call(
        functools.partial(merge_kernel, rank, cards, bits), "merge",
        [SMEM] + [VMEM] * len(payloads), VMEM,
        array((rank + tail_rows(len(payloads) * cards), payloads[0].shape[1]), bf16),
    )(place, *payloads)


def total_kernel(rank, cards, *refs):
    payloads, out = refs[:-1], refs[-1]

    def unpack(ref):
        tail = ref[rank:, :].astype(f32)
        heights, means, sums = [], [], jnp.zeros((1, tail.shape[1]), f32)
        for c in range(cards):
            at = 8 + 4 * c
            heights.append(tail[at + 1 : at + 4])
            means += [tail[at : at + 1]] * 3
            sums = sums + three(tail, at + 1)
        left, right = jnp.concatenate(heights), jnp.concatenate(means)
        joined = lax.dot_general(
            left.T.astype(bf16), right.astype(bf16), (((1,), (0,)), ((), ())),
            preferred_element_type=f32,
        )
        return ref[0:rank, :].astype(f32) + joined, three(tail, 0), sums, three(tail, 3)

    joined = [tree(list(values)) for values in zip(*[unpack(ref) for ref in payloads])]
    out[0:rank, :] = joined[0]
    out[rank:, :] = jnp.concatenate(joined[1:] + [jnp.zeros((5, out.shape[1]), f32)])


def total(rank, cards, *payloads):
    dim = payloads[0].shape[1]
    return call(
        functools.partial(total_kernel, rank, cards), "total", [VMEM] * len(payloads), VMEM,
        array((rank + 8, dim)),
    )(*payloads)


def store_sums(sums, levels, copies):
    both = jnp.concatenate(
        [level * jnp.sum(part, axis=0, keepdims=True) for part, level in zip(sums, levels)]
    )
    for i in range(copies.shape[0]):
        copies[i] = both


def kernel_half(cells, t, mask, emb, q, weights, summed, k, sums_out):
    _, rows, rank = q.shape
    block = rows // STEPS
    inverse = 1.0 / (D * (weights[...] * (cells / rank)))
    matrix = halves((-2.0 * inverse) * summed[0:rank, :].T)
    slope, offset = summed[rank + 1 : rank + 2, :] * inverse, summed[rank : rank + 1, :] * inverse
    sums = None
    for step in range(STEPS):
        at = slice(step * block, (step + 1) * block)
        value = emb[t, at, :]
        norms = jnp.sum(value * value, axis=1, keepdims=True)
        grad = norms * slope + offset + dot3(halves(value), matrix, 1, 0)
        kernel = (q[t, at, :] / rank) * jnp.exp(-step_size * grad)
        k[at, :] = kernel
        scale = mask[t, at, :] / jnp.sum(kernel, axis=1, keepdims=True)
        sums = add_to(sums, fold(scale * kernel))
    sums_out[...] = sums


def other_kernel(cells, place, mask, emb, q, weights, mine, k, sums):
    kernel_half(cells, 1 - (place[0] & 1), mask, emb, q, weights, mine, k, sums)


def levels_of(cells, summed):
    rank = summed.shape[1]
    numbers = summed[rank + 2 : rank + 3, :]
    return cells / numbers[:, 0:1], cells / numbers[:, rank // 2 : rank // 2 + 1]


def in_order(first, own, out):
    return jnp.where(first, own, out), jnp.where(first, out, own)


def write_tables(cells, first, weights, mine, other, consts):
    rank = weights.shape[1]
    a, b = mine[...], other[...]
    col_mass = weights[...] * (cells / rank)
    norm_a, total_a = a[rank : rank + 1], a[rank + 1 : rank + 2]
    norm_b, total_b = b[rank : rank + 1], b[rank + 1 : rank + 2]
    products = jnp.sum((a[0:rank] * b[0:rank]).T, axis=0, keepdims=True)
    mixed = in_order(first, norm_a * total_b, total_a * norm_b)
    cost = (mixed[0] + mixed[1] - 2.0 * products) / D
    consts[0:1, :] = col_mass * jnp.exp(step_size * cost / (col_mass * col_mass))
    for t, level in enumerate(levels_of(cells, mine)):
        consts[1 + t : 2 + t, :] = jnp.broadcast_to(level, (1, rank))


def own_kernel(cells, place, mask, emb, q, weights, mine, other, sums_other, k, copies, consts, sums):
    core = place[0] & 1
    write_tables(cells, core == 0, weights, mine, other, consts)
    kernel_half(cells, core, mask, emb, q, weights, other, k, sums)
    store_sums(in_order(core == 0, sums[...], sums_other[...]), levels_of(cells, mine), copies)


def cube_root(x):
    y = jnp.exp(jnp.log(x) * (1.0 / 3.0))
    refined = y - (y - x / (y * y)) * (1.0 / 3.0)
    return jnp.where((x > 0.0) & (x < jnp.inf), refined, y)


def duals_of(parts, consts):
    sums = jnp.sum(parts[...], axis=0)
    sum_s, sum_t = sums[0:1, :], sums[1:2, :]
    mass = cube_root(consts[0:1, :] * sum_s * sum_t)
    return mass, mass / sum_s, mass / sum_t


def sweep_kernel(last, place, mask, k_own, k_other, parts, consts, *refs):
    copies = refs[-1]
    core = place[0] & 1
    first = core == 0
    block = k_own.shape[0] // STEPS

    _, *duals = duals_of(parts, consts)
    sums = [None, None]
    for step in range(STEPS):
        at = slice(step * block, (step + 1) * block)
        for i, (k, t, dual) in enumerate(
            zip((k_own, k_other), (core, 1 - core), in_order(first, *duals))
        ):
            kernel = k[at, :]
            weighted = jnp.sum(kernel * dual, axis=1, keepdims=True)
            scaled = (mask[t, at, :] / weighted) * kernel
            if last:
                refs[0][t, at, :] = scaled
            sums[i] = add_to(sums[i], fold(scaled))
    store_sums(in_order(first, *sums), (consts[1:2, :], consts[2:3, :]), copies)


def finish_kernel(cells, scaled, parts, consts, fs, ft, weights, held, sems):
    _, rows, rank = scaled.shape
    block = rows // STEPS
    mass, dual_s, dual_t = duals_of(parts, consts)
    weights[...] = mass * (rank / cells)
    dual_s, dual_t = dual_s * (rank * consts[1:2, :]), dual_t * (rank * consts[2:3, :])
    copies = []
    for step in range(STEPS):
        at = slice(step * block, (step + 1) * block)
        for t, (dual, out) in enumerate(((dual_s, fs), (dual_t, ft))):
            held[t, at, :] = scaled[t, at, :] * dual
            copy = pltpu.make_async_copy(held.at[t, at], out.at[at], sems.at[t, step])
            copy.start()
            copies.append(copy)
    for copy in copies:
        copy.wait()


def kernels(cells, count, place, mask, emb, q, weights, mine, other):
    _, rows, rank = q.shape
    dim = emb.shape[2]
    cost = pl.CostEstimate(flops=6 * rows * rank * dim, bytes_accessed=0, transcendentals=rows * rank)
    k_other, sums_other = call(
        functools.partial(other_kernel, cells), "kernel_other", [SMEM] + [VMEM] * 5, [VMEM] * 2,
        [array((rows, rank)), array((8, rank))], cost=cost,
    )(place, mask, emb, *near(q), weights, mine)
    k_own, copies, consts = call(
        functools.partial(own_kernel, cells), "kernel_own", [SMEM] + [VMEM] * 7, [VMEM] * 3,
        [array((rows, rank)), array((count, 2, rank)), array((8, rank))], [pltpu.VMEM((8, rank), f32)], cost,
    )(place, mask, emb, *near(q), weights, mine, other, sums_other)
    return k_own, k_other, copies, consts


def sweep(count, last, place, mask, k_own, k_other, parts, consts):
    rows, rank = k_own.shape
    scaled = [array((2, rows, rank))] if last else []
    return call(
        functools.partial(sweep_kernel, last), "sweep", [SMEM] + [VMEM] * 5,
        [VMEM] * (len(scaled) + 1), scaled + [array((count, 2, rank))],
    )(place, mask, k_own, k_other, parts, consts)


def finish(cells, scaled, parts, consts):
    _, rows, rank = scaled.shape
    return call(
        functools.partial(finish_kernel, cells), "finish", [VMEM] * 3, [HBM, HBM, VMEM],
        [array((rows, rank))] * 2 + [array((1, rank))],
        [pltpu.VMEM((2, rows, rank), f32), pltpu.SemaphoreType.DMA((2, STEPS))],
    )(scaled, parts, consts)


def on_device(
    source_expr, target_expr, loadings, source_prev, target_prev, weights_prev, live_counts
):
    count = lax.axis_size("cell")
    place = lax.axis_index("cell").astype(jnp.int32)[None]
    live = live_counts[:, 0]
    rows, rank = source_prev.shape
    cells = rows * count
    bits = [1 << b for b in range(count.bit_length() - 1)]
    opposite = bits[-1] | bits[-2]
    exchange = functools.partial(lax.all_to_all, axis_name="cell", split_axis=0, concat_axis=0)

    q, own_table, turned, totals = fetch(source_prev, target_prev, loadings)
    stack = stack_pieces([own_table, swap(loadings, count, opposite)], [totals])
    masks = [0, opposite]
    if count == 16 and loadings.shape[0] % 64 == 0:
        quad = [2, 4, 6]
        arrived = [swap(stack, count, m) for m in quad]
        later = [m ^ q for q in quad for m in masks]
        emb, x = first_share(
            place, source_expr, target_expr, masks, later, stack, swap(stack, count, 1)
        )
        arrived = [gate(piece, emb) for piece in arrived]
        for i, piece in enumerate(arrived):
            emb = next_share(2 * i, place, x, emb, piece, swap(piece, count, 1))
    else:
        for bit in reversed(bits[:-1]):
            stack = jnp.concatenate([stack, swap(stack, count, bit)])
            masks = masks + [m ^ bit for m in masks]
        emb = whole_product(place, source_expr, target_expr, masks, stack)
    (send,) = cross(1, place, live, emb, q, turned, totals)
    own, mask = cross(0, place, live, emb, q, turned, totals)

    payload = pack_pair(own, swap(send, count, 1))
    cards = 2
    inner = bits[1:-1]
    while inner:
        used, inner = inner[:2], inner[2:]
        steps = [used[0], used[1], used[0] | used[1]] if len(used) == 2 else used
        others = [swap(payload, count, m) for m in steps]
        payload = merge(rank, cards, used, place, payload, *others)
        cards = cards * (1 + len(others))
    mine = total(rank, cards, payload, swap(payload, count, opposite))
    other = swap(mine, count, 1)

    k_own, k_other, copies, consts = kernels(
        cells, count, place, mask, emb, q, weights_prev[None], mine, other
    )
    scaled = []
    for step_index in range(1, ITERS):
        last = step_index == ITERS - 1
        *scaled, copies = sweep(count, last, place, mask, k_own, k_other, exchange(copies), consts)
    out_s, out_t, weights = finish(cells, *scaled, exchange(copies), consts)
    return out_s, out_t, weights[0]


def solution(mesh):
    in_specs = (
        P(("grp", "cell"), None),
        P(("grp", "cell"), None),
        P("cell", None),
        P(("grp", "cell"), None),
        P(("grp", "cell"), None),
        P("grp"),
        P(None, ("grp", "cell")),
    )
    out_specs = (P(("grp", "cell"), None), P(("grp", "cell"), None), P("grp"))
    return jax.shard_map(
        on_device, mesh=mesh, in_specs=in_specs, out_specs=out_specs, check_vma=False
    )
```

```python
import functools

import jax
import jax.numpy as jnp
from jax import lax
from jax.experimental import pallas as pl
from jax.experimental.pallas import tpu as pltpu
from jax.sharding import PartitionSpec as P

D = 256
ITERS = 3
STEPS = 4

step_size = 1.0
f32 = jnp.float32
bf16 = jnp.bfloat16
LIMIT = 16 * 1024 * 1024


def swap(value, count, mask):
    return lax.ppermute(value, "cell", [(i, i ^ mask) for i in range(count)])


def halves(value):
    upper = value.astype(bf16)
    return upper, (value - upper.astype(f32)).astype(bf16)


def dot3(a, b, left, right):
    dims = (((left,), (right,)), ((), ()))
    dot = functools.partial(lax.dot_general, dimension_numbers=dims, preferred_element_type=f32)
    return dot(a[0], b[0]) + (dot(a[0], b[1]) + dot(a[1], b[0]))


VMEM = pl.BlockSpec(memory_space=pltpu.VMEM)
SMEM = pl.BlockSpec(memory_space=pltpu.SMEM)
HBM = pl.BlockSpec(memory_space=pltpu.HBM)
ANY = pl.BlockSpec(memory_space=pl.ANY)


def far(*arrays):
    return [pltpu.with_memory_space_constraint(a, pltpu.HBM) for a in arrays]


def near(*arrays):
    return [pltpu.with_memory_space_constraint(a, pltpu.VMEM) for a in arrays]


def array(shape, dtype=f32):
    return jax.ShapeDtypeStruct(shape, dtype)


def call(body, name, in_specs, out_specs, out_shape, scratch=(), cost=None):
    return pl.pallas_call(
        body,
        in_specs=in_specs,
        out_specs=out_specs,
        out_shape=out_shape,
        scratch_shapes=list(scratch),
        compiler_params=pltpu.CompilerParams(vmem_limit_bytes=LIMIT),
        cost_estimate=cost,
        name=name,
    )


def rows_of(step, block):
    return pl.ds(pl.multiple_of(step * block, block), block)


def fold(value):
    return jnp.sum(value.reshape(value.shape[0] // 8, 8, value.shape[1]), axis=0)


def add_to(sums, value):
    return value if sums is None else sums + value


def fetch_kernel(qs, qt, table, q_out, table_out, turned, totals, sems):
    pairs = ((qs, q_out.at[0]), (qt, q_out.at[1]), (table, table_out))
    copies = [pltpu.make_async_copy(a, b, sems.at[i]) for i, (a, b) in enumerate(pairs)]
    for copy in copies:
        copy.start()
    rank = qs.shape[1]
    for t in range(2):
        copies[t].wait()
        factor = q_out[t] / rank
        totals[t] = jnp.sum(factor, axis=0, keepdims=True)
        turned[t] = factor.T.astype(bf16)
    copies[2].wait()


def fetch(qs, qt, table):
    rows, rank = qs.shape
    return call(
        fetch_kernel, "fetch", [HBM] * 3, [VMEM] * 4,
        [
            pltpu.VMEM((2, rows, rank), f32), pltpu.VMEM(table.shape, table.dtype),
            pltpu.VMEM((2, rank, rows), bf16), array((2, 1, rank)),
        ],
        [pltpu.SemaphoreType.DMA((3,))],
        pl.CostEstimate(flops=0, bytes_accessed=8 * rows * rank, transcendentals=0),
    )(*far(qs, qt, table))


def stack_kernel(*refs):
    out = refs[-1]
    for i in range(out.shape[0]):
        out[i] = refs[i][...]


def stack_pieces(pieces, after):
    return call(
        stack_kernel, "stack", [VMEM] * len(pieces) + [ANY] * len(after), VMEM,
        array((len(pieces),) + pieces[0].shape, pieces[0].dtype),
    )(*pieces, *after)


def joined_table(me, j, even, odd):
    swapped = (me & 1) == 1
    a, b = even[j], odd[j]
    return jnp.concatenate([jnp.where(swapped, b, a), jnp.where(swapped, a, b)])


def first_kernel(masks, later_masks, place, xs, xt, even, odd, part, later, held, sems):
    me = place[0]
    width = 2 * even.shape[1]

    def copy(x, mask, out, sem):
        start = pl.multiple_of(((me ^ mask) >> 1) * width, width)
        made = pltpu.make_async_copy(x.at[:, pl.ds(start, width)], out, sem)
        made.start()
        return made

    blocks = len(masks)
    now = [
        [copy(x, m, held.at[t, j], sems.at[t, j]) for j, m in enumerate(masks)]
        for t, x in enumerate((xs, xt))
    ]
    after = [
        copy(x, m, later.at[t, j], sems.at[t, blocks + j])
        for j, m in enumerate(later_masks)
        for t, x in enumerate((xs, xt))
    ]
    for t in range(2):
        value = None
        for j in range(blocks):
            now[t][j].wait()
            term = jnp.dot(held[t, j], joined_table(me, j, even, odd), preferred_element_type=f32)
            value = term if value is None else value + term
        part[t] = value
    for made in after:
        made.wait()


def first_share(place, xs, xt, masks, later_masks, even, odd):
    rows, genes = xs.shape
    blocks, width, dim = even.shape
    return call(
        functools.partial(first_kernel, masks, later_masks), "embed_first",
        [SMEM, HBM, HBM, VMEM, VMEM], [VMEM] * 2,
        [array((2, rows, dim)), pltpu.VMEM((2, len(later_masks), rows, 2 * width), bf16)],
        [
            pltpu.VMEM((2, blocks, rows, 2 * width), bf16),
            pltpu.SemaphoreType.DMA((2, blocks + len(later_masks))),
        ],
        pl.CostEstimate(
            flops=2 * rows * genes * dim, bytes_accessed=4 * rows * genes, transcendentals=0
        ),
    )(place, *far(xs, xt), even, odd)


def gate_kernel(value, after, out):
    out[...] = value[...]


def gate(value, after):
    return call(
        gate_kernel, "gate", [VMEM, ANY], VMEM, array(value.shape, value.dtype)
    )(value, after)


def next_kernel(at, place, x, part, even, odd, out, *sums):
    me = place[0]
    tables = [joined_table(me, j, even, odd) for j in range(even.shape[0])]
    for t in range(2):
        value = part[t]
        for j, table in enumerate(tables):
            value = value + jnp.dot(x[t, at + j], table, preferred_element_type=f32)
        out[t] = value
        for ref in sums:
            ref[t] = fold(value)


def next_share(at, last, place, x, part, even, odd):
    _, rows, dim = part.shape
    sums = [array((2, 8, dim))] if last else []
    return call(
        functools.partial(next_kernel, at), "embed_next", [SMEM] + [VMEM] * 4, [VMEM] * (1 + len(sums)),
        [array(part.shape)] + sums,
        cost=pl.CostEstimate(
            flops=16 * rows * dim * even.shape[1], bytes_accessed=0, transcendentals=0
        ),
    )(place, x, part, even, odd)


def whole_kernel(masks, place, xs, xt, pieces, part, sums, table):
    genes = pieces.shape[1]
    for j, mask in enumerate(masks):
        start = pl.multiple_of((place[0] ^ mask) * genes, genes)
        table[pl.ds(start, genes), :] = pieces[j]
    for t, x in enumerate((xs, xt)):
        value = jnp.dot(x[...], table[...], preferred_element_type=f32)
        part[t] = value
        sums[t] = fold(value)


def whole_product(place, xs, xt, masks, pieces):
    rows, genes = xs.shape
    dim = pieces.shape[2]
    return call(
        functools.partial(whole_kernel, masks), "embed_whole", [SMEM] + [VMEM] * 3, [VMEM] * 2,
        [array((2, rows, dim)), array((2, 8, dim))], [pltpu.VMEM((genes, dim), bf16)],
    )(place, xs, xt, pieces)


def cross_kernel(flip, place, live, emb, sums, q, turned, totals, out, norms, *masks):
    t = (place[0] & 1) ^ flip
    _, rows, rank = q.shape
    block = rows // STEPS
    mean = (jnp.sum(sums[t], axis=0, keepdims=True) / rows).astype(bf16).astype(f32)
    norm_sum = rest = None
    for step in range(STEPS):
        at = slice(step * block, (step + 1) * block)
        value = emb[t, at, :]
        centred = (value - mean).astype(bf16)
        rest = add_to(rest, jnp.dot(turned[t, :, at], centred, preferred_element_type=f32))
        squares = jnp.sum(value * value, axis=1, keepdims=True)
        norms[at, :] = squares
        norm_sum = add_to(norm_sum, fold(squares * q[t, at, :]))
    norm_sum = jnp.sum(norm_sum, axis=0, keepdims=True) / rank
    lane = lax.broadcasted_iota(jnp.int32, (1, rank), 1)
    number = jnp.where(lane < rank // 2, live[0], live[1]).astype(f32)
    out[0:rank, :] = rest
    out[rank:, :] = jnp.concatenate([mean, totals[t], norm_sum, number, jnp.zeros((4, rank), f32)])
    for mask in masks:
        for i in range(2):
            mask[i] = (lax.broadcasted_iota(jnp.int32, (rows, 1), 0) < live[i]).astype(f32)


def cross(flip, place, live, emb, sums, q, turned, totals):
    _, rows, rank = q.shape
    dim = emb.shape[2]
    masks = [] if flip else [array((2, rows, 1))]
    return call(
        functools.partial(cross_kernel, flip), "cross", [SMEM] * 2 + [VMEM] * 5,
        [VMEM] * (2 + len(masks)), [array((rank + 8, dim)), array((rows, 1))] + masks,
        cost=pl.CostEstimate(flops=2 * rank * dim * q.shape[1], bytes_accessed=0, transcendentals=0),
    )(place, live, emb, sums, *near(q, turned), totals)


def split_row(row):
    high = row.astype(bf16).astype(f32)
    middle = (row - high).astype(bf16).astype(f32)
    return [high, middle, row - high - middle]


def tail_rows(cards):
    return -(-(8 + 4 * cards) // 16) * 16


def make_tail(norm, number, cards):
    width = norm.shape[1]
    rows = split_row(norm) + split_row(number) + [jnp.zeros((2, width), f32)] + cards
    used = sum(r.shape[0] for r in rows)
    filler = tail_rows((used - 8) // 4) - used
    if filler:
        rows.append(jnp.zeros((filler, width), f32))
    return jnp.concatenate(rows)


def three(tail, start):
    return (tail[start : start + 1] + tail[start + 1 : start + 2]) + tail[start + 2 : start + 3]


def pack_pair_kernel(own, recv, out):
    rank = own.shape[0] - 8
    out[0:rank, :] = (own[0:rank, :] + recv[0:rank, :]).astype(bf16)
    cards = []
    for ref in (own, recv):
        cards += [ref[rank : rank + 1, :]] + split_row(ref[rank + 1 : rank + 2, :])
    norm = own[rank + 2 : rank + 3, :] + recv[rank + 2 : rank + 3, :]
    number = own[rank + 3 : rank + 4, :] + recv[rank + 3 : rank + 4, :]
    out[rank:, :] = make_tail(norm, number, cards).astype(bf16)


def pack_pair(own, recv):
    rank, dim = own.shape[0] - 8, own.shape[1]
    return call(
        pack_pair_kernel, "pack_pair", [VMEM] * 2, VMEM, array((rank + tail_rows(2), dim), bf16)
    )(own, recv)


def ordered_cards(tails, cards, flags):
    lists = [tail[8 : 8 + 4 * cards] for tail in tails]
    for flag in flags:
        lists = [
            jnp.concatenate([jnp.where(flag, a, b), jnp.where(flag, b, a)])
            for a, b in zip(lists[::2], lists[1::2])
        ]
    return lists[0]


def tree(values):
    while len(values) > 1:
        values = [a + b for a, b in zip(values[::2], values[1::2])]
    return values[0]


def merge_kernel(rank, cards, bits, place, *refs):
    payloads, out = refs[:-1], refs[-1]
    out[0:rank, :] = tree([p[0:rank, :].astype(f32) for p in payloads]).astype(bf16)
    tails = [p[rank:, :].astype(f32) for p in payloads]
    listed = ordered_cards(tails, cards, [(place[0] & bit) == 0 for bit in bits])
    norm, number = (tree([three(tail, i) for tail in tails]) for i in (0, 3))
    out[rank:, :] = make_tail(norm, number, [listed]).astype(bf16)


def merge(rank, cards, bits, place, *payloads):
    return call(
        functools.partial(merge_kernel, rank, cards, bits), "merge",
        [SMEM] + [VMEM] * len(payloads), VMEM,
        array((rank + tail_rows(len(payloads) * cards), payloads[0].shape[1]), bf16),
    )(place, *payloads)


def total_kernel(rank, cards, *refs):
    payloads, out = refs[:-1], refs[-1]

    def unpack(ref):
        tail = ref[rank:, :].astype(f32)
        heights, means, sums = [], [], jnp.zeros((1, tail.shape[1]), f32)
        for c in range(cards):
            at = 8 + 4 * c
            heights.append(tail[at + 1 : at + 4])
            means += [tail[at : at + 1]] * 3
            sums = sums + three(tail, at + 1)
        left, right = jnp.concatenate(heights), jnp.concatenate(means)
        joined = lax.dot_general(
            left.T.astype(bf16), right.astype(bf16), (((1,), (0,)), ((), ())),
            preferred_element_type=f32,
        )
        return ref[0:rank, :].astype(f32) + joined, three(tail, 0), sums, three(tail, 3)

    joined = [tree(list(values)) for values in zip(*[unpack(ref) for ref in payloads])]
    out[0:rank, :] = joined[0]
    out[rank:, :] = jnp.concatenate(joined[1:] + [jnp.zeros((5, out.shape[1]), f32)])


def total(rank, cards, *payloads):
    dim = payloads[0].shape[1]
    return call(
        functools.partial(total_kernel, rank, cards), "total", [VMEM] * len(payloads), VMEM,
        array((rank + 8, dim)),
    )(*payloads)


def store_sums(sums, levels, copies):
    both = jnp.concatenate(
        [level * jnp.sum(part, axis=0, keepdims=True) for part, level in zip(sums, levels)]
    )
    for i in range(copies.shape[0]):
        copies[i] = both


def kernel_half(cells, t, mask, norms, emb, q, weights, summed, k, sums_out):
    _, rows, rank = q.shape
    block = rows // STEPS
    inverse = 1.0 / (D * (weights[...] * (cells / rank)))
    matrix = halves((-2.0 * inverse) * summed[0:rank, :].T)
    slope, offset = summed[rank + 1 : rank + 2, :] * inverse, summed[rank : rank + 1, :] * inverse
    sums = None
    for step in range(STEPS):
        at = slice(step * block, (step + 1) * block)
        value = emb[t, at, :]
        grad = norms[at, :] * slope + offset + dot3(halves(value), matrix, 1, 0)
        kernel = (q[t, at, :] / rank) * jnp.exp(-step_size * grad)
        k[at, :] = kernel
        scale = mask[t, at, :] / jnp.sum(kernel, axis=1, keepdims=True)
        sums = add_to(sums, fold(scale * kernel))
    sums_out[...] = sums


def other_kernel(cells, place, mask, norms, emb, q, weights, mine, k, sums):
    kernel_half(cells, 1 - (place[0] & 1), mask, norms, emb, q, weights, mine, k, sums)


def levels_of(cells, summed):
    rank = summed.shape[1]
    numbers = summed[rank + 2 : rank + 3, :]
    return cells / numbers[:, 0:1], cells / numbers[:, rank // 2 : rank // 2 + 1]


def in_order(first, own, out):
    return jnp.where(first, own, out), jnp.where(first, out, own)


def write_tables(cells, first, weights, mine, other, consts):
    rank = weights.shape[1]
    a, b = mine[...], other[...]
    col_mass = weights[...] * (cells / rank)
    norm_a, total_a = a[rank : rank + 1], a[rank + 1 : rank + 2]
    norm_b, total_b = b[rank : rank + 1], b[rank + 1 : rank + 2]
    products = jnp.sum((a[0:rank] * b[0:rank]).T, axis=0, keepdims=True)
    mixed = in_order(first, norm_a * total_b, total_a * norm_b)
    cost = (mixed[0] + mixed[1] - 2.0 * products) / D
    consts[0:1, :] = col_mass * jnp.exp(step_size * cost / (col_mass * col_mass))
    for t, level in enumerate(levels_of(cells, mine)):
        consts[1 + t : 2 + t, :] = jnp.broadcast_to(level, (1, rank))


def own_kernel(
    cells, place, mask, norms, emb, q, weights, mine, other, sums_other, k, copies, consts, sums
):
    core = place[0] & 1
    write_tables(cells, core == 0, weights, mine, other, consts)
    kernel_half(cells, core, mask, norms, emb, q, weights, other, k, sums)
    store_sums(in_order(core == 0, sums[...], sums_other[...]), levels_of(cells, mine), copies)


def cube_root(x):
    y = jnp.exp(jnp.log(x) * (1.0 / 3.0))
    refined = y - (y - x / (y * y)) * (1.0 / 3.0)
    return jnp.where((x > 0.0) & (x < jnp.inf), refined, y)


def duals_of(parts, consts):
    sums = jnp.sum(parts[...], axis=0)
    sum_s, sum_t = sums[0:1, :], sums[1:2, :]
    mass = cube_root(consts[0:1, :] * sum_s * sum_t)
    return mass, mass / sum_s, mass / sum_t


def sweep_kernel(last, place, mask, k_own, k_other, parts, consts, *refs):
    copies = refs[-1]
    core = place[0] & 1
    first = core == 0
    block = k_own.shape[0] // STEPS

    _, *duals = duals_of(parts, consts)
    sums = [None, None]
    for step in range(STEPS):
        at = slice(step * block, (step + 1) * block)
        for i, (k, t, dual) in enumerate(
            zip((k_own, k_other), (core, 1 - core), in_order(first, *duals))
        ):
            kernel = k[at, :]
            weighted = jnp.sum(kernel * dual, axis=1, keepdims=True)
            scaled = (mask[t, at, :] / weighted) * kernel
            if last:
                refs[0][t, at, :] = scaled
            sums[i] = add_to(sums[i], fold(scaled))
    store_sums(in_order(first, *sums), (consts[1:2, :], consts[2:3, :]), copies)


def finish_kernel(cells, scaled, parts, consts, fs, ft, weights, held, mass_held, sems, mass_sem):
    _, rows, rank = scaled.shape
    block = rows // STEPS
    mass, dual_s, dual_t = duals_of(parts, consts)
    mass_held[...] = mass * (rank / cells)
    copies = [pltpu.make_async_copy(mass_held, weights, mass_sem)]
    copies[0].start()
    dual_s, dual_t = dual_s * (rank * consts[1:2, :]), dual_t * (rank * consts[2:3, :])
    for step in range(STEPS):
        at = slice(step * block, (step + 1) * block)
        for t, (dual, out) in enumerate(((dual_s, fs), (dual_t, ft))):
            held[t, at, :] = scaled[t, at, :] * dual
            copy = pltpu.make_async_copy(held.at[t, at], out.at[at], sems.at[t, step])
            copy.start()
            copies.append(copy)
    for copy in copies:
        copy.wait()


def kernels(cells, count, place, mask, norms, emb, q, weights, mine, other):
    _, rows, rank = q.shape
    dim = emb.shape[2]
    cost = pl.CostEstimate(flops=6 * rows * rank * dim, bytes_accessed=0, transcendentals=rows * rank)
    k_other, sums_other = call(
        functools.partial(other_kernel, cells), "kernel_other", [SMEM] + [VMEM] * 6, [VMEM] * 2,
        [array((rows, rank)), array((8, rank))], cost=cost,
    )(place, mask, norms[1], emb, *near(q), weights, mine)
    k_own, copies, consts = call(
        functools.partial(own_kernel, cells), "kernel_own", [SMEM] + [VMEM] * 8, [VMEM] * 3,
        [array((rows, rank)), array((count, 2, rank)), array((8, rank))], [pltpu.VMEM((8, rank), f32)], cost,
    )(place, mask, norms[0], emb, *near(q), weights, mine, other, sums_other)
    return k_own, k_other, copies, consts


def sweep(count, last, place, mask, k_own, k_other, parts, consts):
    rows, rank = k_own.shape
    scaled = [array((2, rows, rank))] if last else []
    return call(
        functools.partial(sweep_kernel, last), "sweep", [SMEM] + [VMEM] * 5,
        [VMEM] * (len(scaled) + 1), scaled + [array((count, 2, rank))],
    )(place, mask, k_own, k_other, parts, consts)


def finish(cells, scaled, parts, consts):
    _, rows, rank = scaled.shape
    return call(
        functools.partial(finish_kernel, cells), "finish", [VMEM] * 3, [HBM] * 3,
        [array((rows, rank))] * 2 + [array((1, rank))],
        [
            pltpu.VMEM((2, rows, rank), f32), pltpu.VMEM((1, rank), f32),
            pltpu.SemaphoreType.DMA((2, STEPS)), pltpu.SemaphoreType.DMA,
        ],
    )(scaled, parts, consts)


def on_device(
    source_expr, target_expr, loadings, source_prev, target_prev, weights_prev, live_counts
):
    count = lax.axis_size("cell")
    place = lax.axis_index("cell").astype(jnp.int32)[None]
    live = live_counts[:, 0]
    rows, rank = source_prev.shape
    cells = rows * count
    bits = [1 << b for b in range(count.bit_length() - 1)]
    opposite = bits[-1] | bits[-2]
    exchange = functools.partial(lax.all_to_all, axis_name="cell", split_axis=0, concat_axis=0)

    q, own_table, turned, totals = fetch(source_prev, target_prev, loadings)
    stack = stack_pieces([own_table, swap(loadings, count, opposite)], [totals])
    masks = [0, opposite]
    if count == 16 and loadings.shape[0] % 64 == 0:
        quad = [2, 4, 6]
        arrived = [swap(stack, count, m) for m in quad]
        later = [m ^ q for q in quad for m in masks]
        emb, x = first_share(
            place, source_expr, target_expr, masks, later, stack, swap(stack, count, 1)
        )
        arrived = [gate(piece, emb) for piece in arrived]
        for i, piece in enumerate(arrived):
            last = i == len(arrived) - 1
            emb, *sums = next_share(2 * i, last, place, x, emb, piece, swap(piece, count, 1))
    else:
        for bit in reversed(bits[:-1]):
            stack = jnp.concatenate([stack, swap(stack, count, bit)])
            masks = masks + [m ^ bit for m in masks]
        emb, *sums = whole_product(place, source_expr, target_expr, masks, stack)
    send, norms_other = cross(1, place, live, emb, *sums, q, turned, totals)
    own, norms_own, mask = cross(0, place, live, emb, *sums, q, turned, totals)

    payload = pack_pair(own, swap(send, count, 1))
    cards = 2
    inner = bits[1:-1]
    while inner:
        used, inner = inner[:2], inner[2:]
        steps = [used[0], used[1], used[0] | used[1]] if len(used) == 2 else used
        others = [swap(payload, count, m) for m in steps]
        payload = merge(rank, cards, used, place, payload, *others)
        cards = cards * (1 + len(others))
    mine = total(rank, cards, payload, swap(payload, count, opposite))
    other = swap(mine, count, 1)

    k_own, k_other, copies, consts = kernels(
        cells, count, place, mask, (norms_own, norms_other), emb, q, weights_prev[None], mine, other
    )
    scaled = []
    for step_index in range(1, ITERS):
        last = step_index == ITERS - 1
        *scaled, copies = sweep(count, last, place, mask, k_own, k_other, exchange(copies), consts)
    out_s, out_t, weights = finish(cells, *scaled, exchange(copies), consts)
    return out_s, out_t, weights[0]


def solution(mesh):
    in_specs = (
        P(("grp", "cell"), None),
        P(("grp", "cell"), None),
        P("cell", None),
        P(("grp", "cell"), None),
        P(("grp", "cell"), None),
        P("grp"),
        P(None, ("grp", "cell")),
    )
    out_specs = (P(("grp", "cell"), None), P(("grp", "cell"), None), P("grp"))
    return jax.shard_map(
        on_device, mesh=mesh, in_specs=in_specs, out_specs=out_specs, check_vma=False
    )
```

```python
import functools

import jax
import jax.numpy as jnp
from jax import lax
from jax.experimental import pallas as pl
from jax.experimental.pallas import tpu as pltpu
from jax.sharding import PartitionSpec as P

D = 256
ITERS = 3
STEPS = 4

step_size = 1.0
LOG2_E = 1.4426950408889634
f32 = jnp.float32
bf16 = jnp.bfloat16
LIMIT = 16 * 1024 * 1024


def swap(value, count, mask):
    return lax.ppermute(value, "cell", [(i, i ^ mask) for i in range(count)])


def halves(value):
    upper = value.astype(bf16)
    return upper, (value - upper.astype(f32)).astype(bf16)


def stacked_left(value):
    upper, lower = halves(value)
    return jnp.concatenate([upper, upper, lower], axis=1)


def stacked_right(value):
    upper, lower = halves(value)
    return jnp.concatenate([upper, lower, upper])


VMEM = pl.BlockSpec(memory_space=pltpu.VMEM)
SMEM = pl.BlockSpec(memory_space=pltpu.SMEM)
HBM = pl.BlockSpec(memory_space=pltpu.HBM)
ANY = pl.BlockSpec(memory_space=pl.ANY)


def far(*arrays):
    return [pltpu.with_memory_space_constraint(a, pltpu.HBM) for a in arrays]


def near(*arrays):
    return [pltpu.with_memory_space_constraint(a, pltpu.VMEM) for a in arrays]


def array(shape, dtype=f32):
    return jax.ShapeDtypeStruct(shape, dtype)


def call(body, name, in_specs, out_specs, out_shape, scratch=(), cost=None):
    return pl.pallas_call(
        body,
        in_specs=in_specs,
        out_specs=out_specs,
        out_shape=out_shape,
        scratch_shapes=list(scratch),
        compiler_params=pltpu.CompilerParams(vmem_limit_bytes=LIMIT),
        cost_estimate=cost,
        name=name,
    )


def rows_of(step, block):
    return pl.ds(pl.multiple_of(step * block, block), block)


def fold(value):
    return jnp.sum(value.reshape(value.shape[0] // 8, 8, value.shape[1]), axis=0)


def add_to(sums, value):
    return value if sums is None else sums + value


def fetch_kernel(qs, qt, table, q_out, table_out, turned, totals, sems):
    pairs = ((qs, q_out.at[0]), (qt, q_out.at[1]), (table, table_out))
    copies = [pltpu.make_async_copy(a, b, sems.at[i]) for i, (a, b) in enumerate(pairs)]
    for copy in copies:
        copy.start()
    rank = qs.shape[1]
    for t in range(2):
        copies[t].wait()
        factor = q_out[t] * (1.0 / rank)
        totals[t] = jnp.sum(factor, axis=0, keepdims=True)
        turned[t] = factor.T.astype(bf16)
    copies[2].wait()


def fetch(qs, qt, table):
    rows, rank = qs.shape
    return call(
        fetch_kernel, "fetch", [HBM] * 3, [VMEM] * 4,
        [
            pltpu.VMEM((2, rows, rank), f32), pltpu.VMEM(table.shape, table.dtype),
            pltpu.VMEM((2, rank, rows), bf16), array((2, 1, rank)),
        ],
        [pltpu.SemaphoreType.DMA((3,))],
        pl.CostEstimate(flops=0, bytes_accessed=8 * rows * rank, transcendentals=0),
    )(*far(qs, qt, table))


def stack_kernel(*refs):
    out = refs[-1]
    for i in range(out.shape[0]):
        out[i] = refs[i][...]


def stack_pieces(pieces, after):
    return call(
        stack_kernel, "stack", [VMEM] * len(pieces) + [ANY] * len(after), VMEM,
        array((len(pieces),) + pieces[0].shape, pieces[0].dtype),
    )(*pieces, *after)


def joined_table(me, j, even, odd):
    swapped = (me & 1) == 1
    a, b = even[j], odd[j]
    return jnp.concatenate([jnp.where(swapped, b, a), jnp.where(swapped, a, b)])


def first_kernel(masks, later_masks, place, xs, xt, even, odd, part, later, held, sems):
    me = place[0]
    width = 2 * even.shape[1]

    def copy(x, mask, out, sem):
        start = pl.multiple_of(((me ^ mask) >> 1) * width, width)
        made = pltpu.make_async_copy(x.at[:, pl.ds(start, width)], out, sem)
        made.start()
        return made

    blocks = len(masks)
    now = [
        [copy(x, m, held.at[t, j], sems.at[t, j]) for j, m in enumerate(masks)]
        for t, x in enumerate((xs, xt))
    ]
    after = [
        copy(x, m, later.at[t, j], sems.at[t, blocks + j])
        for j, m in enumerate(later_masks)
        for t, x in enumerate((xs, xt))
    ]
    for t in range(2):
        value = None
        for j in range(blocks):
            now[t][j].wait()
            term = jnp.dot(held[t, j], joined_table(me, j, even, odd), preferred_element_type=f32)
            value = term if value is None else value + term
        part[t] = value
    for made in after:
        made.wait()


def first_share(place, xs, xt, masks, later_masks, even, odd):
    rows, genes = xs.shape
    blocks, width, dim = even.shape
    return call(
        functools.partial(first_kernel, masks, later_masks), "embed_first",
        [SMEM, HBM, HBM, VMEM, VMEM], [VMEM] * 2,
        [array((2, rows, dim)), pltpu.VMEM((2, len(later_masks), rows, 2 * width), bf16)],
        [
            pltpu.VMEM((2, blocks, rows, 2 * width), bf16),
            pltpu.SemaphoreType.DMA((2, blocks + len(later_masks))),
        ],
        pl.CostEstimate(
            flops=2 * rows * genes * dim, bytes_accessed=4 * rows * genes, transcendentals=0
        ),
    )(place, *far(xs, xt), even, odd)


def gate_kernel(value, after, out):
    out[...] = value[...]


def gate(value, after):
    return call(
        gate_kernel, "gate", [VMEM, ANY], VMEM, array(value.shape, value.dtype)
    )(value, after)


def added_products(me, x, t, at, even, odd, value):
    for j in range(even.shape[0]):
        table = joined_table(me, j, even, odd)
        value = value + jnp.dot(x[t, at + j], table, preferred_element_type=f32)
    return value


def next_kernel(at, place, x, part, even, odd, out):
    for t in range(2):
        out[t] = added_products(place[0], x, t, at, even, odd, part[t])


def next_share(at, place, x, part, even, odd):
    return call(
        functools.partial(next_kernel, at), "embed_next", [SMEM] + [VMEM] * 4, VMEM, array(part.shape),
        cost=pl.CostEstimate(
            flops=16 * part.shape[1] * part.shape[2] * even.shape[1], bytes_accessed=0, transcendentals=0
        ),
    )(place, x, part, even, odd)


def whole_kernel(masks, place, xs, xt, pieces, part, table):
    genes = pieces.shape[1]
    for j, mask in enumerate(masks):
        start = pl.multiple_of((place[0] ^ mask) * genes, genes)
        table[pl.ds(start, genes), :] = pieces[j]
    for t, x in enumerate((xs, xt)):
        part[t] = jnp.dot(x[...], table[...], preferred_element_type=f32)


def whole_product(place, xs, xt, masks, pieces):
    rows, genes = xs.shape
    dim = pieces.shape[2]
    return call(
        functools.partial(whole_kernel, masks), "embed_whole", [SMEM] + [VMEM] * 3, VMEM,
        array((2, rows, dim)), [pltpu.VMEM((genes, dim), bf16)],
    )(place, xs, xt, pieces)


def cross_kernel(flip, at, place, live, part, q, turned, totals, *refs):
    if at is not None:
        (x, even, odd), refs = refs[:3], refs[3:]
    emb, out, norms, *masks = refs
    t = (place[0] & 1) ^ flip
    _, rows, rank = q.shape
    block = rows // STEPS
    value = part[t]
    if at is not None:
        value = added_products(place[0], x, t, at, even, odd, value)
    emb[...] = value
    mean = (jnp.sum(fold(value), axis=0, keepdims=True) / rows).astype(bf16).astype(f32)
    norm_sum = rest = None
    for step in range(STEPS):
        span = slice(step * block, (step + 1) * block)
        value = emb[span, :]
        centred = (value - mean).astype(bf16)
        rest = add_to(rest, jnp.dot(turned[t, :, span], centred, preferred_element_type=f32))
        squares = jnp.sum(value * value, axis=1, keepdims=True)
        norms[span, :] = squares
        norm_sum = add_to(norm_sum, fold(squares * q[t, span, :]))
    norm_sum = jnp.sum(norm_sum, axis=0, keepdims=True) * (1.0 / rank)
    lane = lax.broadcasted_iota(jnp.int32, (1, rank), 1)
    number = jnp.where(lane < rank // 2, live[0], live[1]).astype(f32)
    out[0:rank, :] = rest
    out[rank:, :] = jnp.concatenate([mean, totals[t], norm_sum, number, jnp.zeros((4, rank), f32)])
    for mask in masks:
        for i in range(2):
            mask[i] = (lax.broadcasted_iota(jnp.int32, (rows, 1), 0) < live[i]).astype(f32)


def cross(flip, at, place, live, part, q, turned, totals, *rest):
    _, rows, rank = q.shape
    dim = part.shape[2]
    masks = [] if flip else [array((2, rows, 1))]
    return call(
        functools.partial(cross_kernel, flip, at), "cross", [SMEM] * 2 + [VMEM] * (4 + len(rest)),
        [VMEM] * (3 + len(masks)),
        [array((rows, dim)), array((rank + 8, dim)), array((rows, 1))] + masks,
        cost=pl.CostEstimate(flops=2 * rank * dim * q.shape[1], bytes_accessed=0, transcendentals=0),
    )(place, live, part, *near(q, turned), totals, *rest)


def split_row(row):
    high = row.astype(bf16).astype(f32)
    middle = (row - high).astype(bf16).astype(f32)
    return [high, middle, row - high - middle]


def tail_rows(cards):
    return -(-(8 + 4 * cards) // 16) * 16


def make_tail(norm, number, cards):
    width = norm.shape[1]
    rows = split_row(norm) + split_row(number) + [jnp.zeros((2, width), f32)] + cards
    used = sum(r.shape[0] for r in rows)
    filler = tail_rows((used - 8) // 4) - used
    if filler:
        rows.append(jnp.zeros((filler, width), f32))
    return jnp.concatenate(rows)


def three(tail, start):
    return (tail[start : start + 1] + tail[start + 1 : start + 2]) + tail[start + 2 : start + 3]


def pack_pair_kernel(own, recv, out):
    rank = own.shape[0] - 8
    out[0:rank, :] = (own[0:rank, :] + recv[0:rank, :]).astype(bf16)
    cards = []
    for ref in (own, recv):
        cards += [ref[rank : rank + 1, :]] + split_row(ref[rank + 1 : rank + 2, :])
    norm = own[rank + 2 : rank + 3, :] + recv[rank + 2 : rank + 3, :]
    number = own[rank + 3 : rank + 4, :] + recv[rank + 3 : rank + 4, :]
    out[rank:, :] = make_tail(norm, number, cards).astype(bf16)


def pack_pair(own, recv):
    rank, dim = own.shape[0] - 8, own.shape[1]
    return call(
        pack_pair_kernel, "pack_pair", [VMEM] * 2, VMEM, array((rank + tail_rows(2), dim), bf16)
    )(own, recv)


def ordered_cards(tails, cards, flags):
    lists = [tail[8 : 8 + 4 * cards] for tail in tails]
    for flag in flags:
        lists = [
            jnp.concatenate([jnp.where(flag, a, b), jnp.where(flag, b, a)])
            for a, b in zip(lists[::2], lists[1::2])
        ]
    return lists[0]


def tree(values):
    while len(values) > 1:
        values = [a + b for a, b in zip(values[::2], values[1::2])]
    return values[0]


def merge_kernel(rank, cards, bits, place, *refs):
    payloads, out = refs[:-1], refs[-1]
    out[0:rank, :] = tree([p[0:rank, :].astype(f32) for p in payloads]).astype(bf16)
    tails = [p[rank:, :].astype(f32) for p in payloads]
    listed = ordered_cards(tails, cards, [(place[0] & bit) == 0 for bit in bits])
    norm, number = (tree([three(tail, i) for tail in tails]) for i in (0, 3))
    out[rank:, :] = make_tail(norm, number, [listed]).astype(bf16)


def merge(rank, cards, bits, place, *payloads):
    return call(
        functools.partial(merge_kernel, rank, cards, bits), "merge",
        [SMEM] + [VMEM] * len(payloads), VMEM,
        array((rank + tail_rows(len(payloads) * cards), payloads[0].shape[1]), bf16),
    )(place, *payloads)


def total_kernel(rank, cards, *refs):
    payloads, out = refs[:-1], refs[-1]

    def unpack(ref):
        tail = ref[rank:, :].astype(f32)
        heights, means, sums = [], [], jnp.zeros((1, tail.shape[1]), f32)
        for c in range(cards):
            at = 8 + 4 * c
            heights.append(tail[at + 1 : at + 4])
            means += [tail[at : at + 1]] * 3
            sums = sums + three(tail, at + 1)
        left, right = jnp.concatenate(heights), jnp.concatenate(means)
        joined = lax.dot_general(
            left.T.astype(bf16), right.astype(bf16), (((1,), (0,)), ((), ())),
            preferred_element_type=f32,
        )
        return ref[0:rank, :].astype(f32) + joined, three(tail, 0), sums, three(tail, 3)

    joined = [tree(list(values)) for values in zip(*[unpack(ref) for ref in payloads])]
    out[0:rank, :] = joined[0]
    out[rank:, :] = jnp.concatenate(joined[1:] + [jnp.zeros((5, out.shape[1]), f32)])


def total(rank, cards, *payloads):
    dim = payloads[0].shape[1]
    return call(
        functools.partial(total_kernel, rank, cards), "total", [VMEM] * len(payloads), VMEM,
        array((rank + 8, dim)),
    )(*payloads)


def store_sums(sums, levels, copies):
    both = jnp.concatenate(
        [level * jnp.sum(part, axis=0, keepdims=True) for part, level in zip(sums, levels)]
    )
    for i in range(copies.shape[0]):
        copies[i] = both


def kernel_half(cells, t, mask, norms, emb, q, weights, summed, k, sums_out):
    _, rows, rank = q.shape
    block = rows // STEPS
    inverse = (-step_size * LOG2_E) / (D * (weights[...] * (cells / rank)))
    matrix = stacked_right((-2.0 * inverse) * summed[0:rank, :].T)
    slope, offset = summed[rank + 1 : rank + 2, :] * inverse, summed[rank : rank + 1, :] * inverse
    sums = None
    for step in range(STEPS):
        at = slice(step * block, (step + 1) * block)
        value = emb[at, :]
        grad = norms[at, :] * slope + offset + jnp.dot(
            stacked_left(value), matrix, preferred_element_type=f32
        )
        kernel = (q[t, at, :] * (1.0 / rank)) * jnp.exp2(grad)
        k[at, :] = kernel
        scale = mask[t, at, :] / jnp.sum(kernel, axis=1, keepdims=True)
        sums = add_to(sums, fold(scale * kernel))
    sums_out[...] = sums


def other_kernel(cells, place, mask, norms, emb, q, weights, mine, k, sums):
    kernel_half(cells, 1 - (place[0] & 1), mask, norms, emb, q, weights, mine, k, sums)


def levels_of(cells, summed):
    rank = summed.shape[1]
    numbers = summed[rank + 2 : rank + 3, :]
    return cells / numbers[:, 0:1], cells / numbers[:, rank // 2 : rank // 2 + 1]


def in_order(first, own, out):
    return jnp.where(first, own, out), jnp.where(first, out, own)


def write_tables(cells, first, weights, mine, other, consts):
    rank = weights.shape[1]
    a, b = mine[...], other[...]
    col_mass = weights[...] * (cells / rank)
    norm_a, total_a = a[rank : rank + 1], a[rank + 1 : rank + 2]
    norm_b, total_b = b[rank : rank + 1], b[rank + 1 : rank + 2]
    products = jnp.sum((a[0:rank] * b[0:rank]).T, axis=0, keepdims=True)
    mixed = in_order(first, norm_a * total_b, total_a * norm_b)
    cost = (mixed[0] + mixed[1] - 2.0 * products) / D
    consts[0:1, :] = col_mass * jnp.exp(step_size * cost / (col_mass * col_mass))
    for t, level in enumerate(levels_of(cells, mine)):
        consts[1 + t : 2 + t, :] = jnp.broadcast_to(level, (1, rank))


def own_kernel(
    cells, place, mask, norms, emb, q, weights, mine, other, sums_other, k, copies, consts, sums
):
    core = place[0] & 1
    write_tables(cells, core == 0, weights, mine, other, consts)
    kernel_half(cells, core, mask, norms, emb, q, weights, other, k, sums)
    store_sums(in_order(core == 0, sums[...], sums_other[...]), levels_of(cells, mine), copies)


def cube_root(x):
    y = jnp.exp(jnp.log(x) * (1.0 / 3.0))
    refined = y - (y - x / (y * y)) * (1.0 / 3.0)
    return jnp.where((x > 0.0) & (x < jnp.inf), refined, y)


def duals_of(parts, consts):
    sums = jnp.sum(parts[...], axis=0)
    sum_s, sum_t = sums[0:1, :], sums[1:2, :]
    mass = cube_root(consts[0:1, :] * sum_s * sum_t)
    return mass, mass / sum_s, mass / sum_t


def row_sums(value):
    folded = value[:, 0:128]
    for start in range(128, value.shape[1], 128):
        folded = folded + value[:, start : start + 128]
    parts = jnp.concatenate(halves(folded), axis=1)
    return jnp.dot(parts, jnp.ones((256, 128), bf16), preferred_element_type=f32)


def scale_rows(value, scale):
    return jnp.concatenate(
        [scale * value[:, i : i + 128] for i in range(0, value.shape[1], 128)], axis=1
    )


def sweep_kernel(last, place, mask, k_own, k_other, parts, consts, *refs):
    copies = refs[-1]
    core = place[0] & 1
    first = core == 0
    block = k_own.shape[0] // STEPS

    _, *duals = duals_of(parts, consts)
    sums = [None, None]
    for step in range(STEPS):
        at = slice(step * block, (step + 1) * block)
        for i, (k, t, dual) in enumerate(
            zip((k_own, k_other), (core, 1 - core), in_order(first, *duals))
        ):
            kernel = k[at, :]
            scaled = scale_rows(kernel, mask[t, at, :] / row_sums(kernel * dual))
            if last:
                refs[0][t, at, :] = scaled
            sums[i] = add_to(sums[i], fold(scaled))
    store_sums(in_order(first, *sums), (consts[1:2, :], consts[2:3, :]), copies)


def finish_kernel(cells, scaled, parts, consts, fs, ft, weights, held, mass_held, sems, mass_sem):
    _, rows, rank = scaled.shape
    block = rows // STEPS
    mass, dual_s, dual_t = duals_of(parts, consts)
    mass_held[...] = mass * (rank / cells)
    copies = [pltpu.make_async_copy(mass_held, weights, mass_sem)]
    copies[0].start()
    dual_s, dual_t = dual_s * (rank * consts[1:2, :]), dual_t * (rank * consts[2:3, :])
    for step in range(STEPS):
        at = slice(step * block, (step + 1) * block)
        for t, (dual, out) in enumerate(((dual_s, fs), (dual_t, ft))):
            held[t, at, :] = scaled[t, at, :] * dual
            copy = pltpu.make_async_copy(held.at[t, at], out.at[at], sems.at[t, step])
            copy.start()
            copies.append(copy)
    for copy in copies:
        copy.wait()


def kernels(cells, count, place, mask, norms, emb, q, weights, mine, other):
    _, rows, rank = q.shape
    dim = emb[0].shape[1]
    cost = pl.CostEstimate(flops=6 * rows * rank * dim, bytes_accessed=0, transcendentals=rows * rank)
    k_other, sums_other = call(
        functools.partial(other_kernel, cells), "kernel_other", [SMEM] + [VMEM] * 6, [VMEM] * 2,
        [array((rows, rank)), array((8, rank))], cost=cost,
    )(place, mask, norms[1], emb[1], *near(q), weights, mine)
    k_own, copies, consts = call(
        functools.partial(own_kernel, cells), "kernel_own", [SMEM] + [VMEM] * 8, [VMEM] * 3,
        [array((rows, rank)), array((count, 2, rank)), array((8, rank))], [pltpu.VMEM((8, rank), f32)], cost,
    )(place, mask, norms[0], emb[0], *near(q), weights, mine, other, sums_other)
    return k_own, k_other, copies, consts


def sweep(count, last, place, mask, k_own, k_other, parts, consts):
    rows, rank = k_own.shape
    scaled = [array((2, rows, rank))] if last else []
    return call(
        functools.partial(sweep_kernel, last), "sweep", [SMEM] + [VMEM] * 5,
        [VMEM] * (len(scaled) + 1), scaled + [array((count, 2, rank))],
    )(place, mask, k_own, k_other, parts, consts)


def finish(cells, scaled, parts, consts):
    _, rows, rank = scaled.shape
    return call(
        functools.partial(finish_kernel, cells), "finish", [VMEM] * 3, [HBM] * 3,
        [array((rows, rank))] * 2 + [array((1, rank))],
        [
            pltpu.VMEM((2, rows, rank), f32), pltpu.VMEM((1, rank), f32),
            pltpu.SemaphoreType.DMA((2, STEPS)), pltpu.SemaphoreType.DMA,
        ],
    )(scaled, parts, consts)


def on_device(
    source_expr, target_expr, loadings, source_prev, target_prev, weights_prev, live_counts
):
    count = lax.axis_size("cell")
    place = lax.axis_index("cell").astype(jnp.int32)[None]
    live = live_counts[:, 0]
    rows, rank = source_prev.shape
    cells = rows * count
    bits = [1 << b for b in range(count.bit_length() - 1)]
    opposite = bits[-1] | bits[-2]
    exchange = functools.partial(lax.all_to_all, axis_name="cell", split_axis=0, concat_axis=0)

    q, own_table, turned, totals = fetch(source_prev, target_prev, loadings)
    stack = stack_pieces([own_table, swap(loadings, count, opposite)], [totals])
    masks = [0, opposite]
    if count == 16 and loadings.shape[0] % 64 == 0:
        quad = [2, 4, 6]
        arrived = [swap(stack, count, m) for m in quad]
        later = [m ^ q for q in quad for m in masks]
        emb, x = first_share(
            place, source_expr, target_expr, masks, later, stack, swap(stack, count, 1)
        )
        arrived = [gate(piece, emb) for piece in arrived]
        for i, piece in enumerate(arrived[:-1]):
            emb = next_share(2 * i, place, x, emb, piece, swap(piece, count, 1))
        at, rest = 2 * len(arrived) - 2, (x, arrived[-1], swap(arrived[-1], count, 1))
    else:
        for bit in reversed(bits[:-1]):
            stack = jnp.concatenate([stack, swap(stack, count, bit)])
            masks = masks + [m ^ bit for m in masks]
        emb = whole_product(place, source_expr, target_expr, masks, stack)
        at, rest = None, ()
    emb_other, send, norms_other = cross(1, at, place, live, emb, q, turned, totals, *rest)
    emb_own, own, norms_own, mask = cross(0, at, place, live, emb, q, turned, totals, *rest)

    payload = pack_pair(own, swap(send, count, 1))
    cards = 2
    inner = bits[1:-1]
    while inner:
        used, inner = inner[:2], inner[2:]
        steps = [used[0], used[1], used[0] | used[1]] if len(used) == 2 else used
        others = [swap(payload, count, m) for m in steps]
        payload = merge(rank, cards, used, place, payload, *others)
        cards = cards * (1 + len(others))
    mine = total(rank, cards, payload, swap(payload, count, opposite))
    other = swap(mine, count, 1)

    k_own, k_other, copies, consts = kernels(
        cells, count, place, mask, (norms_own, norms_other), (emb_own, emb_other), q,
        weights_prev[None], mine, other,
    )
    scaled = []
    for step_index in range(1, ITERS):
        last = step_index == ITERS - 1
        *scaled, copies = sweep(count, last, place, mask, k_own, k_other, exchange(copies), consts)
    out_s, out_t, weights = finish(cells, *scaled, exchange(copies), consts)
    return out_s, out_t, weights[0]


def solution(mesh):
    in_specs = (
        P(("grp", "cell"), None),
        P(("grp", "cell"), None),
        P("cell", None),
        P(("grp", "cell"), None),
        P(("grp", "cell"), None),
        P("grp"),
        P(None, ("grp", "cell")),
    )
    out_specs = (P(("grp", "cell"), None), P(("grp", "cell"), None), P("grp"))
    return jax.shard_map(
        on_device, mesh=mesh, in_specs=in_specs, out_specs=out_specs, check_vma=False
    )
```

```python
import functools

import jax
import jax.numpy as jnp
from jax import lax
from jax.experimental import pallas as pl
from jax.experimental.pallas import tpu as pltpu
from jax.sharding import PartitionSpec as P

D = 256
ITERS = 3
STEPS = 4

step_size = 1.0
LOG2_E = 1.4426950408889634
f32 = jnp.float32
bf16 = jnp.bfloat16
LIMIT = 16 * 1024 * 1024


def swap(value, count, mask):
    return lax.ppermute(value, "cell", [(i, i ^ mask) for i in range(count)])


def halves(value):
    upper = value.astype(bf16)
    return upper, (value - upper.astype(f32)).astype(bf16)


def stacked_left(value):
    upper, lower = halves(value)
    return jnp.concatenate([upper, upper, lower], axis=1)


def stacked_right(value):
    upper, lower = halves(value)
    return jnp.concatenate([upper, lower, upper])


VMEM = pl.BlockSpec(memory_space=pltpu.VMEM)
SMEM = pl.BlockSpec(memory_space=pltpu.SMEM)
HBM = pl.BlockSpec(memory_space=pltpu.HBM)
ANY = pl.BlockSpec(memory_space=pl.ANY)


def far(*arrays):
    return [pltpu.with_memory_space_constraint(a, pltpu.HBM) for a in arrays]


def near(*arrays):
    return [pltpu.with_memory_space_constraint(a, pltpu.VMEM) for a in arrays]


def array(shape, dtype=f32):
    return jax.ShapeDtypeStruct(shape, dtype)


def call(body, name, in_specs, out_specs, out_shape, scratch=(), cost=None):
    return pl.pallas_call(
        body,
        in_specs=in_specs,
        out_specs=out_specs,
        out_shape=out_shape,
        scratch_shapes=list(scratch),
        compiler_params=pltpu.CompilerParams(vmem_limit_bytes=LIMIT),
        cost_estimate=cost,
        name=name,
    )


def rows_of(step, block):
    return pl.ds(pl.multiple_of(step * block, block), block)


def fold(value):
    return jnp.sum(value.reshape(value.shape[0] // 8, 8, value.shape[1]), axis=0)


def add_to(sums, value):
    return value if sums is None else sums + value


def fetch_kernel(qs, qt, table, q_out, table_out, turned, totals, sems):
    pairs = ((qs, q_out.at[0]), (qt, q_out.at[1]), (table, table_out))
    copies = [pltpu.make_async_copy(a, b, sems.at[i]) for i, (a, b) in enumerate(pairs)]
    for copy in copies:
        copy.start()
    rank = qs.shape[1]
    for t in range(2):
        copies[t].wait()
        factor = q_out[t] * (1.0 / rank)
        totals[t] = jnp.sum(factor, axis=0, keepdims=True)
        turned[t] = factor.T.astype(bf16)
    copies[2].wait()


def fetch(qs, qt, table):
    rows, rank = qs.shape
    return call(
        fetch_kernel, "fetch", [HBM] * 3, [VMEM] * 4,
        [
            pltpu.VMEM((2, rows, rank), f32), pltpu.VMEM(table.shape, table.dtype),
            pltpu.VMEM((2, rank, rows), bf16), array((2, 1, rank)),
        ],
        [pltpu.SemaphoreType.DMA((3,))],
        pl.CostEstimate(flops=0, bytes_accessed=8 * rows * rank, transcendentals=0),
    )(*far(qs, qt, table))


def stack_kernel(*refs):
    out = refs[-1]
    for i in range(out.shape[0]):
        out[i] = refs[i][...]


def stack_pieces(pieces, after):
    return call(
        stack_kernel, "stack", [VMEM] * len(pieces) + [ANY] * len(after), VMEM,
        array((len(pieces),) + pieces[0].shape, pieces[0].dtype),
    )(*pieces, *after)


def joined_table(me, j, even, odd):
    swapped = (me & 1) == 1
    a, b = even[j], odd[j]
    return jnp.concatenate([jnp.where(swapped, b, a), jnp.where(swapped, a, b)])


def first_kernel(masks, later_masks, place, xs, xt, even, odd, part, later, held, sems):
    me = place[0]
    width = 2 * even.shape[1]

    def copy(x, mask, out, sem):
        start = pl.multiple_of(((me ^ mask) >> 1) * width, width)
        made = pltpu.make_async_copy(x.at[:, pl.ds(start, width)], out, sem)
        made.start()
        return made

    blocks = len(masks)
    now = [
        [copy(x, m, held.at[t, j], sems.at[t, j]) for j, m in enumerate(masks)]
        for t, x in enumerate((xs, xt))
    ]
    after = [
        copy(x, m, later.at[t, j], sems.at[t, blocks + j])
        for j, m in enumerate(later_masks)
        for t, x in enumerate((xs, xt))
    ]
    for t in range(2):
        value = None
        for j in range(blocks):
            now[t][j].wait()
            term = jnp.dot(held[t, j], joined_table(me, j, even, odd), preferred_element_type=f32)
            value = term if value is None else value + term
        part[t] = value
    for made in after:
        made.wait()


def first_share(place, xs, xt, masks, later_masks, even, odd):
    rows, genes = xs.shape
    blocks, width, dim = even.shape
    return call(
        functools.partial(first_kernel, masks, later_masks), "embed_first",
        [SMEM, HBM, HBM, VMEM, VMEM], [VMEM] * 2,
        [array((2, rows, dim)), pltpu.VMEM((2, len(later_masks), rows, 2 * width), bf16)],
        [
            pltpu.VMEM((2, blocks, rows, 2 * width), bf16),
            pltpu.SemaphoreType.DMA((2, blocks + len(later_masks))),
        ],
        pl.CostEstimate(
            flops=2 * rows * genes * dim, bytes_accessed=4 * rows * genes, transcendentals=0
        ),
    )(place, *far(xs, xt), even, odd)


def gate_kernel(value, after, out):
    out[...] = value[...]


def gate(value, after):
    return call(
        gate_kernel, "gate", [VMEM, ANY], VMEM, array(value.shape, value.dtype)
    )(value, after)


def added_products(me, x, t, at, even, odd, value):
    for j in range(even.shape[0]):
        table = joined_table(me, j, even, odd)
        value = value + jnp.dot(x[t, at + j], table, preferred_element_type=f32)
    return value


def next_kernel(at, place, x, part, even, odd, out):
    for t in range(2):
        out[t] = added_products(place[0], x, t, at, even, odd, part[t])


def next_share(at, place, x, part, even, odd):
    return call(
        functools.partial(next_kernel, at), "embed_next", [SMEM] + [VMEM] * 4, VMEM, array(part.shape),
        cost=pl.CostEstimate(
            flops=16 * part.shape[1] * part.shape[2] * even.shape[1], bytes_accessed=0, transcendentals=0
        ),
    )(place, x, part, even, odd)


def whole_kernel(masks, place, xs, xt, pieces, part, table):
    genes = pieces.shape[1]
    for j, mask in enumerate(masks):
        start = pl.multiple_of((place[0] ^ mask) * genes, genes)
        table[pl.ds(start, genes), :] = pieces[j]
    for t, x in enumerate((xs, xt)):
        part[t] = jnp.dot(x[...], table[...], preferred_element_type=f32)


def whole_product(place, xs, xt, masks, pieces):
    rows, genes = xs.shape
    dim = pieces.shape[2]
    return call(
        functools.partial(whole_kernel, masks), "embed_whole", [SMEM] + [VMEM] * 3, VMEM,
        array((2, rows, dim)), [pltpu.VMEM((genes, dim), bf16)],
    )(place, xs, xt, pieces)


def cross_kernel(flip, at, place, live, part, q, turned, totals, *refs):
    if at is not None:
        (x, even, odd), refs = refs[:3], refs[3:]
    emb, out, norms, *masks = refs
    t = (place[0] & 1) ^ flip
    _, rows, rank = q.shape
    block = rows // STEPS
    value = part[t]
    if at is not None:
        value = added_products(place[0], x, t, at, even, odd, value)
    emb[...] = value
    mean = (jnp.sum(fold(value), axis=0, keepdims=True) / rows).astype(bf16).astype(f32)
    norm_sum = rest = None
    for step in range(STEPS):
        span = slice(step * block, (step + 1) * block)
        value = emb[span, :]
        centred = (value - mean).astype(bf16)
        rest = add_to(rest, jnp.dot(turned[t, :, span], centred, preferred_element_type=f32))
        squares = jnp.sum(value * value, axis=1, keepdims=True)
        norms[span, :] = squares
        norm_sum = add_to(norm_sum, fold(squares * q[t, span, :]))
    norm_sum = jnp.sum(norm_sum, axis=0, keepdims=True) * (1.0 / rank)
    lane = lax.broadcasted_iota(jnp.int32, (1, rank), 1)
    number = jnp.where(lane < rank // 2, live[0], live[1]).astype(f32)
    out[0:rank, :] = rest
    out[rank:, :] = jnp.concatenate([mean, totals[t], norm_sum, number, jnp.zeros((4, rank), f32)])
    for mask in masks:
        for i in range(2):
            mask[i] = (lax.broadcasted_iota(jnp.int32, (rows, 1), 0) < live[i]).astype(f32)


def cross(flip, at, place, live, part, q, turned, totals, *rest):
    _, rows, rank = q.shape
    dim = part.shape[2]
    masks = [] if flip else [array((2, rows, 1))]
    return call(
        functools.partial(cross_kernel, flip, at), "cross", [SMEM] * 2 + [VMEM] * (4 + len(rest)),
        [VMEM] * (3 + len(masks)),
        [array((rows, dim)), array((rank + 8, dim)), array((rows, 1))] + masks,
        cost=pl.CostEstimate(flops=2 * rank * dim * q.shape[1], bytes_accessed=0, transcendentals=0),
    )(place, live, part, *near(q, turned), totals, *rest)


def split_row(row):
    high = row.astype(bf16).astype(f32)
    middle = (row - high).astype(bf16).astype(f32)
    return [high, middle, row - high - middle]


def tail_rows(cards):
    return -(-(8 + 4 * cards) // 16) * 16


def make_tail(norm, number, cards):
    width = norm.shape[1]
    rows = split_row(norm) + split_row(number) + [jnp.zeros((2, width), f32)] + cards
    used = sum(r.shape[0] for r in rows)
    filler = tail_rows((used - 8) // 4) - used
    if filler:
        rows.append(jnp.zeros((filler, width), f32))
    return jnp.concatenate(rows)


def three(tail, start):
    return (tail[start : start + 1] + tail[start + 1 : start + 2]) + tail[start + 2 : start + 3]


def pack_pair_kernel(own, recv, out):
    rank = own.shape[0] - 8
    out[0:rank, :] = (own[0:rank, :] + recv[0:rank, :]).astype(bf16)
    cards = []
    for ref in (own, recv):
        cards += [ref[rank : rank + 1, :]] + split_row(ref[rank + 1 : rank + 2, :])
    norm = own[rank + 2 : rank + 3, :] + recv[rank + 2 : rank + 3, :]
    number = own[rank + 3 : rank + 4, :] + recv[rank + 3 : rank + 4, :]
    out[rank:, :] = make_tail(norm, number, cards).astype(bf16)


def pack_pair(own, recv):
    rank, dim = own.shape[0] - 8, own.shape[1]
    return call(
        pack_pair_kernel, "pack_pair", [VMEM] * 2, VMEM, array((rank + tail_rows(2), dim), bf16)
    )(own, recv)


def ordered_cards(tails, cards, flags):
    lists = [tail[8 : 8 + 4 * cards] for tail in tails]
    for flag in flags:
        lists = [
            jnp.concatenate([jnp.where(flag, a, b), jnp.where(flag, b, a)])
            for a, b in zip(lists[::2], lists[1::2])
        ]
    return lists[0]


def tree(values):
    while len(values) > 1:
        values = [a + b for a, b in zip(values[::2], values[1::2])]
    return values[0]


def merge_kernel(rank, cards, bits, place, *refs):
    payloads, out = refs[:-1], refs[-1]
    out[0:rank, :] = tree([p[0:rank, :].astype(f32) for p in payloads]).astype(bf16)
    tails = [p[rank:, :].astype(f32) for p in payloads]
    listed = ordered_cards(tails, cards, [(place[0] & bit) == 0 for bit in bits])
    norm, number = (tree([three(tail, i) for tail in tails]) for i in (0, 3))
    out[rank:, :] = make_tail(norm, number, [listed]).astype(bf16)


def merge(rank, cards, bits, place, *payloads):
    return call(
        functools.partial(merge_kernel, rank, cards, bits), "merge",
        [SMEM] + [VMEM] * len(payloads), VMEM,
        array((rank + tail_rows(len(payloads) * cards), payloads[0].shape[1]), bf16),
    )(place, *payloads)


def total_kernel(rank, cards, *refs):
    payloads, out = refs[:-1], refs[-1]

    def unpack(ref):
        tail = ref[rank:, :].astype(f32)
        heights, means, sums = [], [], jnp.zeros((1, tail.shape[1]), f32)
        for c in range(cards):
            at = 8 + 4 * c
            heights.append(tail[at + 1 : at + 4])
            means += [tail[at : at + 1]] * 3
            sums = sums + three(tail, at + 1)
        left, right = jnp.concatenate(heights), jnp.concatenate(means)
        joined = lax.dot_general(
            left.T.astype(bf16), right.astype(bf16), (((1,), (0,)), ((), ())),
            preferred_element_type=f32,
        )
        return ref[0:rank, :].astype(f32) + joined, three(tail, 0), sums, three(tail, 3)

    joined = [tree(list(values)) for values in zip(*[unpack(ref) for ref in payloads])]
    out[0:rank, :] = joined[0]
    out[rank:, :] = jnp.concatenate(joined[1:] + [jnp.zeros((5, out.shape[1]), f32)])


def total(rank, cards, *payloads):
    dim = payloads[0].shape[1]
    return call(
        functools.partial(total_kernel, rank, cards), "total", [VMEM] * len(payloads), VMEM,
        array((rank + 8, dim)),
    )(*payloads)


def store_sums(sums, levels, copies):
    both = jnp.concatenate(
        [level * jnp.sum(part, axis=0, keepdims=True) for part, level in zip(sums, levels)]
    )
    for i in range(copies.shape[0]):
        copies[i] = both


def kernel_half(cells, t, mask, norms, emb, q, weights, summed, k, sums_out):
    _, rows, rank = q.shape
    block = rows // STEPS
    inverse = (-step_size * LOG2_E) / (D * (weights[...] * (cells / rank)))
    matrix = stacked_right((-2.0 * inverse) * summed[0:rank, :].T)
    slope, offset = summed[rank + 1 : rank + 2, :] * inverse, summed[rank : rank + 1, :] * inverse
    sums = None
    for step in range(STEPS):
        at = slice(step * block, (step + 1) * block)
        value = emb[at, :]
        grad = norms[at, :] * slope + offset + jnp.dot(
            stacked_left(value), matrix, preferred_element_type=f32
        )
        kernel = (q[t, at, :] * (1.0 / rank)) * jnp.exp2(grad)
        k[at, :] = kernel
        scale = mask[t, at, :] / jnp.sum(kernel, axis=1, keepdims=True)
        sums = add_to(sums, fold(scale * kernel))
    sums_out[...] = sums


def other_kernel(cells, place, mask, norms, emb, q, weights, mine, k, sums):
    kernel_half(cells, 1 - (place[0] & 1), mask, norms, emb, q, weights, mine, k, sums)


def levels_of(cells, summed):
    rank = summed.shape[1]
    numbers = summed[rank + 2 : rank + 3, :]
    return cells / numbers[:, 0:1], cells / numbers[:, rank // 2 : rank // 2 + 1]


def in_order(first, own, out):
    return jnp.where(first, own, out), jnp.where(first, out, own)


def write_tables(cells, first, weights, mine, other, consts):
    rank = weights.shape[1]
    a, b = mine[...], other[...]
    col_mass = weights[...] * (cells / rank)
    norm_a, total_a = a[rank : rank + 1], a[rank + 1 : rank + 2]
    norm_b, total_b = b[rank : rank + 1], b[rank + 1 : rank + 2]
    products = jnp.sum((a[0:rank] * b[0:rank]).T, axis=0, keepdims=True)
    mixed = in_order(first, norm_a * total_b, total_a * norm_b)
    cost = (mixed[0] + mixed[1] - 2.0 * products) / D
    consts[0:1, :] = col_mass * jnp.exp(step_size * cost / (col_mass * col_mass))
    for t, level in enumerate(levels_of(cells, mine)):
        consts[1 + t : 2 + t, :] = jnp.broadcast_to(level, (1, rank))


def own_kernel(
    cells, place, mask, norms, emb, q, weights, mine, other, sums_other, k, copies, consts, sums
):
    core = place[0] & 1
    write_tables(cells, core == 0, weights, mine, other, consts)
    kernel_half(cells, core, mask, norms, emb, q, weights, other, k, sums)
    store_sums(in_order(core == 0, sums[...], sums_other[...]), levels_of(cells, mine), copies)


def cube_root(x):
    y = jnp.exp(jnp.log(x) * (1.0 / 3.0))
    refined = y - (y - x / (y * y)) * (1.0 / 3.0)
    return jnp.where((x > 0.0) & (x < jnp.inf), refined, y)


def duals_of(parts, consts):
    sums = jnp.sum(parts[...], axis=0)
    sum_s, sum_t = sums[0:1, :], sums[1:2, :]
    mass = cube_root(consts[0:1, :] * sum_s * sum_t)
    return mass, mass / sum_s, mass / sum_t


def row_sums(value):
    folded = value[:, 0:128]
    for start in range(128, value.shape[1], 128):
        folded = folded + value[:, start : start + 128]
    parts = jnp.concatenate(halves(folded), axis=1)
    return jnp.dot(parts, jnp.ones((256, 128), bf16), preferred_element_type=f32)


def scale_rows(value, scale):
    return jnp.concatenate(
        [scale * value[:, i : i + 128] for i in range(0, value.shape[1], 128)], axis=1
    )


def sweep_kernel(last, place, mask, k_own, k_other, parts, consts, *refs):
    copies = refs[-1]
    core = place[0] & 1
    first = core == 0
    block = k_own.shape[0] // STEPS

    _, *duals = duals_of(parts, consts)
    sums = [None, None]
    for step in range(STEPS):
        at = slice(step * block, (step + 1) * block)
        for i, (k, t, dual) in enumerate(
            zip((k_own, k_other), (core, 1 - core), in_order(first, *duals))
        ):
            kernel = k[at, :]
            scaled = scale_rows(kernel, mask[t, at, :] / row_sums(kernel * dual))
            if last:
                refs[0][t, at, :] = scaled
            sums[i] = add_to(sums[i], fold(scaled))
    store_sums(in_order(first, *sums), (consts[1:2, :], consts[2:3, :]), copies)


def finish_kernel(cells, scaled, parts, consts, fs, ft, weights, held, mass_held, sems, mass_sem):
    _, rows, rank = scaled.shape
    block = rows // STEPS
    mass, dual_s, dual_t = duals_of(parts, consts)
    mass_held[...] = mass * (rank / cells)
    copies = [pltpu.make_async_copy(mass_held, weights, mass_sem)]
    copies[0].start()
    dual_s, dual_t = dual_s * (rank * consts[1:2, :]), dual_t * (rank * consts[2:3, :])
    for step in range(STEPS):
        at = slice(step * block, (step + 1) * block)
        for t, (dual, out) in enumerate(((dual_s, fs), (dual_t, ft))):
            held[t, at, :] = scaled[t, at, :] * dual
            copy = pltpu.make_async_copy(held.at[t, at], out.at[at], sems.at[t, step])
            copy.start()
            copies.append(copy)
    for copy in copies:
        copy.wait()


def kernels(cells, count, place, mask, norms, emb, q, weights, mine, other):
    _, rows, rank = q.shape
    dim = emb[0].shape[1]
    cost = pl.CostEstimate(flops=6 * rows * rank * dim, bytes_accessed=0, transcendentals=rows * rank)
    k_other, sums_other = call(
        functools.partial(other_kernel, cells), "kernel_other", [SMEM] + [VMEM] * 6, [VMEM] * 2,
        [array((rows, rank)), array((8, rank))], cost=cost,
    )(place, mask, norms[1], emb[1], *near(q), weights, mine)
    k_own, copies, consts = call(
        functools.partial(own_kernel, cells), "kernel_own", [SMEM] + [VMEM] * 8, [VMEM] * 3,
        [array((rows, rank)), array((count, 2, rank)), array((8, rank))], [pltpu.VMEM((8, rank), f32)], cost,
    )(place, mask, norms[0], emb[0], *near(q), weights, mine, other, sums_other)
    return k_own, k_other, copies, consts


def sweep(count, last, place, mask, k_own, k_other, parts, consts):
    rows, rank = k_own.shape
    scaled = [array((2, rows, rank))] if last else []
    return call(
        functools.partial(sweep_kernel, last), "sweep", [SMEM] + [VMEM] * 5,
        [VMEM] * (len(scaled) + 1), scaled + [array((count, 2, rank))],
    )(place, mask, k_own, k_other, parts, consts)


def finish(cells, scaled, parts, consts):
    _, rows, rank = scaled.shape
    return call(
        functools.partial(finish_kernel, cells), "finish", [VMEM] * 3, [HBM] * 3,
        [array((rows, rank))] * 2 + [array((1, rank))],
        [
            pltpu.VMEM((2, rows, rank), f32), pltpu.VMEM((1, rank), f32),
            pltpu.SemaphoreType.DMA((2, STEPS)), pltpu.SemaphoreType.DMA,
        ],
    )(scaled, parts, consts)


def on_device(
    source_expr, target_expr, loadings, source_prev, target_prev, weights_prev, live_counts
):
    count = lax.axis_size("cell")
    place = lax.axis_index("cell").astype(jnp.int32)[None]
    live = live_counts[:, 0]
    rows, rank = source_prev.shape
    cells = rows * count
    bits = [1 << b for b in range(count.bit_length() - 1)]
    opposite = bits[-1] | bits[-2]
    exchange = functools.partial(lax.all_to_all, axis_name="cell", split_axis=0, concat_axis=0)

    q, own_table, turned, totals = fetch(source_prev, target_prev, loadings)
    stack = stack_pieces([own_table, swap(loadings, count, opposite)], [totals])
    masks = [0, opposite]
    if count == 16 and loadings.shape[0] % 64 == 0:
        quad = [6, 4, 2]
        arrived = [swap(stack, count, m) for m in quad]
        later = [m ^ q for q in quad for m in masks]
        emb, x = first_share(
            place, source_expr, target_expr, masks, later, stack, swap(stack, count, 1)
        )
        arrived = [gate(piece, emb) for piece in arrived]
        for i, piece in enumerate(arrived[:-1]):
            emb = next_share(2 * i, place, x, emb, piece, swap(piece, count, 1))
        at, rest = 2 * len(arrived) - 2, (x, arrived[-1], swap(arrived[-1], count, 1))
    else:
        for bit in reversed(bits[:-1]):
            stack = jnp.concatenate([stack, swap(stack, count, bit)])
            masks = masks + [m ^ bit for m in masks]
        emb = whole_product(place, source_expr, target_expr, masks, stack)
        at, rest = None, ()
    emb_other, send, norms_other = cross(1, at, place, live, emb, q, turned, totals, *rest)
    emb_own, own, norms_own, mask = cross(0, at, place, live, emb, q, turned, totals, *rest)

    payload = pack_pair(own, swap(send, count, 1))
    cards = 2
    inner = bits[1:-1]
    while inner:
        used, inner = inner[:2], inner[2:]
        steps = [used[0], used[1], used[0] | used[1]] if len(used) == 2 else used
        moved = {m: swap(payload, count, m) for m in steps[1:2] + steps[:1] + steps[2:]}
        others = [moved[m] for m in steps]
        payload = merge(rank, cards, used, place, payload, *others)
        cards = cards * (1 + len(others))
    mine = total(rank, cards, payload, swap(payload, count, opposite))
    other = swap(mine, count, 1)

    k_own, k_other, copies, consts = kernels(
        cells, count, place, mask, (norms_own, norms_other), (emb_own, emb_other), q,
        weights_prev[None], mine, other,
    )
    scaled = []
    for step_index in range(1, ITERS):
        last = step_index == ITERS - 1
        *scaled, copies = sweep(count, last, place, mask, k_own, k_other, exchange(copies), consts)
    out_s, out_t, weights = finish(cells, *scaled, exchange(copies), consts)
    return out_s, out_t, weights[0]


def solution(mesh):
    in_specs = (
        P(("grp", "cell"), None),
        P(("grp", "cell"), None),
        P("cell", None),
        P(("grp", "cell"), None),
        P(("grp", "cell"), None),
        P("grp"),
        P(None, ("grp", "cell")),
    )
    out_specs = (P(("grp", "cell"), None), P(("grp", "cell"), None), P("grp"))
    return jax.shard_map(
        on_device, mesh=mesh, in_specs=in_specs, out_specs=out_specs, check_vma=False
    )
```

```python
import functools

import jax
import jax.numpy as jnp
from jax import lax
from jax.experimental import pallas as pl
from jax.experimental.pallas import tpu as pltpu
from jax.sharding import PartitionSpec as P

D = 256
ITERS = 3
STEPS = 4

step_size = 1.0
LOG2_E = 1.4426950408889634
f32 = jnp.float32
bf16 = jnp.bfloat16
LIMIT = 16 * 1024 * 1024


def swap(value, count, mask):
    return lax.ppermute(value, "cell", [(i, i ^ mask) for i in range(count)])


def halves(value):
    upper = value.astype(bf16)
    return upper, (value - upper.astype(f32)).astype(bf16)


def stacked_left(value):
    upper, lower = halves(value)
    return jnp.concatenate([upper, upper, lower], axis=1)


def stacked_right(value):
    upper, lower = halves(value)
    return jnp.concatenate([upper, lower, upper])


VMEM = pl.BlockSpec(memory_space=pltpu.VMEM)
SMEM = pl.BlockSpec(memory_space=pltpu.SMEM)
HBM = pl.BlockSpec(memory_space=pltpu.HBM)
ANY = pl.BlockSpec(memory_space=pl.ANY)


def far(*arrays):
    return [pltpu.with_memory_space_constraint(a, pltpu.HBM) for a in arrays]


def near(*arrays):
    return [pltpu.with_memory_space_constraint(a, pltpu.VMEM) for a in arrays]


def array(shape, dtype=f32):
    return jax.ShapeDtypeStruct(shape, dtype)


def call(body, name, in_specs, out_specs, out_shape, scratch=(), cost=None):
    return pl.pallas_call(
        body,
        in_specs=in_specs,
        out_specs=out_specs,
        out_shape=out_shape,
        scratch_shapes=list(scratch),
        compiler_params=pltpu.CompilerParams(vmem_limit_bytes=LIMIT),
        cost_estimate=cost,
        name=name,
    )


def rows_of(step, block):
    return pl.ds(pl.multiple_of(step * block, block), block)


def fold(value):
    return jnp.sum(value.reshape(value.shape[0] // 8, 8, value.shape[1]), axis=0)


def add_to(sums, value):
    return value if sums is None else sums + value


def fetch_kernel(qs, qt, table, q_out, table_out, turned, totals, sems):
    pairs = ((qs, q_out.at[0]), (qt, q_out.at[1]), (table, table_out))
    copies = [pltpu.make_async_copy(a, b, sems.at[i]) for i, (a, b) in enumerate(pairs)]
    for copy in copies:
        copy.start()
    rank = qs.shape[1]
    for t in range(2):
        copies[t].wait()
        factor = q_out[t] * (1.0 / rank)
        totals[t] = jnp.sum(factor, axis=0, keepdims=True)
        turned[t] = factor.T.astype(bf16)
    copies[2].wait()


def fetch(qs, qt, table):
    rows, rank = qs.shape
    return call(
        fetch_kernel, "fetch", [HBM] * 3, [VMEM] * 4,
        [
            pltpu.VMEM((2, rows, rank), f32), pltpu.VMEM(table.shape, table.dtype),
            pltpu.VMEM((2, rank, rows), bf16), array((2, 1, rank)),
        ],
        [pltpu.SemaphoreType.DMA((3,))],
        pl.CostEstimate(flops=0, bytes_accessed=8 * rows * rank, transcendentals=0),
    )(*far(qs, qt, table))


def stack_kernel(*refs):
    out = refs[-1]
    for i in range(out.shape[0]):
        out[i] = refs[i][...]


def stack_pieces(pieces, after):
    return call(
        stack_kernel, "stack", [VMEM] * len(pieces) + [ANY] * len(after), VMEM,
        array((len(pieces),) + pieces[0].shape, pieces[0].dtype),
    )(*pieces, *after)


def joined_table(me, j, even, odd):
    swapped = (me & 1) == 1
    a, b = even[j], odd[j]
    return jnp.concatenate([jnp.where(swapped, b, a), jnp.where(swapped, a, b)])


def first_kernel(masks, later_masks, place, xs, xt, even, odd, part, later, held, sems):
    me = place[0]
    width = 2 * even.shape[1]

    def copy(x, mask, out, sem):
        start = pl.multiple_of(((me ^ mask) >> 1) * width, width)
        made = pltpu.make_async_copy(x.at[:, pl.ds(start, width)], out, sem)
        made.start()
        return made

    blocks = len(masks)
    now = [
        [copy(x, m, held.at[t, j], sems.at[t, j]) for j, m in enumerate(masks)]
        for t, x in enumerate((xs, xt))
    ]
    after = [
        copy(x, m, later.at[t, j], sems.at[t, blocks + j])
        for j, m in enumerate(later_masks)
        for t, x in enumerate((xs, xt))
    ]
    for t in range(2):
        value = None
        for j in range(blocks):
            now[t][j].wait()
            term = jnp.dot(held[t, j], joined_table(me, j, even, odd), preferred_element_type=f32)
            value = term if value is None else value + term
        part[t] = value
    for made in after:
        made.wait()


def first_share(place, xs, xt, masks, later_masks, even, odd):
    rows, genes = xs.shape
    blocks, width, dim = even.shape
    return call(
        functools.partial(first_kernel, masks, later_masks), "embed_first",
        [SMEM, HBM, HBM, VMEM, VMEM], [VMEM] * 2,
        [array((2, rows, dim)), pltpu.VMEM((2, len(later_masks), rows, 2 * width), bf16)],
        [
            pltpu.VMEM((2, blocks, rows, 2 * width), bf16),
            pltpu.SemaphoreType.DMA((2, blocks + len(later_masks))),
        ],
        pl.CostEstimate(
            flops=2 * rows * genes * dim, bytes_accessed=4 * rows * genes, transcendentals=0
        ),
    )(place, *far(xs, xt), even, odd)


def gate_kernel(value, after, out):
    out[...] = value[...]


def gate(value, after):
    return call(
        gate_kernel, "gate", [VMEM, ANY], VMEM, array(value.shape, value.dtype)
    )(value, after)


def added_products(me, x, t, at, even, odd, value):
    for j in range(even.shape[0]):
        table = joined_table(me, j, even, odd)
        value = value + jnp.dot(x[t, at + j], table, preferred_element_type=f32)
    return value


def next_kernel(at, place, x, part, even, odd, out):
    for t in range(2):
        out[t] = added_products(place[0], x, t, at, even, odd, part[t])


def next_share(at, place, x, part, even, odd):
    return call(
        functools.partial(next_kernel, at), "embed_next", [SMEM] + [VMEM] * 4, VMEM, array(part.shape),
        cost=pl.CostEstimate(
            flops=16 * part.shape[1] * part.shape[2] * even.shape[1], bytes_accessed=0, transcendentals=0
        ),
    )(place, x, part, even, odd)


def whole_kernel(masks, place, xs, xt, pieces, part, table):
    genes = pieces.shape[1]
    for j, mask in enumerate(masks):
        start = pl.multiple_of((place[0] ^ mask) * genes, genes)
        table[pl.ds(start, genes), :] = pieces[j]
    for t, x in enumerate((xs, xt)):
        part[t] = jnp.dot(x[...], table[...], preferred_element_type=f32)


def whole_product(place, xs, xt, masks, pieces):
    rows, genes = xs.shape
    dim = pieces.shape[2]
    return call(
        functools.partial(whole_kernel, masks), "embed_whole", [SMEM] + [VMEM] * 3, VMEM,
        array((2, rows, dim)), [pltpu.VMEM((genes, dim), bf16)],
    )(place, xs, xt, pieces)


def cross_kernel(flip, at, place, live, part, q, turned, totals, *refs):
    if at is not None:
        (x, even, odd), refs = refs[:3], refs[3:]
    emb, out, norms, *masks = refs
    t = (place[0] & 1) ^ flip
    _, rows, rank = q.shape
    block = rows // STEPS
    value = part[t]
    if at is not None:
        value = added_products(place[0], x, t, at, even, odd, value)
    emb[...] = value
    mean = (jnp.sum(fold(value), axis=0, keepdims=True) / rows).astype(bf16).astype(f32)
    norm_sum = rest = None
    for step in range(STEPS):
        span = slice(step * block, (step + 1) * block)
        value = emb[span, :]
        centred = (value - mean).astype(bf16)
        rest = add_to(rest, jnp.dot(turned[t, :, span], centred, preferred_element_type=f32))
        squares = jnp.sum(value * value, axis=1, keepdims=True)
        norms[span, :] = squares
        norm_sum = add_to(norm_sum, fold(squares * q[t, span, :]))
    norm_sum = jnp.sum(norm_sum, axis=0, keepdims=True) * (1.0 / rank)
    lane = lax.broadcasted_iota(jnp.int32, (1, rank), 1)
    number = jnp.where(lane < rank // 2, live[0], live[1]).astype(f32)
    out[0:rank, :] = rest
    out[rank:, :] = jnp.concatenate([mean, totals[t], norm_sum, number, jnp.zeros((4, rank), f32)])
    for mask in masks:
        for i in range(2):
            mask[i] = (lax.broadcasted_iota(jnp.int32, (rows, 1), 0) < live[i]).astype(f32)


def cross(flip, at, place, live, part, q, turned, totals, *rest):
    _, rows, rank = q.shape
    dim = part.shape[2]
    masks = [] if flip else [array((2, rows, 1))]
    return call(
        functools.partial(cross_kernel, flip, at), "cross", [SMEM] * 2 + [VMEM] * (4 + len(rest)),
        [VMEM] * (3 + len(masks)),
        [array((rows, dim)), array((rank + 8, dim)), array((rows, 1))] + masks,
        cost=pl.CostEstimate(flops=2 * rank * dim * q.shape[1], bytes_accessed=0, transcendentals=0),
    )(place, live, part, *near(q, turned), totals, *rest)


def split_row(row):
    high = row.astype(bf16).astype(f32)
    middle = (row - high).astype(bf16).astype(f32)
    return [high, middle, row - high - middle]


def tail_rows(cards):
    return -(-(8 + 4 * cards) // 16) * 16


def make_tail(norm, number, cards):
    width = norm.shape[1]
    rows = split_row(norm) + split_row(number) + [jnp.zeros((2, width), f32)] + cards
    used = sum(r.shape[0] for r in rows)
    filler = tail_rows((used - 8) // 4) - used
    if filler:
        rows.append(jnp.zeros((filler, width), f32))
    return jnp.concatenate(rows)


def three(tail, start):
    return (tail[start : start + 1] + tail[start + 1 : start + 2]) + tail[start + 2 : start + 3]


def pack_pair_kernel(own, recv, out):
    rank = own.shape[0] - 8
    out[0:rank, :] = (own[0:rank, :] + recv[0:rank, :]).astype(bf16)
    cards = []
    for ref in (own, recv):
        cards += [ref[rank : rank + 1, :]] + split_row(ref[rank + 1 : rank + 2, :])
    norm = own[rank + 2 : rank + 3, :] + recv[rank + 2 : rank + 3, :]
    number = own[rank + 3 : rank + 4, :] + recv[rank + 3 : rank + 4, :]
    out[rank:, :] = make_tail(norm, number, cards).astype(bf16)


def pack_pair(own, recv):
    rank, dim = own.shape[0] - 8, own.shape[1]
    return call(
        pack_pair_kernel, "pack_pair", [VMEM] * 2, VMEM, array((rank + tail_rows(2), dim), bf16)
    )(own, recv)


def ordered_cards(tails, cards, flags):
    lists = [tail[8 : 8 + 4 * cards] for tail in tails]
    for flag in flags:
        lists = [
            jnp.concatenate([jnp.where(flag, a, b), jnp.where(flag, b, a)])
            for a, b in zip(lists[::2], lists[1::2])
        ]
    return lists[0]


def tree(values):
    while len(values) > 1:
        values = [a + b for a, b in zip(values[::2], values[1::2])]
    return values[0]


def merge_kernel(rank, cards, bits, place, *refs):
    payloads, out = refs[:-1], refs[-1]
    out[0:rank, :] = tree([p[0:rank, :].astype(f32) for p in payloads]).astype(bf16)
    tails = [p[rank:, :].astype(f32) for p in payloads]
    listed = ordered_cards(tails, cards, [(place[0] & bit) == 0 for bit in bits])
    norm, number = (tree([three(tail, i) for tail in tails]) for i in (0, 3))
    out[rank:, :] = make_tail(norm, number, [listed]).astype(bf16)


def merge(rank, cards, bits, place, *payloads):
    return call(
        functools.partial(merge_kernel, rank, cards, bits), "merge",
        [SMEM] + [VMEM] * len(payloads), VMEM,
        array((rank + tail_rows(len(payloads) * cards), payloads[0].shape[1]), bf16),
    )(place, *payloads)


def total_of(rank, cards, *payloads):
    def unpack(ref):
        tail = ref[rank:, :].astype(f32)
        heights, means, sums = [], [], jnp.zeros((1, tail.shape[1]), f32)
        for c in range(cards):
            at = 8 + 4 * c
            heights.append(tail[at + 1 : at + 4])
            means += [tail[at : at + 1]] * 3
            sums = sums + three(tail, at + 1)
        left, right = jnp.concatenate(heights), jnp.concatenate(means)
        joined = lax.dot_general(
            left.T.astype(bf16), right.astype(bf16), (((1,), (0,)), ((), ())),
            preferred_element_type=f32,
        )
        return ref[0:rank, :].astype(f32) + joined, three(tail, 0), sums, three(tail, 3)

    return [tree(list(values)) for values in zip(*[unpack(ref) for ref in payloads])]


def store_total(parts, out):
    rank = parts[0].shape[0]
    out[0:rank, :] = parts[0]
    out[rank:, :] = jnp.concatenate(parts[1:] + [jnp.zeros((5, out.shape[1]), f32)])


def store_sums(sums, levels, copies):
    both = jnp.concatenate(
        [level * jnp.sum(part, axis=0, keepdims=True) for part, level in zip(sums, levels)]
    )
    for i in range(copies.shape[0]):
        copies[i] = both


def kernel_half(cells, t, mask, norms, emb, q, weights, parts, k, sums_out):
    _, rows, rank = q.shape
    block = rows // STEPS
    inverse = (-step_size * LOG2_E) / (D * (weights[...] * (cells / rank)))
    product, norm, total, _ = parts
    matrix = stacked_right((-2.0 * inverse) * product.T)
    slope, offset = total * inverse, norm * inverse
    sums = None
    for step in range(STEPS):
        at = slice(step * block, (step + 1) * block)
        value = emb[at, :]
        grad = norms[at, :] * slope + offset + jnp.dot(
            stacked_left(value), matrix, preferred_element_type=f32
        )
        kernel = (q[t, at, :] * (1.0 / rank)) * jnp.exp2(grad)
        k[at, :] = kernel
        scale = mask[t, at, :] / jnp.sum(kernel, axis=1, keepdims=True)
        sums = add_to(sums, fold(scale * kernel))
    sums_out[...] = sums


def other_kernel(cells, cards, place, mask, norms, emb, q, weights, near_part, far_part, k, sums, mine):
    parts = total_of(q.shape[2], cards, near_part, far_part)
    store_total(parts, mine)
    kernel_half(cells, 1 - (place[0] & 1), mask, norms, emb, q, weights, parts, k, sums)


def levels_of(cells, summed):
    rank = summed.shape[1]
    numbers = summed[rank + 2 : rank + 3, :]
    return cells / numbers[:, 0:1], cells / numbers[:, rank // 2 : rank // 2 + 1]


def in_order(first, own, out):
    return jnp.where(first, own, out), jnp.where(first, out, own)


def write_tables(cells, first, weights, mine, other, consts):
    rank = weights.shape[1]
    a = mine[...]
    product_b, norm_b, total_b, _ = other
    col_mass = weights[...] * (cells / rank)
    norm_a, total_a = a[rank : rank + 1], a[rank + 1 : rank + 2]
    products = jnp.sum((a[0:rank] * product_b).T, axis=0, keepdims=True)
    mixed = in_order(first, norm_a * total_b, total_a * norm_b)
    cost = (mixed[0] + mixed[1] - 2.0 * products) / D
    consts[0:1, :] = col_mass * jnp.exp(step_size * cost / (col_mass * col_mass))
    for t, level in enumerate(levels_of(cells, mine)):
        consts[1 + t : 2 + t, :] = jnp.broadcast_to(level, (1, rank))


def own_kernel(
    cells, cards, place, mask, norms, emb, q, weights, mine, near_part, far_part, sums_other,
    k, copies, consts, sums,
):
    core = place[0] & 1
    parts = total_of(q.shape[2], cards, near_part, far_part)
    write_tables(cells, core == 0, weights, mine, parts, consts)
    kernel_half(cells, core, mask, norms, emb, q, weights, parts, k, sums)
    store_sums(in_order(core == 0, sums[...], sums_other[...]), levels_of(cells, mine), copies)


def cube_root(x):
    y = jnp.exp(jnp.log(x) * (1.0 / 3.0))
    refined = y - (y - x / (y * y)) * (1.0 / 3.0)
    return jnp.where((x > 0.0) & (x < jnp.inf), refined, y)


def duals_of(parts, consts):
    sums = jnp.sum(parts[...], axis=0)
    sum_s, sum_t = sums[0:1, :], sums[1:2, :]
    mass = cube_root(consts[0:1, :] * sum_s * sum_t)
    return mass, mass / sum_s, mass / sum_t


def row_sums(value):
    folded = value[:, 0:128]
    for start in range(128, value.shape[1], 128):
        folded = folded + value[:, start : start + 128]
    parts = jnp.concatenate(halves(folded), axis=1)
    return jnp.dot(parts, jnp.ones((256, 128), bf16), preferred_element_type=f32)


def scale_rows(value, scale):
    return jnp.concatenate(
        [scale * value[:, i : i + 128] for i in range(0, value.shape[1], 128)], axis=1
    )


def sweep_kernel(last, place, mask, k_own, k_other, parts, consts, *refs):
    copies = refs[-1]
    core = place[0] & 1
    first = core == 0
    block = k_own.shape[0] // STEPS

    _, *duals = duals_of(parts, consts)
    sums = [None, None]
    for step in range(STEPS):
        at = slice(step * block, (step + 1) * block)
        for i, (k, t, dual) in enumerate(
            zip((k_own, k_other), (core, 1 - core), in_order(first, *duals))
        ):
            kernel = k[at, :]
            scaled = scale_rows(kernel, mask[t, at, :] / row_sums(kernel * dual))
            if last:
                refs[0][t, at, :] = scaled
            sums[i] = add_to(sums[i], fold(scaled))
    store_sums(in_order(first, *sums), (consts[1:2, :], consts[2:3, :]), copies)


def finish_kernel(cells, scaled, parts, consts, fs, ft, weights, held, mass_held, sems, mass_sem):
    _, rows, rank = scaled.shape
    block = rows // STEPS
    mass, dual_s, dual_t = duals_of(parts, consts)
    mass_held[...] = mass * (rank / cells)
    copies = [pltpu.make_async_copy(mass_held, weights, mass_sem)]
    copies[0].start()
    dual_s, dual_t = dual_s * (rank * consts[1:2, :]), dual_t * (rank * consts[2:3, :])
    for step in range(STEPS):
        at = slice(step * block, (step + 1) * block)
        for t, (dual, out) in enumerate(((dual_s, fs), (dual_t, ft))):
            held[t, at, :] = scaled[t, at, :] * dual
            copy = pltpu.make_async_copy(held.at[t, at], out.at[at], sems.at[t, step])
            copy.start()
            copies.append(copy)
    for copy in copies:
        copy.wait()


def kernels(cells, cards, count, place, mask, norms, emb, q, weights, mine, other):
    _, rows, rank = q.shape
    dim = emb[0].shape[1]
    cost = pl.CostEstimate(flops=6 * rows * rank * dim, bytes_accessed=0, transcendentals=rows * rank)
    k_other, sums_other, total = call(
        functools.partial(other_kernel, cells, cards), "kernel_other", [SMEM] + [VMEM] * 7, [VMEM] * 3,
        [array((rows, rank)), array((8, rank)), array((rank + 8, dim))], cost=cost,
    )(place, mask, norms[1], emb[1], *near(q), weights, *mine)
    k_own, copies, consts = call(
        functools.partial(own_kernel, cells, cards), "kernel_own", [SMEM] + [VMEM] * 9, [VMEM] * 3,
        [array((rows, rank)), array((count, 2, rank)), array((8, rank))], [pltpu.VMEM((8, rank), f32)], cost,
    )(place, mask, norms[0], emb[0], *near(q), weights, total, *other, sums_other)
    return k_own, k_other, copies, consts


def sweep(count, last, place, mask, k_own, k_other, parts, consts):
    rows, rank = k_own.shape
    scaled = [array((2, rows, rank))] if last else []
    return call(
        functools.partial(sweep_kernel, last), "sweep", [SMEM] + [VMEM] * 5,
        [VMEM] * (len(scaled) + 1), scaled + [array((count, 2, rank))],
    )(place, mask, k_own, k_other, parts, consts)


def finish(cells, scaled, parts, consts):
    _, rows, rank = scaled.shape
    return call(
        functools.partial(finish_kernel, cells), "finish", [VMEM] * 3, [HBM] * 3,
        [array((rows, rank))] * 2 + [array((1, rank))],
        [
            pltpu.VMEM((2, rows, rank), f32), pltpu.VMEM((1, rank), f32),
            pltpu.SemaphoreType.DMA((2, STEPS)), pltpu.SemaphoreType.DMA,
        ],
    )(scaled, parts, consts)


def on_device(
    source_expr, target_expr, loadings, source_prev, target_prev, weights_prev, live_counts
):
    count = lax.axis_size("cell")
    place = lax.axis_index("cell").astype(jnp.int32)[None]
    live = live_counts[:, 0]
    rows, rank = source_prev.shape
    cells = rows * count
    bits = [1 << b for b in range(count.bit_length() - 1)]
    opposite = bits[-1] | bits[-2]
    exchange = functools.partial(lax.all_to_all, axis_name="cell", split_axis=0, concat_axis=0)

    q, own_table, turned, totals = fetch(source_prev, target_prev, loadings)
    stack = stack_pieces([own_table, swap(loadings, count, opposite)], [totals])
    masks = [0, opposite]
    if count == 16 and loadings.shape[0] % 64 == 0:
        quad = [6, 4, 2]
        arrived = [swap(stack, count, m) for m in quad]
        later = [m ^ q for q in quad for m in masks]
        emb, x = first_share(
            place, source_expr, target_expr, masks, later, stack, swap(stack, count, 1)
        )
        arrived = [gate(piece, emb) for piece in arrived]
        for i, piece in enumerate(arrived[:-1]):
            emb = next_share(2 * i, place, x, emb, piece, swap(piece, count, 1))
        at, rest = 2 * len(arrived) - 2, (x, arrived[-1], swap(arrived[-1], count, 1))
    else:
        for bit in reversed(bits[:-1]):
            stack = jnp.concatenate([stack, swap(stack, count, bit)])
            masks = masks + [m ^ bit for m in masks]
        emb = whole_product(place, source_expr, target_expr, masks, stack)
        at, rest = None, ()
    emb_other, send, norms_other = cross(1, at, place, live, emb, q, turned, totals, *rest)
    emb_own, own, norms_own, mask = cross(0, at, place, live, emb, q, turned, totals, *rest)

    payload = pack_pair(own, swap(send, count, 1))
    cards = 2
    inner = bits[1:-1]
    while inner:
        used, inner = inner[:2], inner[2:]
        steps = [used[0], used[1], used[0] | used[1]] if len(used) == 2 else used
        moved = {m: swap(payload, count, m) for m in steps[1:2] + steps[:1] + steps[2:]}
        others = [moved[m] for m in steps]
        payload = merge(rank, cards, used, place, payload, *others)
        cards = cards * (1 + len(others))
    mine = [payload, swap(payload, count, opposite)]
    other = [swap(part, count, 1) for part in mine]

    k_own, k_other, copies, consts = kernels(
        cells, cards, count, place, mask, (norms_own, norms_other), (emb_own, emb_other), q,
        weights_prev[None], mine, other,
    )
    scaled = []
    for step_index in range(1, ITERS):
        last = step_index == ITERS - 1
        *scaled, copies = sweep(count, last, place, mask, k_own, k_other, exchange(copies), consts)
    out_s, out_t, weights = finish(cells, *scaled, exchange(copies), consts)
    return out_s, out_t, weights[0]


def solution(mesh):
    in_specs = (
        P(("grp", "cell"), None),
        P(("grp", "cell"), None),
        P("cell", None),
        P(("grp", "cell"), None),
        P(("grp", "cell"), None),
        P("grp"),
        P(None, ("grp", "cell")),
    )
    out_specs = (P(("grp", "cell"), None), P(("grp", "cell"), None), P("grp"))
    return jax.shard_map(
        on_device, mesh=mesh, in_specs=in_specs, out_specs=out_specs, check_vma=False
    )
```

```python
import functools

import jax
import jax.numpy as jnp
from jax import lax
from jax.experimental import pallas as pl
from jax.experimental.pallas import tpu as pltpu
from jax.sharding import PartitionSpec as P

D = 256
ITERS = 3
STEPS = 4

step_size = 1.0
LOG2_E = 1.4426950408889634
f32 = jnp.float32
bf16 = jnp.bfloat16
LIMIT = 16 * 1024 * 1024


def swap(value, count, mask):
    return lax.ppermute(value, "cell", [(i, i ^ mask) for i in range(count)])


def halves(value):
    upper = value.astype(bf16)
    return upper, (value - upper.astype(f32)).astype(bf16)


def stacked_left(value):
    upper, lower = halves(value)
    return jnp.concatenate([upper, upper, lower], axis=1)


def stacked_right(value):
    upper, lower = halves(value)
    return jnp.concatenate([upper, lower, upper])


VMEM = pl.BlockSpec(memory_space=pltpu.VMEM)
SMEM = pl.BlockSpec(memory_space=pltpu.SMEM)
HBM = pl.BlockSpec(memory_space=pltpu.HBM)
ANY = pl.BlockSpec(memory_space=pl.ANY)


def far(*arrays):
    return [pltpu.with_memory_space_constraint(a, pltpu.HBM) for a in arrays]


def near(*arrays):
    return [pltpu.with_memory_space_constraint(a, pltpu.VMEM) for a in arrays]


def array(shape, dtype=f32):
    return jax.ShapeDtypeStruct(shape, dtype)


def call(body, name, in_specs, out_specs, out_shape, scratch=(), cost=None):
    return pl.pallas_call(
        body,
        in_specs=in_specs,
        out_specs=out_specs,
        out_shape=out_shape,
        scratch_shapes=list(scratch),
        compiler_params=pltpu.CompilerParams(vmem_limit_bytes=LIMIT),
        cost_estimate=cost,
        name=name,
    )


def rows_of(step, block):
    return pl.ds(pl.multiple_of(step * block, block), block)


def fold(value):
    return jnp.sum(value.reshape(value.shape[0] // 8, 8, value.shape[1]), axis=0)


def add_to(sums, value):
    return value if sums is None else sums + value


def fetch_kernel(qs, qt, table, live, q_out, table_out, turned, totals, live_held, sems):
    pairs = ((qs, q_out.at[0]), (qt, q_out.at[1]), (table, table_out), (live, live_held))
    copies = [pltpu.make_async_copy(a, b, sems.at[i]) for i, (a, b) in enumerate(pairs)]
    for copy in copies:
        copy.start()
    rank = qs.shape[1]
    for t in range(2):
        copies[t].wait()
        factor = q_out[t] * (1.0 / rank)
        totals[t] = jnp.sum(factor, axis=0, keepdims=True)
        turned[t] = factor.T.astype(bf16)
    copies[2].wait()
    copies[3].wait()
    lane = lax.broadcasted_iota(jnp.int32, (1, rank), 1)
    totals[2] = jnp.where(lane < rank // 2, live_held[0], live_held[1]).astype(f32)


def fetch(qs, qt, table, live):
    rows, rank = qs.shape
    return call(
        fetch_kernel, "fetch", [HBM] * 4, [VMEM] * 4,
        [
            pltpu.VMEM((2, rows, rank), f32), pltpu.VMEM(table.shape, table.dtype),
            pltpu.VMEM((2, rank, rows), bf16), array((3, 1, rank)),
        ],
        [pltpu.SMEM((2,), jnp.int32), pltpu.SemaphoreType.DMA((4,))],
        pl.CostEstimate(flops=0, bytes_accessed=8 * rows * rank, transcendentals=0),
    )(*far(qs, qt, table, live))


def stack_kernel(*refs):
    out = refs[-1]
    for i in range(out.shape[0]):
        out[i] = refs[i][...]


def stack_pieces(pieces, after):
    return call(
        stack_kernel, "stack", [VMEM] * len(pieces) + [ANY] * len(after), VMEM,
        array((len(pieces),) + pieces[0].shape, pieces[0].dtype),
    )(*pieces, *after)


def joined_table(me, j, even, odd):
    swapped = (me & 1) == 1
    a, b = even[j], odd[j]
    return jnp.concatenate([jnp.where(swapped, b, a), jnp.where(swapped, a, b)])


def first_kernel(masks, later_masks, place, xs, xt, even, odd, part, later, held, sems):
    me = place[0]
    width = 2 * even.shape[1]

    def copy(x, mask, out, sem):
        start = pl.multiple_of(((me ^ mask) >> 1) * width, width)
        made = pltpu.make_async_copy(x.at[:, pl.ds(start, width)], out, sem)
        made.start()
        return made

    blocks = len(masks)
    now = [
        [copy(x, m, held.at[t, j], sems.at[t, j]) for j, m in enumerate(masks)]
        for t, x in enumerate((xs, xt))
    ]
    after = [
        copy(x, m, later.at[t, j], sems.at[t, blocks + j])
        for j, m in enumerate(later_masks)
        for t, x in enumerate((xs, xt))
    ]
    for t in range(2):
        value = None
        for j in range(blocks):
            now[t][j].wait()
            term = jnp.dot(held[t, j], joined_table(me, j, even, odd), preferred_element_type=f32)
            value = term if value is None else value + term
        part[t] = value
    for made in after:
        made.wait()


def first_share(place, xs, xt, masks, later_masks, even, odd):
    rows, genes = xs.shape
    blocks, width, dim = even.shape
    return call(
        functools.partial(first_kernel, masks, later_masks), "embed_first",
        [SMEM, HBM, HBM, VMEM, VMEM], [VMEM] * 2,
        [array((2, rows, dim)), pltpu.VMEM((2, len(later_masks), rows, 2 * width), bf16)],
        [
            pltpu.VMEM((2, blocks, rows, 2 * width), bf16),
            pltpu.SemaphoreType.DMA((2, blocks + len(later_masks))),
        ],
        pl.CostEstimate(
            flops=2 * rows * genes * dim, bytes_accessed=4 * rows * genes, transcendentals=0
        ),
    )(place, *far(xs, xt), even, odd)


def gate_kernel(value, after, out):
    out[...] = value[...]


def gate(value, after):
    return call(
        gate_kernel, "gate", [VMEM, ANY], VMEM, array(value.shape, value.dtype)
    )(value, after)


def added_products(me, x, t, at, even, odd, value):
    for j in range(even.shape[0]):
        table = joined_table(me, j, even, odd)
        value = value + jnp.dot(x[t, at + j], table, preferred_element_type=f32)
    return value


def next_kernel(at, place, x, part, even, odd, out):
    for t in range(2):
        out[t] = added_products(place[0], x, t, at, even, odd, part[t])


def next_share(at, place, x, part, even, odd):
    return call(
        functools.partial(next_kernel, at), "embed_next", [SMEM] + [VMEM] * 4, VMEM, array(part.shape),
        cost=pl.CostEstimate(
            flops=16 * part.shape[1] * part.shape[2] * even.shape[1], bytes_accessed=0, transcendentals=0
        ),
    )(place, x, part, even, odd)


def whole_kernel(masks, place, xs, xt, pieces, part, table):
    genes = pieces.shape[1]
    for j, mask in enumerate(masks):
        start = pl.multiple_of((place[0] ^ mask) * genes, genes)
        table[pl.ds(start, genes), :] = pieces[j]
    for t, x in enumerate((xs, xt)):
        part[t] = jnp.dot(x[...], table[...], preferred_element_type=f32)


def whole_product(place, xs, xt, masks, pieces):
    rows, genes = xs.shape
    dim = pieces.shape[2]
    return call(
        functools.partial(whole_kernel, masks), "embed_whole", [SMEM] + [VMEM] * 3, VMEM,
        array((2, rows, dim)), [pltpu.VMEM((genes, dim), bf16)],
    )(place, xs, xt, pieces)


def cross_kernel(flip, at, place, part, q, turned, totals, *refs):
    if at is not None:
        (x, even, odd), refs = refs[:3], refs[3:]
    emb, out, norms, *masks = refs
    t = (place[0] & 1) ^ flip
    _, rows, rank = q.shape
    block = rows // STEPS
    value = part[t]
    if at is not None:
        value = added_products(place[0], x, t, at, even, odd, value)
    emb[...] = value
    mean = (jnp.sum(fold(value), axis=0, keepdims=True) / rows).astype(bf16).astype(f32)
    norm_sum = rest = None
    for step in range(STEPS):
        span = slice(step * block, (step + 1) * block)
        value = emb[span, :]
        centred = (value - mean).astype(bf16)
        rest = add_to(rest, jnp.dot(turned[t, :, span], centred, preferred_element_type=f32))
        squares = jnp.sum(value * value, axis=1, keepdims=True)
        norms[span, :] = squares
        norm_sum = add_to(norm_sum, fold(squares * q[t, span, :]))
    norm_sum = jnp.sum(norm_sum, axis=0, keepdims=True) * (1.0 / rank)
    number = totals[2]
    out[0:rank, :] = rest
    out[rank:, :] = jnp.concatenate([mean, totals[t], norm_sum, number, jnp.zeros((4, rank), f32)])
    for mask in masks:
        for i in range(2):
            live = number[:, i * (rank // 2) : i * (rank // 2) + 1].astype(jnp.int32)
            mask[i] = (lax.broadcasted_iota(jnp.int32, (rows, 1), 0) < live).astype(f32)


def cross(flip, at, place, part, q, turned, totals, *rest):
    _, rows, rank = q.shape
    dim = part.shape[2]
    masks = [] if flip else [array((2, rows, 1))]
    return call(
        functools.partial(cross_kernel, flip, at), "cross", [SMEM] + [VMEM] * (4 + len(rest)),
        [VMEM] * (3 + len(masks)),
        [array((rows, dim)), array((rank + 8, dim)), array((rows, 1))] + masks,
        cost=pl.CostEstimate(flops=2 * rank * dim * q.shape[1], bytes_accessed=0, transcendentals=0),
    )(place, part, *near(q, turned), totals, *rest)


def split_row(row):
    high = row.astype(bf16).astype(f32)
    middle = (row - high).astype(bf16).astype(f32)
    return [high, middle, row - high - middle]


def tail_rows(cards):
    return -(-(8 + 4 * cards) // 16) * 16


def make_tail(norm, number, cards):
    width = norm.shape[1]
    rows = split_row(norm) + split_row(number) + [jnp.zeros((2, width), f32)] + cards
    used = sum(r.shape[0] for r in rows)
    filler = tail_rows((used - 8) // 4) - used
    if filler:
        rows.append(jnp.zeros((filler, width), f32))
    return jnp.concatenate(rows)


def three(tail, start):
    return (tail[start : start + 1] + tail[start + 1 : start + 2]) + tail[start + 2 : start + 3]


def pack_pair_kernel(own, recv, out):
    rank = own.shape[0] - 8
    out[0:rank, :] = (own[0:rank, :] + recv[0:rank, :]).astype(bf16)
    cards = []
    for ref in (own, recv):
        cards += [ref[rank : rank + 1, :]] + split_row(ref[rank + 1 : rank + 2, :])
    norm = own[rank + 2 : rank + 3, :] + recv[rank + 2 : rank + 3, :]
    number = own[rank + 3 : rank + 4, :] + recv[rank + 3 : rank + 4, :]
    out[rank:, :] = make_tail(norm, number, cards).astype(bf16)


def pack_pair(own, recv):
    rank, dim = own.shape[0] - 8, own.shape[1]
    return call(
        pack_pair_kernel, "pack_pair", [VMEM] * 2, VMEM, array((rank + tail_rows(2), dim), bf16)
    )(own, recv)


def ordered_cards(tails, cards, flags):
    lists = [tail[8 : 8 + 4 * cards] for tail in tails]
    for flag in flags:
        lists = [
            jnp.concatenate([jnp.where(flag, a, b), jnp.where(flag, b, a)])
            for a, b in zip(lists[::2], lists[1::2])
        ]
    return lists[0]


def tree(values):
    while len(values) > 1:
        values = [a + b for a, b in zip(values[::2], values[1::2])]
    return values[0]


def merge_kernel(rank, cards, bits, place, *refs):
    payloads, out = refs[:-1], refs[-1]
    out[0:rank, :] = tree([p[0:rank, :].astype(f32) for p in payloads]).astype(bf16)
    tails = [p[rank:, :].astype(f32) for p in payloads]
    listed = ordered_cards(tails, cards, [(place[0] & bit) == 0 for bit in bits])
    norm, number = (tree([three(tail, i) for tail in tails]) for i in (0, 3))
    out[rank:, :] = make_tail(norm, number, [listed]).astype(bf16)


def merge(rank, cards, bits, place, *payloads):
    return call(
        functools.partial(merge_kernel, rank, cards, bits), "merge",
        [SMEM] + [VMEM] * len(payloads), VMEM,
        array((rank + tail_rows(len(payloads) * cards), payloads[0].shape[1]), bf16),
    )(place, *payloads)


def total_of(rank, cards, *payloads):
    def unpack(ref):
        tail = ref[rank:, :].astype(f32)
        heights, means, sums = [], [], jnp.zeros((1, tail.shape[1]), f32)
        for c in range(cards):
            at = 8 + 4 * c
            heights.append(tail[at + 1 : at + 4])
            means += [tail[at : at + 1]] * 3
            sums = sums + three(tail, at + 1)
        left, right = jnp.concatenate(heights), jnp.concatenate(means)
        joined = lax.dot_general(
            left.T.astype(bf16), right.astype(bf16), (((1,), (0,)), ((), ())),
            preferred_element_type=f32,
        )
        return ref[0:rank, :].astype(f32) + joined, three(tail, 0), sums, three(tail, 3)

    return [tree(list(values)) for values in zip(*[unpack(ref) for ref in payloads])]


def store_total(parts, out):
    rank = parts[0].shape[0]
    out[0:rank, :] = parts[0]
    out[rank:, :] = jnp.concatenate(parts[1:] + [jnp.zeros((5, out.shape[1]), f32)])


def store_sums(sums, levels, copies):
    both = jnp.concatenate(
        [level * jnp.sum(part, axis=0, keepdims=True) for part, level in zip(sums, levels)]
    )
    for i in range(copies.shape[0]):
        copies[i] = both


def kernel_half(cells, t, mask, norms, emb, q, weights, parts, k, sums_out):
    _, rows, rank = q.shape
    block = rows // STEPS
    inverse = (-step_size * LOG2_E) / (D * (weights[...] * (cells / rank)))
    product, norm, total, _ = parts
    matrix = stacked_right((-2.0 * inverse) * product.T)
    slope, offset = total * inverse, norm * inverse
    sums = None
    for step in range(STEPS):
        at = slice(step * block, (step + 1) * block)
        value = emb[at, :]
        grad = norms[at, :] * slope + offset + jnp.dot(
            stacked_left(value), matrix, preferred_element_type=f32
        )
        kernel = (q[t, at, :] * (1.0 / rank)) * jnp.exp2(grad)
        k[at, :] = kernel
        scale = mask[t, at, :] / jnp.sum(kernel, axis=1, keepdims=True)
        sums = add_to(sums, fold(scale * kernel))
    sums_out[...] = sums


def other_kernel(cells, cards, place, mask, norms, emb, q, weights, near_part, far_part, k, sums, mine):
    parts = total_of(q.shape[2], cards, near_part, far_part)
    store_total(parts, mine)
    kernel_half(cells, 1 - (place[0] & 1), mask, norms, emb, q, weights, parts, k, sums)


def levels_of(cells, summed):
    rank = summed.shape[1]
    numbers = summed[rank + 2 : rank + 3, :]
    return cells / numbers[:, 0:1], cells / numbers[:, rank // 2 : rank // 2 + 1]


def in_order(first, own, out):
    return jnp.where(first, own, out), jnp.where(first, out, own)


def write_tables(cells, first, weights, mine, other, consts):
    rank = weights.shape[1]
    a = mine[...]
    product_b, norm_b, total_b, _ = other
    col_mass = weights[...] * (cells / rank)
    norm_a, total_a = a[rank : rank + 1], a[rank + 1 : rank + 2]
    products = jnp.sum((a[0:rank] * product_b).T, axis=0, keepdims=True)
    mixed = in_order(first, norm_a * total_b, total_a * norm_b)
    cost = (mixed[0] + mixed[1] - 2.0 * products) / D
    consts[0:1, :] = col_mass * jnp.exp(step_size * cost / (col_mass * col_mass))
    for t, level in enumerate(levels_of(cells, mine)):
        consts[1 + t : 2 + t, :] = jnp.broadcast_to(level, (1, rank))


def own_kernel(
    cells, cards, place, mask, norms, emb, q, weights, mine, near_part, far_part, sums_other,
    k, copies, consts, sums,
):
    core = place[0] & 1
    parts = total_of(q.shape[2], cards, near_part, far_part)
    write_tables(cells, core == 0, weights, mine, parts, consts)
    kernel_half(cells, core, mask, norms, emb, q, weights, parts, k, sums)
    store_sums(in_order(core == 0, sums[...], sums_other[...]), levels_of(cells, mine), copies)


def cube_root(x):
    y = jnp.exp(jnp.log(x) * (1.0 / 3.0))
    refined = y - (y - x / (y * y)) * (1.0 / 3.0)
    return jnp.where((x > 0.0) & (x < jnp.inf), refined, y)


def duals_of(parts, consts):
    sums = jnp.sum(parts[...], axis=0)
    sum_s, sum_t = sums[0:1, :], sums[1:2, :]
    mass = cube_root(consts[0:1, :] * sum_s * sum_t)
    return mass, mass / sum_s, mass / sum_t


def row_sums(value):
    folded = value[:, 0:128]
    for start in range(128, value.shape[1], 128):
        folded = folded + value[:, start : start + 128]
    parts = jnp.concatenate(halves(folded), axis=1)
    return jnp.dot(parts, jnp.ones((256, 128), bf16), preferred_element_type=f32)


def scale_rows(value, scale):
    return jnp.concatenate(
        [scale * value[:, i : i + 128] for i in range(0, value.shape[1], 128)], axis=1
    )


def sweep_kernel(last, place, mask, k_own, k_other, parts, consts, *refs):
    copies = refs[-1]
    core = place[0] & 1
    first = core == 0
    block = k_own.shape[0] // STEPS

    _, *duals = duals_of(parts, consts)
    sums = [None, None]
    for step in range(STEPS):
        at = slice(step * block, (step + 1) * block)
        for i, (k, t, dual) in enumerate(
            zip((k_own, k_other), (core, 1 - core), in_order(first, *duals))
        ):
            kernel = k[at, :]
            scaled = scale_rows(kernel, mask[t, at, :] / row_sums(kernel * dual))
            if last:
                refs[0][t, at, :] = scaled
            sums[i] = add_to(sums[i], fold(scaled))
    store_sums(in_order(first, *sums), (consts[1:2, :], consts[2:3, :]), copies)


def finish_kernel(cells, scaled, parts, consts, fs, ft, weights, held, mass_held, sems, mass_sem):
    _, rows, rank = scaled.shape
    block = rows // STEPS
    mass, dual_s, dual_t = duals_of(parts, consts)
    mass_held[...] = mass * (rank / cells)
    copies = [pltpu.make_async_copy(mass_held, weights, mass_sem)]
    copies[0].start()
    dual_s, dual_t = dual_s * (rank * consts[1:2, :]), dual_t * (rank * consts[2:3, :])
    for step in range(STEPS):
        at = slice(step * block, (step + 1) * block)
        for t, (dual, out) in enumerate(((dual_s, fs), (dual_t, ft))):
            held[t, at, :] = scaled[t, at, :] * dual
            copy = pltpu.make_async_copy(held.at[t, at], out.at[at], sems.at[t, step])
            copy.start()
            copies.append(copy)
    for copy in copies:
        copy.wait()


def kernels(cells, cards, count, place, mask, norms, emb, q, weights, mine, other):
    _, rows, rank = q.shape
    dim = emb[0].shape[1]
    cost = pl.CostEstimate(flops=6 * rows * rank * dim, bytes_accessed=0, transcendentals=rows * rank)
    k_other, sums_other, total = call(
        functools.partial(other_kernel, cells, cards), "kernel_other", [SMEM] + [VMEM] * 7, [VMEM] * 3,
        [array((rows, rank)), array((8, rank)), array((rank + 8, dim))], cost=cost,
    )(place, mask, norms[1], emb[1], *near(q), weights, *mine)
    k_own, copies, consts = call(
        functools.partial(own_kernel, cells, cards), "kernel_own", [SMEM] + [VMEM] * 9, [VMEM] * 3,
        [array((rows, rank)), array((count, 2, rank)), array((8, rank))], [pltpu.VMEM((8, rank), f32)], cost,
    )(place, mask, norms[0], emb[0], *near(q), weights, total, *other, sums_other)
    return k_own, k_other, copies, consts


def sweep(count, last, place, mask, k_own, k_other, parts, consts):
    rows, rank = k_own.shape
    scaled = [array((2, rows, rank))] if last else []
    return call(
        functools.partial(sweep_kernel, last), "sweep", [SMEM] + [VMEM] * 5,
        [VMEM] * (len(scaled) + 1), scaled + [array((count, 2, rank))],
    )(place, mask, k_own, k_other, parts, consts)


def finish(cells, scaled, parts, consts):
    _, rows, rank = scaled.shape
    return call(
        functools.partial(finish_kernel, cells), "finish", [VMEM] * 3, [HBM] * 3,
        [array((rows, rank))] * 2 + [array((1, rank))],
        [
            pltpu.VMEM((2, rows, rank), f32), pltpu.VMEM((1, rank), f32),
            pltpu.SemaphoreType.DMA((2, STEPS)), pltpu.SemaphoreType.DMA,
        ],
    )(scaled, parts, consts)


def on_device(
    source_expr, target_expr, loadings, source_prev, target_prev, weights_prev, live_counts
):
    count = lax.axis_size("cell")
    place = lax.axis_index("cell").astype(jnp.int32)[None]
    live = live_counts[:, 0]
    rows, rank = source_prev.shape
    cells = rows * count
    bits = [1 << b for b in range(count.bit_length() - 1)]
    opposite = bits[-1] | bits[-2]
    exchange = functools.partial(lax.all_to_all, axis_name="cell", split_axis=0, concat_axis=0)

    q, own_table, turned, totals = fetch(source_prev, target_prev, loadings, live)
    stack = stack_pieces([own_table, swap(loadings, count, opposite)], [totals])
    masks = [0, opposite]
    if count == 16 and loadings.shape[0] % 64 == 0:
        quad = [6, 4, 2]
        arrived = [swap(stack, count, m) for m in quad]
        later = [m ^ q for q in quad for m in masks]
        emb, x = first_share(
            place, source_expr, target_expr, masks, later, stack, swap(stack, count, 1)
        )
        arrived = [gate(piece, emb) for piece in arrived]
        for i, piece in enumerate(arrived[:-1]):
            emb = next_share(2 * i, place, x, emb, piece, swap(piece, count, 1))
        at, rest = 2 * len(arrived) - 2, (x, arrived[-1], swap(arrived[-1], count, 1))
    else:
        for bit in reversed(bits[:-1]):
            stack = jnp.concatenate([stack, swap(stack, count, bit)])
            masks = masks + [m ^ bit for m in masks]
        emb = whole_product(place, source_expr, target_expr, masks, stack)
        at, rest = None, ()
    emb_other, send, norms_other = cross(1, at, place, emb, q, turned, totals, *rest)
    emb_own, own, norms_own, mask = cross(0, at, place, emb, q, turned, totals, *rest)

    payload = pack_pair(own, swap(send, count, 1))
    cards = 2
    inner = bits[1:-1]
    while inner:
        used, inner = inner[:2], inner[2:]
        steps = [used[0], used[1], used[0] | used[1]] if len(used) == 2 else used
        moved = {m: swap(payload, count, m) for m in steps[1:2] + steps[:1] + steps[2:]}
        others = [moved[m] for m in steps]
        payload = merge(rank, cards, used, place, payload, *others)
        cards = cards * (1 + len(others))
    mine = [payload, swap(payload, count, opposite)]
    other = [swap(part, count, 1) for part in mine]

    k_own, k_other, copies, consts = kernels(
        cells, cards, count, place, mask, (norms_own, norms_other), (emb_own, emb_other), q,
        weights_prev[None], mine, other,
    )
    scaled = []
    for step_index in range(1, ITERS):
        last = step_index == ITERS - 1
        *scaled, copies = sweep(count, last, place, mask, k_own, k_other, exchange(copies), consts)
    out_s, out_t, weights = finish(cells, *scaled, exchange(copies), consts)
    return out_s, out_t, weights[0]


def solution(mesh):
    in_specs = (
        P(("grp", "cell"), None),
        P(("grp", "cell"), None),
        P("cell", None),
        P(("grp", "cell"), None),
        P(("grp", "cell"), None),
        P("grp"),
        P(None, ("grp", "cell")),
    )
    out_specs = (P(("grp", "cell"), None), P(("grp", "cell"), None), P("grp"))
    return jax.shard_map(
        on_device, mesh=mesh, in_specs=in_specs, out_specs=out_specs, check_vma=False
    )
```

```python
import functools

import jax
import jax.numpy as jnp
from jax import lax
from jax.experimental import pallas as pl
from jax.experimental.pallas import tpu as pltpu
from jax.sharding import PartitionSpec as P

D = 256
ITERS = 3
STEPS = 4
SWEEP_STEPS = 1

step_size = 1.0
LOG2_E = 1.4426950408889634
f32 = jnp.float32
bf16 = jnp.bfloat16
LIMIT = 16 * 1024 * 1024


def swap(value, count, mask):
    return lax.ppermute(value, "cell", [(i, i ^ mask) for i in range(count)])


def halves(value):
    upper = value.astype(bf16)
    return upper, (value - upper.astype(f32)).astype(bf16)


def stacked_left(value):
    upper, lower = halves(value)
    return jnp.concatenate([upper, upper, lower], axis=1)


def stacked_right(value):
    upper, lower = halves(value)
    return jnp.concatenate([upper, lower, upper])


VMEM = pl.BlockSpec(memory_space=pltpu.VMEM)
SMEM = pl.BlockSpec(memory_space=pltpu.SMEM)
HBM = pl.BlockSpec(memory_space=pltpu.HBM)
ANY = pl.BlockSpec(memory_space=pl.ANY)


def far(*arrays):
    return [pltpu.with_memory_space_constraint(a, pltpu.HBM) for a in arrays]


def near(*arrays):
    return [pltpu.with_memory_space_constraint(a, pltpu.VMEM) for a in arrays]


def array(shape, dtype=f32):
    return jax.ShapeDtypeStruct(shape, dtype)


def call(body, name, in_specs, out_specs, out_shape, scratch=(), cost=None):
    return pl.pallas_call(
        body,
        in_specs=in_specs,
        out_specs=out_specs,
        out_shape=out_shape,
        scratch_shapes=list(scratch),
        compiler_params=pltpu.CompilerParams(vmem_limit_bytes=LIMIT),
        cost_estimate=cost,
        name=name,
    )


def rows_of(step, block):
    return pl.ds(pl.multiple_of(step * block, block), block)


def fold(value):
    return jnp.sum(value.reshape(value.shape[0] // 8, 8, value.shape[1]), axis=0)


def add_to(sums, value):
    return value if sums is None else sums + value


def fetch_kernel(qs, qt, table, live, q_out, table_out, turned, totals, live_held, sems):
    pairs = ((qs, q_out.at[0]), (qt, q_out.at[1]), (table, table_out), (live, live_held))
    copies = [pltpu.make_async_copy(a, b, sems.at[i]) for i, (a, b) in enumerate(pairs)]
    for copy in copies:
        copy.start()
    rank = qs.shape[1]
    for t in range(2):
        copies[t].wait()
        factor = q_out[t] * (1.0 / rank)
        totals[t] = jnp.sum(factor, axis=0, keepdims=True)
        turned[t] = factor.T.astype(bf16)
    copies[2].wait()
    copies[3].wait()
    lane = lax.broadcasted_iota(jnp.int32, (1, rank), 1)
    totals[2] = jnp.where(lane < rank // 2, live_held[0], live_held[1]).astype(f32)


def fetch(qs, qt, table, live):
    rows, rank = qs.shape
    return call(
        fetch_kernel, "fetch", [HBM] * 4, [VMEM] * 4,
        [
            pltpu.VMEM((2, rows, rank), f32), pltpu.VMEM(table.shape, table.dtype),
            pltpu.VMEM((2, rank, rows), bf16), array((3, 1, rank)),
        ],
        [pltpu.SMEM((2,), jnp.int32), pltpu.SemaphoreType.DMA((4,))],
        pl.CostEstimate(flops=0, bytes_accessed=8 * rows * rank, transcendentals=0),
    )(*far(qs, qt, table, live))


def stack_kernel(*refs):
    out = refs[-1]
    for i in range(out.shape[0]):
        out[i] = refs[i][...]


def stack_pieces(pieces, after):
    return call(
        stack_kernel, "stack", [VMEM] * len(pieces) + [ANY] * len(after), VMEM,
        array((len(pieces),) + pieces[0].shape, pieces[0].dtype),
    )(*pieces, *after)


def joined_table(me, j, even, odd):
    swapped = (me & 1) == 1
    a, b = even[j], odd[j]
    return jnp.concatenate([jnp.where(swapped, b, a), jnp.where(swapped, a, b)])


def first_kernel(masks, later_masks, place, xs, xt, even, odd, part, later, held, sems):
    me = place[0]
    width = 2 * even.shape[1]

    def copy(x, mask, out, sem):
        start = pl.multiple_of(((me ^ mask) >> 1) * width, width)
        made = pltpu.make_async_copy(x.at[:, pl.ds(start, width)], out, sem)
        made.start()
        return made

    blocks = len(masks)
    now = [
        [copy(x, m, held.at[t, j], sems.at[t, j]) for j, m in enumerate(masks)]
        for t, x in enumerate((xs, xt))
    ]
    after = [
        copy(x, m, later.at[t, j], sems.at[t, blocks + j])
        for j, m in enumerate(later_masks)
        for t, x in enumerate((xs, xt))
    ]
    for t in range(2):
        value = None
        for j in range(blocks):
            now[t][j].wait()
            term = jnp.dot(held[t, j], joined_table(me, j, even, odd), preferred_element_type=f32)
            value = term if value is None else value + term
        part[t] = value
    for made in after:
        made.wait()


def first_share(place, xs, xt, masks, later_masks, even, odd):
    rows, genes = xs.shape
    blocks, width, dim = even.shape
    return call(
        functools.partial(first_kernel, masks, later_masks), "embed_first",
        [SMEM, HBM, HBM, VMEM, VMEM], [VMEM] * 2,
        [array((2, rows, dim)), pltpu.VMEM((2, len(later_masks), rows, 2 * width), bf16)],
        [
            pltpu.VMEM((2, blocks, rows, 2 * width), bf16),
            pltpu.SemaphoreType.DMA((2, blocks + len(later_masks))),
        ],
        pl.CostEstimate(
            flops=2 * rows * genes * dim, bytes_accessed=4 * rows * genes, transcendentals=0
        ),
    )(place, *far(xs, xt), even, odd)


def gate_kernel(value, after, out):
    out[...] = value[...]


def gate(value, after):
    return call(
        gate_kernel, "gate", [VMEM, ANY], VMEM, array(value.shape, value.dtype)
    )(value, after)


def added_products(me, x, t, at, even, odd, value):
    for j in range(even.shape[0]):
        table = joined_table(me, j, even, odd)
        value = value + jnp.dot(x[t, at + j], table, preferred_element_type=f32)
    return value


def next_kernel(at, place, x, part, even, odd, out):
    for t in range(2):
        out[t] = added_products(place[0], x, t, at, even, odd, part[t])


def next_share(at, place, x, part, even, odd):
    return call(
        functools.partial(next_kernel, at), "embed_next", [SMEM] + [VMEM] * 4, VMEM, array(part.shape),
        cost=pl.CostEstimate(
            flops=16 * part.shape[1] * part.shape[2] * even.shape[1], bytes_accessed=0, transcendentals=0
        ),
    )(place, x, part, even, odd)


def whole_kernel(masks, place, xs, xt, pieces, part, table):
    genes = pieces.shape[1]
    for j, mask in enumerate(masks):
        start = pl.multiple_of((place[0] ^ mask) * genes, genes)
        table[pl.ds(start, genes), :] = pieces[j]
    for t, x in enumerate((xs, xt)):
        part[t] = jnp.dot(x[...], table[...], preferred_element_type=f32)


def whole_product(place, xs, xt, masks, pieces):
    rows, genes = xs.shape
    dim = pieces.shape[2]
    return call(
        functools.partial(whole_kernel, masks), "embed_whole", [SMEM] + [VMEM] * 3, VMEM,
        array((2, rows, dim)), [pltpu.VMEM((genes, dim), bf16)],
    )(place, xs, xt, pieces)


def cross_kernel(flip, at, place, part, q, turned, totals, *refs):
    if at is not None:
        (x, even, odd), refs = refs[:3], refs[3:]
    emb, out, norms, *masks = refs
    t = (place[0] & 1) ^ flip
    _, rows, rank = q.shape
    block = rows // STEPS
    value = part[t]
    if at is not None:
        value = added_products(place[0], x, t, at, even, odd, value)
    emb[...] = value
    mean = (jnp.sum(fold(value), axis=0, keepdims=True) / rows).astype(bf16).astype(f32)
    norm_sum = rest = None
    for step in range(STEPS):
        span = slice(step * block, (step + 1) * block)
        value = emb[span, :]
        centred = (value - mean).astype(bf16)
        rest = add_to(rest, jnp.dot(turned[t, :, span], centred, preferred_element_type=f32))
        squares = jnp.sum(value * value, axis=1, keepdims=True)
        norms[span, :] = squares
        norm_sum = add_to(norm_sum, fold(squares * q[t, span, :]))
    norm_sum = jnp.sum(norm_sum, axis=0, keepdims=True) * (1.0 / rank)
    number = totals[2]
    out[0:rank, :] = rest
    out[rank:, :] = jnp.concatenate([mean, totals[t], norm_sum, number, jnp.zeros((4, rank), f32)])
    for mask in masks:
        for i in range(2):
            live = number[:, i * (rank // 2) : i * (rank // 2) + 1].astype(jnp.int32)
            mask[i] = (lax.broadcasted_iota(jnp.int32, (rows, 1), 0) < live).astype(f32)


def cross(flip, at, place, part, q, turned, totals, *rest):
    _, rows, rank = q.shape
    dim = part.shape[2]
    masks = [] if flip else [array((2, rows, 1))]
    return call(
        functools.partial(cross_kernel, flip, at), "cross", [SMEM] + [VMEM] * (4 + len(rest)),
        [VMEM] * (3 + len(masks)),
        [array((rows, dim)), array((rank + 8, dim)), array((rows, 1))] + masks,
        cost=pl.CostEstimate(flops=2 * rank * dim * q.shape[1], bytes_accessed=0, transcendentals=0),
    )(place, part, *near(q, turned), totals, *rest)


def split_row(row):
    high = row.astype(bf16).astype(f32)
    middle = (row - high).astype(bf16).astype(f32)
    return [high, middle, row - high - middle]


def tail_rows(cards):
    return -(-(8 + 4 * cards) // 16) * 16


def make_tail(norm, number, cards):
    width = norm.shape[1]
    rows = split_row(norm) + split_row(number) + [jnp.zeros((2, width), f32)] + cards
    used = sum(r.shape[0] for r in rows)
    filler = tail_rows((used - 8) // 4) - used
    if filler:
        rows.append(jnp.zeros((filler, width), f32))
    return jnp.concatenate(rows)


def three(tail, start):
    return (tail[start : start + 1] + tail[start + 1 : start + 2]) + tail[start + 2 : start + 3]


def pack_pair_kernel(own, recv, out):
    rank = own.shape[0] - 8
    out[0:rank, :] = (own[0:rank, :] + recv[0:rank, :]).astype(bf16)
    cards = []
    for ref in (own, recv):
        cards += [ref[rank : rank + 1, :]] + split_row(ref[rank + 1 : rank + 2, :])
    norm = own[rank + 2 : rank + 3, :] + recv[rank + 2 : rank + 3, :]
    number = own[rank + 3 : rank + 4, :] + recv[rank + 3 : rank + 4, :]
    out[rank:, :] = make_tail(norm, number, cards).astype(bf16)


def pack_pair(own, recv):
    rank, dim = own.shape[0] - 8, own.shape[1]
    return call(
        pack_pair_kernel, "pack_pair", [VMEM] * 2, VMEM, array((rank + tail_rows(2), dim), bf16)
    )(own, recv)


def ordered_cards(tails, cards, flags):
    lists = [tail[8 : 8 + 4 * cards] for tail in tails]
    for flag in flags:
        lists = [
            jnp.concatenate([jnp.where(flag, a, b), jnp.where(flag, b, a)])
            for a, b in zip(lists[::2], lists[1::2])
        ]
    return lists[0]


def tree(values):
    while len(values) > 1:
        values = [a + b for a, b in zip(values[::2], values[1::2])]
    return values[0]


def merge_kernel(rank, cards, bits, place, *refs):
    payloads, out = refs[:-1], refs[-1]
    out[0:rank, :] = tree([p[0:rank, :].astype(f32) for p in payloads]).astype(bf16)
    tails = [p[rank:, :].astype(f32) for p in payloads]
    listed = ordered_cards(tails, cards, [(place[0] & bit) == 0 for bit in bits])
    norm, number = (tree([three(tail, i) for tail in tails]) for i in (0, 3))
    out[rank:, :] = make_tail(norm, number, [listed]).astype(bf16)


def merge(rank, cards, bits, place, *payloads):
    return call(
        functools.partial(merge_kernel, rank, cards, bits), "merge",
        [SMEM] + [VMEM] * len(payloads), VMEM,
        array((rank + tail_rows(len(payloads) * cards), payloads[0].shape[1]), bf16),
    )(place, *payloads)


def total_of(rank, cards, *payloads):
    def unpack(ref):
        tail = ref[rank:, :].astype(f32)
        heights, means, sums = [], [], jnp.zeros((1, tail.shape[1]), f32)
        for c in range(cards):
            at = 8 + 4 * c
            heights.append(tail[at + 1 : at + 4])
            means += [tail[at : at + 1]] * 3
            sums = sums + three(tail, at + 1)
        left, right = jnp.concatenate(heights), jnp.concatenate(means)
        joined = lax.dot_general(
            left.T.astype(bf16), right.astype(bf16), (((1,), (0,)), ((), ())),
            preferred_element_type=f32,
        )
        return ref[0:rank, :].astype(f32) + joined, three(tail, 0), sums, three(tail, 3)

    return [tree(list(values)) for values in zip(*[unpack(ref) for ref in payloads])]


def store_total(parts, out):
    rank = parts[0].shape[0]
    out[0:rank, :] = parts[0]
    out[rank:, :] = jnp.concatenate(parts[1:] + [jnp.zeros((5, out.shape[1]), f32)])


def store_sums(sums, levels, copies):
    both = jnp.concatenate(
        [level * jnp.sum(part, axis=0, keepdims=True) for part, level in zip(sums, levels)]
    )
    for i in range(copies.shape[0]):
        copies[i] = both


def kernel_half(cells, t, mask, norms, emb, q, weights, parts, k, sums_out):
    _, rows, rank = q.shape
    block = rows // STEPS
    inverse = (-step_size * LOG2_E) / (D * (weights[...] * (cells / rank)))
    product, norm, total, _ = parts
    matrix = stacked_right((-2.0 * inverse) * product.T)
    slope, offset = total * inverse, norm * inverse
    sums = None
    for step in range(STEPS):
        at = slice(step * block, (step + 1) * block)
        value = emb[at, :]
        grad = norms[at, :] * slope + offset + jnp.dot(
            stacked_left(value), matrix, preferred_element_type=f32
        )
        kernel = (q[t, at, :] * (1.0 / rank)) * jnp.exp2(grad)
        k[at, :] = kernel
        scale = mask[t, at, :] / jnp.sum(kernel, axis=1, keepdims=True)
        sums = add_to(sums, fold(scale * kernel))
    sums_out[...] = sums


def other_kernel(cells, cards, place, mask, norms, emb, q, weights, near_part, far_part, k, sums, mine):
    parts = total_of(q.shape[2], cards, near_part, far_part)
    store_total(parts, mine)
    kernel_half(cells, 1 - (place[0] & 1), mask, norms, emb, q, weights, parts, k, sums)


def levels_of(cells, summed):
    rank = summed.shape[1]
    numbers = summed[rank + 2 : rank + 3, :]
    return cells / numbers[:, 0:1], cells / numbers[:, rank // 2 : rank // 2 + 1]


def in_order(first, own, out):
    return jnp.where(first, own, out), jnp.where(first, out, own)


def write_tables(cells, first, weights, mine, other, consts):
    rank = weights.shape[1]
    a = mine[...]
    product_b, norm_b, total_b, _ = other
    col_mass = weights[...] * (cells / rank)
    norm_a, total_a = a[rank : rank + 1], a[rank + 1 : rank + 2]
    products = jnp.sum((a[0:rank] * product_b).T, axis=0, keepdims=True)
    mixed = in_order(first, norm_a * total_b, total_a * norm_b)
    cost = (mixed[0] + mixed[1] - 2.0 * products) / D
    consts[0:1, :] = col_mass * jnp.exp(step_size * cost / (col_mass * col_mass))
    for t, level in enumerate(levels_of(cells, mine)):
        consts[1 + t : 2 + t, :] = jnp.broadcast_to(level, (1, rank))


def own_kernel(
    cells, cards, place, mask, norms, emb, q, weights, mine, near_part, far_part, sums_other,
    k, copies, consts, sums,
):
    core = place[0] & 1
    parts = total_of(q.shape[2], cards, near_part, far_part)
    write_tables(cells, core == 0, weights, mine, parts, consts)
    kernel_half(cells, core, mask, norms, emb, q, weights, parts, k, sums)
    store_sums(in_order(core == 0, sums[...], sums_other[...]), levels_of(cells, mine), copies)


def cube_root(x):
    y = jnp.exp(jnp.log(x) * (1.0 / 3.0))
    refined = y - (y - x / (y * y)) * (1.0 / 3.0)
    return jnp.where((x > 0.0) & (x < jnp.inf), refined, y)


def duals_of(parts, consts):
    sums = jnp.sum(parts[...], axis=0)
    sum_s, sum_t = sums[0:1, :], sums[1:2, :]
    mass = cube_root(consts[0:1, :] * sum_s * sum_t)
    return mass, mass / sum_s, mass / sum_t


def row_sums(value):
    folded = value[:, 0:128]
    for start in range(128, value.shape[1], 128):
        folded = folded + value[:, start : start + 128]
    parts = jnp.concatenate(halves(folded), axis=1)
    return jnp.dot(parts, jnp.ones((256, 128), bf16), preferred_element_type=f32)


def scale_rows(value, scale):
    return jnp.concatenate(
        [scale * value[:, i : i + 128] for i in range(0, value.shape[1], 128)], axis=1
    )


def sweep_kernel(last, place, mask, k_own, k_other, parts, consts, *refs):
    copies = refs[-1]
    core = place[0] & 1
    first = core == 0
    block = k_own.shape[0] // SWEEP_STEPS

    _, *duals = duals_of(parts, consts)
    sums = [None, None]
    for step in range(SWEEP_STEPS):
        at = slice(step * block, (step + 1) * block)
        for i, (k, t, dual) in enumerate(
            zip((k_own, k_other), (core, 1 - core), in_order(first, *duals))
        ):
            kernel = k[at, :]
            scaled = scale_rows(kernel, mask[t, at, :] / row_sums(kernel * dual))
            if last:
                refs[0][t, at, :] = scaled
            sums[i] = add_to(sums[i], fold(scaled))
    store_sums(in_order(first, *sums), (consts[1:2, :], consts[2:3, :]), copies)


def finish_kernel(cells, scaled, parts, consts, fs, ft, weights, held, mass_held, sems, mass_sem):
    _, rows, rank = scaled.shape
    block = rows // STEPS
    mass, dual_s, dual_t = duals_of(parts, consts)
    mass_held[...] = mass * (rank / cells)
    copies = [pltpu.make_async_copy(mass_held, weights, mass_sem)]
    copies[0].start()
    dual_s, dual_t = dual_s * (rank * consts[1:2, :]), dual_t * (rank * consts[2:3, :])
    for step in range(STEPS):
        at = slice(step * block, (step + 1) * block)
        for t, (dual, out) in enumerate(((dual_s, fs), (dual_t, ft))):
            held[t, at, :] = scaled[t, at, :] * dual
            copy = pltpu.make_async_copy(held.at[t, at], out.at[at], sems.at[t, step])
            copy.start()
            copies.append(copy)
    for copy in copies:
        copy.wait()


def kernels(cells, cards, count, place, mask, norms, emb, q, weights, mine, other):
    _, rows, rank = q.shape
    dim = emb[0].shape[1]
    cost = pl.CostEstimate(flops=6 * rows * rank * dim, bytes_accessed=0, transcendentals=rows * rank)
    k_other, sums_other, total = call(
        functools.partial(other_kernel, cells, cards), "kernel_other", [SMEM] + [VMEM] * 7, [VMEM] * 3,
        [array((rows, rank)), array((8, rank)), array((rank + 8, dim))], cost=cost,
    )(place, mask, norms[1], emb[1], *near(q), weights, *mine)
    k_own, copies, consts = call(
        functools.partial(own_kernel, cells, cards), "kernel_own", [SMEM] + [VMEM] * 9, [VMEM] * 3,
        [array((rows, rank)), array((count, 2, rank)), array((8, rank))], [pltpu.VMEM((8, rank), f32)], cost,
    )(place, mask, norms[0], emb[0], *near(q), weights, total, *other, sums_other)
    return k_own, k_other, copies, consts


def sweep(count, last, place, mask, k_own, k_other, parts, consts):
    rows, rank = k_own.shape
    scaled = [array((2, rows, rank))] if last else []
    return call(
        functools.partial(sweep_kernel, last), "sweep", [SMEM] + [VMEM] * 5,
        [VMEM] * (len(scaled) + 1), scaled + [array((count, 2, rank))],
    )(place, mask, k_own, k_other, parts, consts)


def finish(cells, scaled, parts, consts):
    _, rows, rank = scaled.shape
    return call(
        functools.partial(finish_kernel, cells), "finish", [VMEM] * 3, [HBM] * 3,
        [array((rows, rank))] * 2 + [array((1, rank))],
        [
            pltpu.VMEM((2, rows, rank), f32), pltpu.VMEM((1, rank), f32),
            pltpu.SemaphoreType.DMA((2, STEPS)), pltpu.SemaphoreType.DMA,
        ],
    )(scaled, parts, consts)


def on_device(
    source_expr, target_expr, loadings, source_prev, target_prev, weights_prev, live_counts
):
    count = lax.axis_size("cell")
    place = lax.axis_index("cell").astype(jnp.int32)[None]
    live = live_counts[:, 0]
    rows, rank = source_prev.shape
    cells = rows * count
    bits = [1 << b for b in range(count.bit_length() - 1)]
    opposite = bits[-1] | bits[-2]
    exchange = functools.partial(lax.all_to_all, axis_name="cell", split_axis=0, concat_axis=0)

    q, own_table, turned, totals = fetch(source_prev, target_prev, loadings, live)
    stack = stack_pieces([own_table, swap(loadings, count, opposite)], [totals])
    masks = [0, opposite]
    if count == 16 and loadings.shape[0] % 64 == 0:
        quad = [6, 4, 2]
        arrived = [swap(stack, count, m) for m in quad]
        later = [m ^ q for q in quad for m in masks]
        emb, x = first_share(
            place, source_expr, target_expr, masks, later, stack, swap(stack, count, 1)
        )
        arrived = [gate(piece, emb) for piece in arrived]
        for i, piece in enumerate(arrived[:-1]):
            emb = next_share(2 * i, place, x, emb, piece, swap(piece, count, 1))
        at, rest = 2 * len(arrived) - 2, (x, arrived[-1], swap(arrived[-1], count, 1))
    else:
        for bit in reversed(bits[:-1]):
            stack = jnp.concatenate([stack, swap(stack, count, bit)])
            masks = masks + [m ^ bit for m in masks]
        emb = whole_product(place, source_expr, target_expr, masks, stack)
        at, rest = None, ()
    emb_other, send, norms_other = cross(1, at, place, emb, q, turned, totals, *rest)
    emb_own, own, norms_own, mask = cross(0, at, place, emb, q, turned, totals, *rest)

    payload = pack_pair(own, swap(send, count, 1))
    cards = 2
    inner = bits[1:-1]
    while inner:
        used, inner = inner[:2], inner[2:]
        steps = [used[0], used[1], used[0] | used[1]] if len(used) == 2 else used
        moved = {m: swap(payload, count, m) for m in steps[1:2] + steps[:1] + steps[2:]}
        others = [moved[m] for m in steps]
        payload = merge(rank, cards, used, place, payload, *others)
        cards = cards * (1 + len(others))
    mine = [payload, swap(payload, count, opposite)]
    other = [swap(part, count, 1) for part in mine]

    k_own, k_other, copies, consts = kernels(
        cells, cards, count, place, mask, (norms_own, norms_other), (emb_own, emb_other), q,
        weights_prev[None], mine, other,
    )
    scaled = []
    for step_index in range(1, ITERS):
        last = step_index == ITERS - 1
        *scaled, copies = sweep(count, last, place, mask, k_own, k_other, exchange(copies), consts)
    out_s, out_t, weights = finish(cells, *scaled, exchange(copies), consts)
    return out_s, out_t, weights[0]


def solution(mesh):
    in_specs = (
        P(("grp", "cell"), None),
        P(("grp", "cell"), None),
        P("cell", None),
        P(("grp", "cell"), None),
        P(("grp", "cell"), None),
        P("grp"),
        P(None, ("grp", "cell")),
    )
    out_specs = (P(("grp", "cell"), None), P(("grp", "cell"), None), P("grp"))
    return jax.shard_map(
        on_device, mesh=mesh, in_specs=in_specs, out_specs=out_specs, check_vma=False
    )
```

```python
import functools

import jax
import jax.numpy as jnp
from jax import lax
from jax.experimental import pallas as pl
from jax.experimental.pallas import tpu as pltpu
from jax.sharding import PartitionSpec as P

D = 256
ITERS = 3
STEPS = 4
SWEEP_STEPS = 1

step_size = 1.0
LOG2_E = 1.4426950408889634
f32 = jnp.float32
bf16 = jnp.bfloat16
LIMIT = 16 * 1024 * 1024


def swap(value, count, mask):
    return lax.ppermute(value, "cell", [(i, i ^ mask) for i in range(count)])


def halves(value):
    upper = value.astype(bf16)
    return upper, (value - upper.astype(f32)).astype(bf16)


def stacked_left(value):
    upper, lower = halves(value)
    return jnp.concatenate([upper, upper, lower], axis=1)


def stacked_right(value):
    upper, lower = halves(value)
    return jnp.concatenate([upper, lower, upper])


VMEM = pl.BlockSpec(memory_space=pltpu.VMEM)
SMEM = pl.BlockSpec(memory_space=pltpu.SMEM)
HBM = pl.BlockSpec(memory_space=pltpu.HBM)
ANY = pl.BlockSpec(memory_space=pl.ANY)


def far(*arrays):
    return [pltpu.with_memory_space_constraint(a, pltpu.HBM) for a in arrays]


def near(*arrays):
    return [pltpu.with_memory_space_constraint(a, pltpu.VMEM) for a in arrays]


def array(shape, dtype=f32):
    return jax.ShapeDtypeStruct(shape, dtype)


def call(body, name, in_specs, out_specs, out_shape, scratch=(), cost=None):
    return pl.pallas_call(
        body,
        in_specs=in_specs,
        out_specs=out_specs,
        out_shape=out_shape,
        scratch_shapes=list(scratch),
        compiler_params=pltpu.CompilerParams(vmem_limit_bytes=LIMIT),
        cost_estimate=cost,
        name=name,
    )


def rows_of(step, block):
    return pl.ds(pl.multiple_of(step * block, block), block)


def fold(value):
    return jnp.sum(value.reshape(value.shape[0] // 8, 8, value.shape[1]), axis=0)


def add_to(sums, value):
    return value if sums is None else sums + value


def fetch_kernel(qs, qt, table, live, q_out, table_out, turned, totals, live_held, sems):
    pairs = ((qs, q_out.at[0]), (qt, q_out.at[1]), (table, table_out), (live, live_held))
    copies = [pltpu.make_async_copy(a, b, sems.at[i]) for i, (a, b) in enumerate(pairs)]
    for copy in copies:
        copy.start()
    rank = qs.shape[1]
    for t in range(2):
        copies[t].wait()
        factor = q_out[t] * (1.0 / rank)
        totals[t] = jnp.sum(factor, axis=0, keepdims=True)
        turned[t] = factor.T.astype(bf16)
    copies[2].wait()
    copies[3].wait()
    lane = lax.broadcasted_iota(jnp.int32, (1, rank), 1)
    totals[2] = jnp.where(lane < rank // 2, live_held[0], live_held[1]).astype(f32)


def fetch(qs, qt, table, live):
    rows, rank = qs.shape
    return call(
        fetch_kernel, "fetch", [HBM] * 4, [VMEM] * 4,
        [
            pltpu.VMEM((2, rows, rank), f32), pltpu.VMEM(table.shape, table.dtype),
            pltpu.VMEM((2, rank, rows), bf16), array((3, 1, rank)),
        ],
        [pltpu.SMEM((2,), jnp.int32), pltpu.SemaphoreType.DMA((4,))],
        pl.CostEstimate(flops=0, bytes_accessed=8 * rows * rank, transcendentals=0),
    )(*far(qs, qt, table, live))


def stack_kernel(*refs):
    out = refs[-1]
    for i in range(out.shape[0]):
        out[i] = refs[i][...]


def stack_pieces(pieces, after):
    return call(
        stack_kernel, "stack", [VMEM] * len(pieces) + [ANY] * len(after), VMEM,
        array((len(pieces),) + pieces[0].shape, pieces[0].dtype),
    )(*pieces, *after)


def joined_table(me, j, even, odd):
    swapped = (me & 1) == 1
    a, b = even[j], odd[j]
    return jnp.concatenate([jnp.where(swapped, b, a), jnp.where(swapped, a, b)])


def first_kernel(masks, later_masks, place, xs, xt, even, odd, part, later, held, sems):
    me = place[0]
    width = 2 * even.shape[1]

    def copy(x, mask, out, sem):
        start = pl.multiple_of(((me ^ mask) >> 1) * width, width)
        made = pltpu.make_async_copy(x.at[:, pl.ds(start, width)], out, sem)
        made.start()
        return made

    blocks = len(masks)
    now = [
        [copy(x, m, held.at[t, j], sems.at[t, j]) for j, m in enumerate(masks)]
        for t, x in enumerate((xs, xt))
    ]
    after = [
        copy(x, m, later.at[t, j], sems.at[t, blocks + j])
        for j, m in enumerate(later_masks)
        for t, x in enumerate((xs, xt))
    ]
    for t in range(2):
        value = None
        for j in range(blocks):
            now[t][j].wait()
            term = jnp.dot(held[t, j], joined_table(me, j, even, odd), preferred_element_type=f32)
            value = term if value is None else value + term
        part[t] = value
    for made in after:
        made.wait()


def first_share(place, xs, xt, masks, later_masks, even, odd):
    rows, genes = xs.shape
    blocks, width, dim = even.shape
    return call(
        functools.partial(first_kernel, masks, later_masks), "embed_first",
        [SMEM, HBM, HBM, VMEM, VMEM], [VMEM] * 2,
        [array((2, rows, dim)), pltpu.VMEM((2, len(later_masks), rows, 2 * width), bf16)],
        [
            pltpu.VMEM((2, blocks, rows, 2 * width), bf16),
            pltpu.SemaphoreType.DMA((2, blocks + len(later_masks))),
        ],
        pl.CostEstimate(
            flops=2 * rows * genes * dim, bytes_accessed=4 * rows * genes, transcendentals=0
        ),
    )(place, *far(xs, xt), even, odd)


def gate_kernel(value, after, out):
    out[...] = value[...]


def gate(value, after):
    return call(
        gate_kernel, "gate", [VMEM, ANY], VMEM, array(value.shape, value.dtype)
    )(value, after)


def added_products(me, x, t, at, even, odd, value):
    for j in range(even.shape[0]):
        table = joined_table(me, j, even, odd)
        value = value + jnp.dot(x[t, at + j], table, preferred_element_type=f32)
    return value


def next_kernel(at, place, x, part, even, odd, out):
    for t in range(2):
        out[t] = added_products(place[0], x, t, at, even, odd, part[t])


def next_share(at, place, x, part, even, odd):
    return call(
        functools.partial(next_kernel, at), "embed_next", [SMEM] + [VMEM] * 4, VMEM, array(part.shape),
        cost=pl.CostEstimate(
            flops=16 * part.shape[1] * part.shape[2] * even.shape[1], bytes_accessed=0, transcendentals=0
        ),
    )(place, x, part, even, odd)


def whole_kernel(masks, place, xs, xt, pieces, part, table):
    genes = pieces.shape[1]
    for j, mask in enumerate(masks):
        start = pl.multiple_of((place[0] ^ mask) * genes, genes)
        table[pl.ds(start, genes), :] = pieces[j]
    for t, x in enumerate((xs, xt)):
        part[t] = jnp.dot(x[...], table[...], preferred_element_type=f32)


def whole_product(place, xs, xt, masks, pieces):
    rows, genes = xs.shape
    dim = pieces.shape[2]
    return call(
        functools.partial(whole_kernel, masks), "embed_whole", [SMEM] + [VMEM] * 3, VMEM,
        array((2, rows, dim)), [pltpu.VMEM((genes, dim), bf16)],
    )(place, xs, xt, pieces)


def cross_kernel(flip, at, place, part, q, turned, totals, *refs):
    if at is not None:
        (x, even, odd), refs = refs[:3], refs[3:]
    emb, out, norms, *masks = refs
    t = (place[0] & 1) ^ flip
    _, rows, rank = q.shape
    block = rows // STEPS
    value = part[t]
    if at is not None:
        value = added_products(place[0], x, t, at, even, odd, value)
    emb[...] = value
    mean = (jnp.sum(fold(value), axis=0, keepdims=True) / rows).astype(bf16).astype(f32)
    norm_sum = rest = None
    for step in range(STEPS):
        span = slice(step * block, (step + 1) * block)
        value = emb[span, :]
        centred = (value - mean).astype(bf16)
        rest = add_to(rest, jnp.dot(turned[t, :, span], centred, preferred_element_type=f32))
        squares = jnp.sum(value * value, axis=1, keepdims=True)
        norms[span, :] = squares
        norm_sum = add_to(norm_sum, fold(squares * q[t, span, :]))
    norm_sum = jnp.sum(norm_sum, axis=0, keepdims=True) * (1.0 / rank)
    number = totals[2]
    out[0:rank, :] = rest
    out[rank:, :] = jnp.concatenate([mean, totals[t], norm_sum, number, jnp.zeros((4, rank), f32)])
    for mask in masks:
        for i in range(2):
            live = number[:, i * (rank // 2) : i * (rank // 2) + 1].astype(jnp.int32)
            mask[i] = (lax.broadcasted_iota(jnp.int32, (rows, 1), 0) < live).astype(f32)


def cross(flip, at, place, part, q, turned, totals, *rest):
    _, rows, rank = q.shape
    dim = part.shape[2]
    masks = [] if flip else [array((2, rows, 1))]
    return call(
        functools.partial(cross_kernel, flip, at), "cross", [SMEM] + [VMEM] * (4 + len(rest)),
        [VMEM] * (3 + len(masks)),
        [array((rows, dim)), array((rank + 8, dim)), array((rows, 1))] + masks,
        cost=pl.CostEstimate(flops=2 * rank * dim * q.shape[1], bytes_accessed=0, transcendentals=0),
    )(place, part, *near(q, turned), totals, *rest)


def split_row(row):
    high = row.astype(bf16).astype(f32)
    middle = (row - high).astype(bf16).astype(f32)
    return [high, middle, row - high - middle]


def tail_rows(cards):
    return -(-(8 + 4 * cards) // 16) * 16


def make_tail(norm, number, cards):
    width = norm.shape[1]
    rows = split_row(norm) + split_row(number) + [jnp.zeros((2, width), f32)] + cards
    used = sum(r.shape[0] for r in rows)
    filler = tail_rows((used - 8) // 4) - used
    if filler:
        rows.append(jnp.zeros((filler, width), f32))
    return jnp.concatenate(rows)


def three(tail, start):
    return (tail[start : start + 1] + tail[start + 1 : start + 2]) + tail[start + 2 : start + 3]


def pack_pair_kernel(own, recv, out):
    rank = own.shape[0] - 8
    out[0:rank, :] = (own[0:rank, :] + recv[0:rank, :]).astype(bf16)
    cards = []
    for ref in (own, recv):
        cards += [ref[rank : rank + 1, :]] + split_row(ref[rank + 1 : rank + 2, :])
    norm = own[rank + 2 : rank + 3, :] + recv[rank + 2 : rank + 3, :]
    number = own[rank + 3 : rank + 4, :] + recv[rank + 3 : rank + 4, :]
    out[rank:, :] = make_tail(norm, number, cards).astype(bf16)


def pack_pair(own, recv):
    rank, dim = own.shape[0] - 8, own.shape[1]
    return call(
        pack_pair_kernel, "pack_pair", [VMEM] * 2, VMEM, array((rank + tail_rows(2), dim), bf16)
    )(own, recv)


def ordered_cards(tails, cards, flags):
    lists = [tail[8 : 8 + 4 * cards] for tail in tails]
    for flag in flags:
        lists = [
            jnp.concatenate([jnp.where(flag, a, b), jnp.where(flag, b, a)])
            for a, b in zip(lists[::2], lists[1::2])
        ]
    return lists[0]


def tree(values):
    while len(values) > 1:
        values = [a + b for a, b in zip(values[::2], values[1::2])]
    return values[0]


def merge_kernel(rank, cards, bits, place, *refs):
    payloads, out = refs[:-1], refs[-1]
    out[0:rank, :] = tree([p[0:rank, :].astype(f32) for p in payloads]).astype(bf16)
    tails = [p[rank:, :].astype(f32) for p in payloads]
    listed = ordered_cards(tails, cards, [(place[0] & bit) == 0 for bit in bits])
    norm, number = (tree([three(tail, i) for tail in tails]) for i in (0, 3))
    out[rank:, :] = make_tail(norm, number, [listed]).astype(bf16)


def merge(rank, cards, bits, place, *payloads):
    return call(
        functools.partial(merge_kernel, rank, cards, bits), "merge",
        [SMEM] + [VMEM] * len(payloads), VMEM,
        array((rank + tail_rows(len(payloads) * cards), payloads[0].shape[1]), bf16),
    )(place, *payloads)


def total_of(rank, cards, *payloads):
    def unpack(ref):
        tail = ref[rank:, :].astype(f32)
        heights, means, sums = [], [], jnp.zeros((1, tail.shape[1]), f32)
        for c in range(cards):
            at = 8 + 4 * c
            heights.append(tail[at + 1 : at + 4])
            means += [tail[at : at + 1]] * 3
            sums = sums + three(tail, at + 1)
        left, right = jnp.concatenate(heights), jnp.concatenate(means)
        joined = lax.dot_general(
            left.T.astype(bf16), right.astype(bf16), (((1,), (0,)), ((), ())),
            preferred_element_type=f32,
        )
        return ref[0:rank, :].astype(f32) + joined, three(tail, 0), sums, three(tail, 3)

    return [tree(list(values)) for values in zip(*[unpack(ref) for ref in payloads])]


def store_total(parts, out):
    rank = parts[0].shape[0]
    out[0:rank, :] = parts[0]
    out[rank:, :] = jnp.concatenate(parts[1:] + [jnp.zeros((5, out.shape[1]), f32)])


def store_sums(sums, levels, copies):
    both = jnp.concatenate(
        [level * jnp.sum(part, axis=0, keepdims=True) for part, level in zip(sums, levels)]
    )
    for i in range(copies.shape[0]):
        copies[i] = both


def kernel_half(cells, t, mask, norms, emb, q, weights, parts, k, sums_out):
    _, rows, rank = q.shape
    block = rows // STEPS
    inverse = (-step_size * LOG2_E) / (D * (weights[...] * (cells / rank)))
    product, norm, total, _ = parts
    matrix = stacked_right((-2.0 * inverse) * product.T)
    slope, offset = total * inverse, norm * inverse
    sums = None
    for step in range(STEPS):
        at = slice(step * block, (step + 1) * block)
        value = emb[at, :]
        grad = norms[at, :] * slope + offset + jnp.dot(
            stacked_left(value), matrix, preferred_element_type=f32
        )
        kernel = (q[t, at, :] * (1.0 / rank)) * jnp.exp2(grad)
        k[at, :] = kernel
        scale = mask[t, at, :] / jnp.sum(kernel, axis=1, keepdims=True)
        sums = add_to(sums, fold(scale * kernel))
    sums_out[...] = sums


def other_kernel(cells, cards, place, mask, norms, emb, q, weights, near_part, far_part, k, sums, mine):
    parts = total_of(q.shape[2], cards, near_part, far_part)
    store_total(parts, mine)
    kernel_half(cells, 1 - (place[0] & 1), mask, norms, emb, q, weights, parts, k, sums)


def levels_of(cells, summed):
    rank = summed.shape[1]
    numbers = summed[rank + 2 : rank + 3, :]
    return cells / numbers[:, 0:1], cells / numbers[:, rank // 2 : rank // 2 + 1]


def in_order(first, own, out):
    return jnp.where(first, own, out), jnp.where(first, out, own)


def write_tables(cells, first, weights, mine, other, consts):
    rank = weights.shape[1]
    a = mine[...]
    product_b, norm_b, total_b, _ = other
    col_mass = weights[...] * (cells / rank)
    norm_a, total_a = a[rank : rank + 1], a[rank + 1 : rank + 2]
    products = jnp.sum((a[0:rank] * product_b).T, axis=0, keepdims=True)
    mixed = in_order(first, norm_a * total_b, total_a * norm_b)
    cost = (mixed[0] + mixed[1] - 2.0 * products) / D
    consts[0:1, :] = col_mass * jnp.exp(step_size * cost / (col_mass * col_mass))
    for t, level in enumerate(levels_of(cells, mine)):
        consts[1 + t : 2 + t, :] = jnp.broadcast_to(level, (1, rank))


def own_kernel(
    cells, cards, place, mask, norms, emb, q, weights, mine, near_part, far_part, sums_other,
    k, copies, consts, sums,
):
    core = place[0] & 1
    parts = total_of(q.shape[2], cards, near_part, far_part)
    write_tables(cells, core == 0, weights, mine, parts, consts)
    kernel_half(cells, core, mask, norms, emb, q, weights, parts, k, sums)
    store_sums(in_order(core == 0, sums[...], sums_other[...]), levels_of(cells, mine), copies)


def cube_root(x):
    y = jnp.exp(jnp.log(x) * (1.0 / 3.0))
    refined = y - (y - x / (y * y)) * (1.0 / 3.0)
    return jnp.where((x > 0.0) & (x < jnp.inf), refined, y)


def duals_of(parts, consts):
    sums = jnp.sum(parts[...], axis=0)
    sum_s, sum_t = sums[0:1, :], sums[1:2, :]
    mass = cube_root(consts[0:1, :] * sum_s * sum_t)
    return mass, mass / sum_s, mass / sum_t


def row_sums(value):
    folded = value[:, 0:128]
    for start in range(128, value.shape[1], 128):
        folded = folded + value[:, start : start + 128]
    parts = jnp.concatenate(halves(folded), axis=1)
    return jnp.dot(parts, jnp.ones((256, 128), bf16), preferred_element_type=f32)


def scale_rows(value, scale):
    return jnp.concatenate(
        [scale * value[:, i : i + 128] for i in range(0, value.shape[1], 128)], axis=1
    )


def sweep_kernel(last, place, mask, k_own, k_other, parts, consts, *refs):
    copies = refs[-1]
    core = place[0] & 1
    first = core == 0
    block = k_own.shape[0] // SWEEP_STEPS

    _, *duals = duals_of(parts, consts)
    sums = [None, None]
    for step in range(SWEEP_STEPS):
        at = slice(step * block, (step + 1) * block)
        for i, (k, t, dual) in enumerate(
            zip((k_own, k_other), (core, 1 - core), in_order(first, *duals))
        ):
            kernel = k[at, :]
            scaled = scale_rows(kernel, mask[t, at, :] / row_sums(kernel * dual))
            if last:
                refs[0][t, at, :] = scaled
            sums[i] = add_to(sums[i], fold(scaled))
    store_sums(in_order(first, *sums), (consts[1:2, :], consts[2:3, :]), copies)


def finish_kernel(cells, scaled, parts, consts, fs, ft, weights, held, mass_held, sems, mass_sem):
    _, rows, rank = scaled.shape
    block = rows // STEPS
    mass, dual_s, dual_t = duals_of(parts, consts)
    mass_held[...] = mass * (rank / cells)
    copies = [pltpu.make_async_copy(mass_held, weights, mass_sem)]
    copies[0].start()
    dual_s, dual_t = dual_s * (rank * consts[1:2, :]), dual_t * (rank * consts[2:3, :])
    for step in range(STEPS):
        at = slice(step * block, (step + 1) * block)
        for t, (dual, out) in enumerate(((dual_s, fs), (dual_t, ft))):
            held[t, at, :] = scaled[t, at, :] * dual
            copy = pltpu.make_async_copy(held.at[t, at], out.at[at], sems.at[t, step])
            copy.start()
            copies.append(copy)
    for copy in copies:
        copy.wait()


def kernels(cells, cards, count, place, mask, norms, emb, q, weights, mine, other):
    _, rows, rank = q.shape
    dim = emb[0].shape[1]
    cost = pl.CostEstimate(flops=6 * rows * rank * dim, bytes_accessed=0, transcendentals=rows * rank)
    k_other, sums_other, total = call(
        functools.partial(other_kernel, cells, cards), "kernel_other", [SMEM] + [VMEM] * 7, [VMEM] * 3,
        [array((rows, rank)), array((8, rank)), array((rank + 8, dim))], cost=cost,
    )(place, mask, norms[1], emb[1], *near(q), weights, *mine)
    k_own, copies, consts = call(
        functools.partial(own_kernel, cells, cards), "kernel_own", [SMEM] + [VMEM] * 9, [VMEM] * 3,
        [array((rows, rank)), array((count, 2, rank)), array((8, rank))], [pltpu.VMEM((8, rank), f32)], cost,
    )(place, mask, norms[0], emb[0], *near(q), weights, total, *other, sums_other)
    return k_own, k_other, copies, consts


def sweep(count, last, place, mask, k_own, k_other, parts, consts):
    rows, rank = k_own.shape
    scaled = [array((2, rows, rank))] if last else []
    return call(
        functools.partial(sweep_kernel, last), "sweep", [SMEM] + [VMEM] * 5,
        [VMEM] * (len(scaled) + 1), scaled + [array((count, 2, rank))],
    )(place, mask, k_own, k_other, parts, consts)


def finish(cells, scaled, parts, consts):
    _, rows, rank = scaled.shape
    return call(
        functools.partial(finish_kernel, cells), "finish", [VMEM] * 3, [HBM] * 3,
        [array((rows, rank))] * 2 + [array((1, rank))],
        [
            pltpu.VMEM((2, rows, rank), f32), pltpu.VMEM((1, rank), f32),
            pltpu.SemaphoreType.DMA((2, STEPS)), pltpu.SemaphoreType.DMA,
        ],
    )(scaled, parts, consts)


def on_device(
    source_expr, target_expr, loadings, source_prev, target_prev, weights_prev, live_counts
):
    count = lax.axis_size("cell")
    place = lax.axis_index("cell").astype(jnp.int32)[None]
    live = live_counts[:, 0]
    rows, rank = source_prev.shape
    cells = rows * count
    bits = [1 << b for b in range(count.bit_length() - 1)]
    opposite = bits[-1]
    exchange = functools.partial(lax.all_to_all, axis_name="cell", split_axis=0, concat_axis=0)

    q, own_table, turned, totals = fetch(source_prev, target_prev, loadings, live)
    stack = stack_pieces([own_table, swap(loadings, count, opposite)], [totals])
    masks = [0, opposite]
    if count == 16 and loadings.shape[0] % 64 == 0:
        quad = [6, 4, 2]
        arrived = [swap(stack, count, m) for m in quad]
        later = [m ^ q for q in quad for m in masks]
        emb, x = first_share(
            place, source_expr, target_expr, masks, later, stack, swap(stack, count, 1)
        )
        arrived = [gate(piece, emb) for piece in arrived]
        for i, piece in enumerate(arrived[:-1]):
            emb = next_share(2 * i, place, x, emb, piece, swap(piece, count, 1))
        at, rest = 2 * len(arrived) - 2, (x, arrived[-1], swap(arrived[-1], count, 1))
    else:
        for bit in reversed(bits[:-1]):
            stack = jnp.concatenate([stack, swap(stack, count, bit)])
            masks = masks + [m ^ bit for m in masks]
        emb = whole_product(place, source_expr, target_expr, masks, stack)
        at, rest = None, ()
    emb_other, send, norms_other = cross(1, at, place, emb, q, turned, totals, *rest)
    emb_own, own, norms_own, mask = cross(0, at, place, emb, q, turned, totals, *rest)

    payload = pack_pair(own, swap(send, count, 1))
    cards = 2
    inner = bits[1:-1]
    while inner:
        used, inner = inner[:2], inner[2:]
        steps = [used[0], used[1], used[0] | used[1]] if len(used) == 2 else used
        moved = {m: swap(payload, count, m) for m in steps[1:2] + steps[:1] + steps[2:]}
        others = [moved[m] for m in steps]
        payload = merge(rank, cards, used, place, payload, *others)
        cards = cards * (1 + len(others))
    mine = [payload, swap(payload, count, bits[-1] | bits[-2])]
    other = [swap(part, count, 1) for part in mine]

    k_own, k_other, copies, consts = kernels(
        cells, cards, count, place, mask, (norms_own, norms_other), (emb_own, emb_other), q,
        weights_prev[None], mine, other,
    )
    scaled = []
    for step_index in range(1, ITERS):
        last = step_index == ITERS - 1
        *scaled, copies = sweep(count, last, place, mask, k_own, k_other, exchange(copies), consts)
    out_s, out_t, weights = finish(cells, *scaled, exchange(copies), consts)
    return out_s, out_t, weights[0]


def solution(mesh):
    in_specs = (
        P(("grp", "cell"), None),
        P(("grp", "cell"), None),
        P("cell", None),
        P(("grp", "cell"), None),
        P(("grp", "cell"), None),
        P("grp"),
        P(None, ("grp", "cell")),
    )
    out_specs = (P(("grp", "cell"), None), P(("grp", "cell"), None), P("grp"))
    return jax.shard_map(
        on_device, mesh=mesh, in_specs=in_specs, out_specs=out_specs, check_vma=False
    )
```
